128 devices in a mesh: seq: 16 (over y, x), tp: 8 (over z, core).
Axes of the slice: x: 4, y: 4, z: 4, core: 2. Of those that a mesh axis runs over, the one named last changes fastest.
Arguments:
- hidden: bfloat16 [8192, 4096], P('seq', 'tp'), may hold values from -6 to 6
- norm_gain: bfloat16 [4096], replicated, may hold values from 0.25 to 1.75
- gate_x_weight: bfloat16 [4096, 2, 4096], P(None, None, 'tp'), may hold values from -0.09375 to 0.09375
- state_weight: bfloat16 [4096, 2, 1024], P(None, None, 'tp'), may hold values from -0.09375 to 0.09375
- step_weight: bfloat16 [4096, 64], P(None, 'tp'), may hold values from -0.09375 to 0.09375
- conv_inner: bfloat16 [4, 4096], P(None, 'tp'), may hold values from -0.75 to 0.75
- conv_state: bfloat16 [4, 2, 1024], P(None, None, 'tp'), may hold values from -0.75 to 0.75
- step_bias: float32 [64], P('tp'), may hold values from -6 to -1.5
- decay_log: float32 [64], P('tp'), may hold values from -12 to 1
- skip_gain: float32 [64], P('tp'), may hold values from 0.1 to 0.5
- inner_gain: bfloat16 [4096], P('tp'), may hold values from 0.25 to 1.75
- out_weight: bfloat16 [4096, 4096], P('tp'), may hold values from -0.09375 to 0.09375
- initial_state: float32 [64, 64, 128], P('tp'), may hold values from -0.3 to 0.3
Outputs:
- new_hidden: bfloat16 [8192, 4096], P('seq', 'tp')
The draws below stay inside these ranges and needn't reach their ends.
All inputs are finite; a program needn't handle non-finite values.
Results may differ from the reference program's by a relative error of at most 0.009.
Values may be sent and summed in bfloat16 or wider, within the bound.
A program may use at most 128 MiB of HBM per device.

```python
import math
import jax
import jax.numpy as jnp
from jax import lax

MODEL = 4096
HEADS = 64
HEAD_DIM = 64
GROUPS = 8
STATE = 128
CONV = 4
SPAN = 128
INNER = 4096
LENGTH = 8192


def head_rates(key):
    base = jax.random.fold_in(key, 7)
    pick_key, step_key, rate_key = jax.random.split(base, 3)
    picked = jax.random.uniform(pick_key, (HEADS,), jnp.float32)
    slow_heads = picked < 0.5
    step_draw = jax.random.uniform(step_key, (HEADS,), jnp.float32)
    rate_draw = jax.random.uniform(rate_key, (HEADS,), jnp.float32)
    slow_step = 0.003 * jnp.exp(step_draw * math.log(0.01 / 0.003))
    fast_step = 0.05 * jnp.exp(step_draw * math.log(4.0))
    step_base = jnp.where(slow_heads, slow_step, fast_step)
    slow_rate = 0.12 * jnp.exp(rate_draw * math.log(6.0)) / (LENGTH * step_base)
    fast_rate = 0.012 * jnp.exp(rate_draw * math.log(0.02 / 0.012)) / step_base
    coefficient = jnp.where(slow_heads, slow_rate, fast_rate)
    return (jnp.log(jnp.expm1(step_base)), jnp.log(coefficient))


def draw_step_bias(key, part):
    return head_rates(key)[0].astype(jnp.float32)


def draw_decay_log(key, part):
    return head_rates(key)[1].astype(jnp.float32)


def levels(own_key, dims, shards, smallest, largest):
    gain = 1.0
    for dim, shards_of in shards:
        steps = jax.random.uniform(jax.random.fold_in(jax.random.fold_in(own_key, 6), dim), (shards_of,), jnp.float32, smallest / len(shards), largest / len(shards))
        gain = gain * jnp.repeat(jnp.exp(steps), dims[dim] // shards_of).reshape((-1,) + (1,) * (len(dims) - 1 - dim))
    return gain


def scatter_about(stream_key, dims, scale, limit, cuts=(), kind=jnp.bfloat16):
    entries = jax.random.normal(stream_key, dims, jnp.float32) * scale
    if len(cuts) > 0:
        entries = levels(stream_key, dims, cuts, -0.22, 0.18) * entries
    return jnp.clip(entries, min=-limit, max=limit).astype(kind)


def setup_inputs(seed: int = 0) -> dict:
    key_of = jax.random.split(jax.random.key(seed), 14)
    hidden = scatter_about(key_of[0], (LENGTH, MODEL), 1.0, 6.0, ((0, 16), (1, 8)))
    norm_gain = jnp.clip(1.0 + 0.15 * jax.random.normal(key_of[1], (MODEL,), jnp.float32), 0.25, 1.75).astype(jnp.bfloat16)
    gate_x_weight = scatter_about(key_of[2], (MODEL, 2, INNER), MODEL ** -0.5, 0.09375, ((2, 8),))
    state_weight = scatter_about(key_of[3], (MODEL, 2, GROUPS * STATE), MODEL ** -0.5, 0.09375, ((2, 8),))
    step_weight = scatter_about(key_of[4], (MODEL, HEADS), MODEL ** -0.5, 0.09375, ((1, 8),))
    conv_inner = scatter_about(key_of[5], (CONV, INNER), (16 * CONV) ** -0.5, 0.75, ((1, 8),))
    conv_state = scatter_about(key_of[6], (CONV, 2, GROUPS * STATE), (16 * CONV) ** -0.5, 0.75, ((2, 8),))
    step_bias = draw_step_bias(jax.random.fold_in(key_of[13], 71), 0)
    decay_log = draw_decay_log(jax.random.fold_in(key_of[13], 71), 0)
    skip_gain = jnp.clip(0.1 + 0.4 * jax.random.uniform(key_of[9], (HEADS,), jnp.float32) ** levels(key_of[9], (HEADS,), ((0, 8),), -0.2, 0.2), 0.1, 0.5)
    inner_gain = jnp.clip(1.0 + 0.15 * jax.random.normal(key_of[10], (INNER,), jnp.float32), 0.25, 1.75).astype(jnp.bfloat16)
    out_weight = scatter_about(key_of[11], (INNER, MODEL), INNER ** -0.5, 0.09375, ((0, 8),))
    initial_state = scatter_about(key_of[12], (HEADS, HEAD_DIM, STATE), 0.05, 0.3, ((0, 8),), jnp.float32)
    return dict(hidden=hidden, norm_gain=norm_gain, gate_x_weight=gate_x_weight, state_weight=state_weight, step_weight=step_weight, conv_inner=conv_inner, conv_state=conv_state, step_bias=step_bias, decay_log=decay_log, skip_gain=skip_gain, inner_gain=inner_gain, out_weight=out_weight, initial_state=initial_state)


EPSILON = 1e-05
PRECISE = lax.Precision.HIGHEST

def causal_filter(padded, kernel, length):
    summed = kernel[0].astype(jnp.float32) * padded[0:length].astype(jnp.float32)
    for offset in range(1, kernel.shape[0]):
        summed = summed + kernel[offset].astype(jnp.float32) * padded[offset:offset + length].astype(jnp.float32)
    return jax.nn.silu(summed).astype(jnp.bfloat16)

def block_step(carried, inputs):
    memory, log_total = carried
    values, in_map, out_map, step_size, log_decay = inputs
    head_count = values.shape[1]
    group_count = in_map.shape[1]
    ratio_heads = head_count // group_count
    length = values.shape[0]
    row_pos = lax.broadcasted_iota(jnp.int32, (length, length), 0)
    col_pos = lax.broadcasted_iota(jnp.int32, (length, length), 1)
    causal = row_pos >= col_pos
    cumulative = jnp.cumsum(log_decay, axis=0)
    across = cumulative.T
    spread = across[:, :, None] - across[:, None, :]
    weights = jnp.where(causal[None], jnp.exp(jnp.where(causal[None], spread, 0.0)), 0.0)
    group_scores = jnp.einsum('tgn,sgn->gts', out_map, in_map, preferred_element_type=jnp.float32)
    scores = (weights.reshape(group_count, ratio_heads, length, length) * group_scores[:, None]).reshape(head_count, length, length)
    scaled = values * step_size[:, :, None]
    within = jnp.einsum('hts,shp->thp', scores, scaled, precision=PRECISE)
    in_heads = jnp.repeat(in_map.astype(jnp.float32), ratio_heads, axis=1)
    out_heads = jnp.repeat(out_map.astype(jnp.float32), ratio_heads, axis=1)
    from_memory = jnp.einsum('thn,hpn->thp', out_heads * jnp.exp(cumulative)[:, :, None], memory, precision=PRECISE)
    final_log = cumulative[-1]
    remaining = jnp.exp(final_log[None, :] - cumulative)
    update = jnp.einsum('shp,shn->hpn', scaled * remaining[:, :, None], in_heads, precision=PRECISE)
    new_memory = jnp.exp(final_log)[:, None, None] * memory + update
    return ((new_memory, log_total + final_log), (within + from_memory, cumulative + log_total[None, :]))

def run_blocks(values, in_map, out_map, step_size, log_decay, memory):
    blocks = values.shape[0] // SPAN

    def in_blocks(tensor):
        return tensor.reshape((blocks, SPAN) + tensor.shape[1:])
    start_total = jnp.zeros((values.shape[1],), jnp.float32)
    finals, traced = lax.scan(block_step, (memory, start_total), (in_blocks(values), in_blocks(in_map), in_blocks(out_map), in_blocks(step_size), in_blocks(log_decay)))
    outputs = traced[0].reshape(values.shape)
    cumulative = traced[1].reshape(step_size.shape)
    return (finals[0], finals[1], outputs, cumulative)

def reference(hidden, norm_gain, gate_x_weight, state_weight, step_weight, conv_inner, conv_state, step_bias, decay_log, skip_gain, inner_gain, out_weight, initial_state):
    hidden_wide = hidden.astype(jnp.float32)
    moments = lax.optimization_barrier(jnp.mean(hidden_wide * hidden_wide, axis=-1, keepdims=True))
    normed = (hidden_wide * lax.rsqrt(moments + EPSILON) * norm_gain.astype(jnp.float32)).astype(jnp.bfloat16)
    gate_and_x = jnp.dot(normed, gate_x_weight.reshape(MODEL, 2 * INNER), preferred_element_type=jnp.float32).astype(jnp.bfloat16).reshape(LENGTH, 2, INNER)
    state_raw = jnp.dot(normed, state_weight.reshape(MODEL, 2 * GROUPS * STATE), preferred_element_type=jnp.float32).astype(jnp.bfloat16).reshape(LENGTH, 2, GROUPS * STATE)
    step_raw = jnp.dot(normed, step_weight, preferred_element_type=jnp.float32).astype(jnp.bfloat16)
    rim_rows = CONV - 1
    inner_pad = jnp.concatenate([jnp.zeros((rim_rows, INNER), jnp.bfloat16), gate_and_x[:, 1]], axis=0)
    inner_conv = causal_filter(inner_pad, conv_inner, LENGTH)
    state_pad = jnp.concatenate([jnp.zeros((rim_rows, 2, GROUPS * STATE), jnp.bfloat16), state_raw], axis=0)
    state_conv = causal_filter(state_pad, conv_state, LENGTH)
    step_size = jax.nn.softplus(step_raw.astype(jnp.float32) + step_bias[None, :])
    log_decay = -step_size * jnp.exp(decay_log)[None, :]
    values = inner_conv.astype(jnp.float32).reshape(LENGTH, HEADS, HEAD_DIM)
    in_map = state_conv[:, 0].reshape(LENGTH, GROUPS, STATE)
    out_map = state_conv[:, 1].reshape(LENGTH, GROUPS, STATE)
    memory_end, total_end, outputs, cumulative = run_blocks(values, in_map, out_map, step_size, log_decay, initial_state)
    mixer_out = outputs + skip_gain[None, :, None] * values
    gated_out = mixer_out.reshape(LENGTH, INNER) * jax.nn.silu(gate_and_x[:, 0].astype(jnp.float32))
    grouped = gated_out.reshape(LENGTH, GROUPS, INNER // GROUPS)
    scale_rows = lax.rsqrt(lax.optimization_barrier(jnp.mean(grouped * grouped, axis=-1, keepdims=True)) + EPSILON)
    mixed_rows = ((grouped * scale_rows).reshape(LENGTH, INNER) * inner_gain.astype(jnp.float32)).astype(jnp.bfloat16)
    projected = jnp.dot(mixed_rows, out_weight, preferred_element_type=jnp.float32)
    return (projected + hidden_wide).astype(jnp.bfloat16)
```

```python
import jax
import jax.numpy as jnp
from jax import lax
from jax.sharding import PartitionSpec as P

SPAN = 128


EPSILON = 1e-05
PRECISE = lax.Precision.HIGHEST


def from_behind(block, axis, distance):
    devices = range(lax.axis_size(axis))
    route = [(i - distance, i) for i in devices if i - distance in devices]
    return lax.ppermute(block, axis, route)


def causal_filter(padded, kernel, length):
    summed = kernel[0].astype(jnp.float32) * padded[0:length].astype(jnp.float32)
    for offset in range(1, kernel.shape[0]):
        summed = summed + kernel[offset].astype(jnp.float32) * padded[
            offset : offset + length
        ].astype(jnp.float32)
    return jax.nn.silu(summed).astype(jnp.bfloat16)


def block_step(carried, inputs):
    memory, log_total = carried
    values, in_map, out_map, step_size, log_decay = inputs
    head_count = values.shape[1]
    group_count = in_map.shape[1]
    ratio_heads = head_count // group_count
    length = values.shape[0]
    row_pos = lax.broadcasted_iota(jnp.int32, (length, length), 0)
    col_pos = lax.broadcasted_iota(jnp.int32, (length, length), 1)
    causal = row_pos >= col_pos
    cumulative = jnp.dot(causal.astype(jnp.float32), log_decay, precision=PRECISE)
    across = cumulative.T
    spread = across[:, :, None] - across[:, None, :]
    weights = jnp.where(causal[None], jnp.exp(jnp.where(causal[None], spread, 0.0)), 0.0)
    group_scores = jnp.einsum("tgn,sgn->gts", out_map, in_map, preferred_element_type=jnp.float32)
    scores = (
        weights.reshape(group_count, ratio_heads, length, length) * group_scores[:, None]
    ).reshape(head_count, length, length)
    scaled = values * step_size[:, :, None]
    within = jnp.einsum("hts,shp->thp", scores, scaled, precision=PRECISE)
    in_heads = jnp.repeat(in_map.astype(jnp.float32), ratio_heads, axis=1)
    out_heads = jnp.repeat(out_map.astype(jnp.float32), ratio_heads, axis=1)
    from_memory = jnp.einsum(
        "thn,hpn->thp", out_heads * jnp.exp(cumulative)[:, :, None], memory, precision=PRECISE
    )
    final_log = cumulative[-1]
    remaining = jnp.exp(final_log[None, :] - cumulative)
    update = jnp.einsum("shp,shn->hpn", scaled * remaining[:, :, None], in_heads, precision=PRECISE)
    new_memory = jnp.exp(final_log)[:, None, None] * memory + update
    return (
        (new_memory, log_total + final_log),
        (within + from_memory, cumulative + log_total[None, :]),
    )


def run_blocks(values, in_map, out_map, step_size, log_decay, memory):
    blocks = values.shape[0] // SPAN

    def in_blocks(tensor):
        return tensor.reshape((blocks, SPAN) + tensor.shape[1:])

    start_total = jnp.zeros((values.shape[1],), jnp.float32)
    finals, traced = lax.scan(
        block_step,
        (memory, start_total),
        (
            in_blocks(values),
            in_blocks(in_map),
            in_blocks(out_map),
            in_blocks(step_size),
            in_blocks(log_decay),
        ),
    )
    outputs = traced[0].reshape(values.shape)
    cumulative = traced[1].reshape(step_size.shape)
    return (finals[0], finals[1], outputs, cumulative)


def on_device(
    hidden,
    norm_gain,
    gate_x_weight,
    state_weight,
    step_weight,
    conv_inner,
    conv_state,
    step_bias,
    decay_log,
    skip_gain,
    inner_gain,
    out_weight,
    initial_state,
):
    gathered = lax.all_gather(hidden, "tp", axis=1, tiled=True)
    row_count = gathered.shape[0]
    model_width = gathered.shape[1]
    inner_local = gate_x_weight.shape[2]
    state_local = state_weight.shape[2]
    heads_local = step_weight.shape[1]
    head_width = inner_local // heads_local
    state_size = initial_state.shape[2]
    groups_local = state_local // state_size
    hidden_wide = gathered.astype(jnp.float32)
    moments = jnp.mean(hidden_wide * hidden_wide, axis=-1, keepdims=True)
    normed = (hidden_wide * lax.rsqrt(moments + EPSILON) * norm_gain.astype(jnp.float32)).astype(
        jnp.bfloat16
    )
    gate_and_x = (
        jnp.dot(
            normed,
            gate_x_weight.reshape(model_width, 2 * inner_local),
            preferred_element_type=jnp.float32,
        )
        .astype(jnp.bfloat16)
        .reshape(row_count, 2, inner_local)
    )
    state_raw = jnp.dot(
        normed,
        state_weight.reshape(model_width, 2 * state_local),
        preferred_element_type=jnp.float32,
    ).astype(jnp.bfloat16)
    step_raw = jnp.dot(normed, step_weight, preferred_element_type=jnp.float32).astype(jnp.bfloat16)
    inner_raw = gate_and_x[:, 1]
    rim_rows = conv_inner.shape[0] - 1
    tail_rows = jnp.concatenate(
        [inner_raw[row_count - rim_rows :], state_raw[row_count - rim_rows :]], axis=1
    )
    arrived_rim = from_behind(tail_rows, "seq", 1)
    inner_pad = jnp.concatenate([arrived_rim[:, :inner_local], inner_raw], axis=0)
    state_pad = jnp.concatenate([arrived_rim[:, inner_local:], state_raw], axis=0).reshape(
        row_count + rim_rows, 2, state_local
    )
    inner_conv = causal_filter(inner_pad, conv_inner, row_count)
    state_conv = causal_filter(state_pad, conv_state, row_count)
    step_size = jax.nn.softplus(step_raw.astype(jnp.float32) + step_bias[None, :])
    log_decay = -step_size * jnp.exp(decay_log)[None, :]
    values = inner_conv.astype(jnp.float32).reshape(row_count, heads_local, head_width)
    in_map = state_conv[:, 0].reshape(row_count, groups_local, state_size)
    out_map = state_conv[:, 1].reshape(row_count, groups_local, state_size)
    memory_zero = jnp.zeros_like(initial_state)
    local_memory, local_total, outputs, cumulative = run_blocks(
        values, in_map, out_map, step_size, log_decay, memory_zero
    )
    decay_all = jnp.exp(local_total)
    first_mask = (lax.axis_index("seq") == 0).astype(jnp.float32)

    def relay_turn(turn_index, incoming):
        leaving = decay_all[:, None, None] * incoming + local_memory
        arrived_state = from_behind(leaving, "seq", 1)
        return arrived_state + first_mask * initial_state

    entering = lax.fori_loop(0, lax.axis_size("seq") - 1, relay_turn, first_mask * initial_state)
    out_heads = jnp.repeat(out_map.astype(jnp.float32), heads_local // groups_local, axis=1)
    correction = jnp.einsum(
        "thn,hpn->thp", out_heads * jnp.exp(cumulative)[:, :, None], entering, precision=PRECISE
    )
    mixer_out = outputs + correction + skip_gain[None, :, None] * values
    gated_out = mixer_out.reshape(row_count, inner_local) * jax.nn.silu(
        gate_and_x[:, 0].astype(jnp.float32)
    )
    grouped = gated_out.reshape(row_count, groups_local, inner_local // groups_local)
    scale_rows = lax.rsqrt(jnp.mean(grouped * grouped, axis=-1, keepdims=True) + EPSILON)
    mixed_rows = (
        (grouped * scale_rows).reshape(row_count, inner_local) * inner_gain.astype(jnp.float32)
    ).astype(jnp.bfloat16)
    partial_terms = jnp.dot(mixed_rows, out_weight, preferred_element_type=jnp.float32)
    projected = lax.psum_scatter(partial_terms, "tp", scatter_dimension=1, tiled=True)
    return (projected + hidden.astype(jnp.float32)).astype(jnp.bfloat16)


def solution(mesh):
    return jax.shard_map(
        on_device,
        mesh=mesh,
        in_specs=(
            P("seq", "tp"),
            P(),
            P(None, None, "tp"),
            P(None, None, "tp"),
            P(None, "tp"),
            P(None, "tp"),
            P(None, None, "tp"),
            P("tp"),
            P("tp"),
            P("tp"),
            P("tp"),
            P("tp", None),
            P("tp", None, None),
        ),
        out_specs=P("seq", "tp"),
        check_vma=False,
    )
```

```python
import functools

import jax
import jax.numpy as jnp
from jax import lax
from jax.experimental import pallas as pl
from jax.experimental.pallas import tpu as pltpu
from jax.sharding import PartitionSpec as P

F32 = jnp.float32
BF16 = jnp.bfloat16
EPSILON = 1e-05
MESH = pl.DeviceIdType.MESH
HIGHEST = lax.Precision.HIGHEST

ROWS = 512
FEAT = 512
MODEL = 4096
HEADS = 8
WIDTH = 64
STATE = 128
CHUNK = 128
NCHUNK = ROWS // CHUNK
HALF = CHUNK // 2
NSEQ = 16
NTP = 8
NCHIP = 4
COLS = 1408
RING_AG = 9
RING_RS = 8


def silu(v):
    return v / (1.0 + jnp.exp(-v))


def softplus(v):
    return jnp.maximum(v, 0.0) + jnp.log1p(jnp.exp(-jnp.abs(v)))


def dot(a, b, precision=None):
    return jnp.dot(a, b, preferred_element_type=F32, precision=precision)


def iota(shape, dim):
    return lax.broadcasted_iota(jnp.int32, shape, dim)


def across_heads(rows):
    lane = iota((1, 128), 1)
    parts = [
        jnp.where(lane < WIDTH, rows[2 * j : 2 * j + 1, :], rows[2 * j + 1 : 2 * j + 2, :])
        for j in range(4)
    ]
    return jnp.concatenate(parts, axis=1)


def kernel(
    hidden,
    gain_ref,
    gx_hbm,
    sw_hbm,
    stepw_ref,
    tap_x,
    tap_s,
    bias_ref,
    decay_ref,
    skip_ref,
    igain_ref,
    wo_hbm,
    init_ref,
    out_ref,
    gx_raw,
    sw_raw,
    w,
    wo,
    g,
    ss_send,
    ss_recv,
    rfull,
    xf,
    steps,
    sz,
    y,
    ec,
    sloc,
    pre,
    state,
    total_log,
    cmap,
    halo_send,
    halo_recv,
    piece_send,
    piece_recv,
    enter_send,
    enter_recv,
    init_t,
    entering,
    xs,
    xr,
    part,
    far_send,
    near_send,
    far_recv,
    near_recv,
    load_sem,
    ag_send,
    ag_recv,
    ss_ssem,
    ss_rsem,
    halo_ssem,
    halo_rsem,
    p_ssem,
    p_rsem,
    e_ssem,
    e_rsem,
    rs_ssem,
    rs_rsem,
):
    seq = lax.axis_index("seq")
    tp = lax.axis_index("tp")
    chip = tp // 2
    core = tp % 2
    up = (chip + 1) % NCHIP
    down = (chip + 3) % NCHIP
    far = (chip + 2) % NCHIP
    tp_up = up * 2 + core
    tp_down = down * 2 + core
    tp_far = far * 2 + core
    sibling = chip * 2 + (1 - core)

    loads = [
        pltpu.make_async_copy(gx_hbm, gx_raw, load_sem.at[0]),
        pltpu.make_async_copy(sw_hbm, sw_raw, load_sem.at[1]),
        pltpu.make_async_copy(wo_hbm, wo, load_sem.at[2]),
    ]
    for load in loads:
        load.start()

    barrier = pltpu.get_barrier_semaphore()

    @pl.loop(1, NTP)
    def _(k):
        pl.semaphore_signal(
            barrier, inc=1, device_id={"tp": (tp + k) % NTP}, device_id_type=MESH
        )

    @pl.loop(1, NSEQ)
    def _(k):
        pl.semaphore_signal(
            barrier, inc=1, device_id={"seq": (seq + k) % NSEQ}, device_id_type=MESH
        )

    gain_rows = gain_ref[...].astype(F32)
    gain_at = iota((MODEL // 128, 128), 0)
    gain = jnp.concatenate(
        [
            jnp.sum(jnp.where(gain_at == tp * 4 + j, gain_rows, 0.0), axis=0, keepdims=True)
            for j in range(4)
        ],
        axis=1,
    )
    own = pl.ds(pl.multiple_of(tp * FEAT, FEAT), FEAT)
    squares = []
    for c in range(NCHUNK):
        rows = slice(c * CHUNK, (c + 1) * CHUNK)
        h = hidden[rows, :].astype(F32)
        g[rows, own] = (h * gain).astype(BF16)
        summed = jnp.sum(h * h, axis=1, keepdims=True)
        squares.append(jnp.broadcast_to(summed, (CHUNK, 128)).T[0:1, :])
    ss_send[...] = jnp.concatenate(squares + [jnp.zeros((4, 128), F32)], axis=0)

    pl.semaphore_wait(barrier, NTP - 1 + NSEQ - 1)

    def ag_copy(step, kind):
        row = pl.multiple_of(((step + NCHUNK - 1) % NCHUNK) * CHUNK, CHUNK)
        whole, first, second = (row, CHUNK), (row, HALF), (pl.multiple_of(row + HALF, HALF), HALF)
        (start, size), shard, target = (
            (whole, tp, tp_up),
            (whole, tp, tp_down),
            (whole, tp, sibling),
            (first, tp_down, tp_up),
            (second, tp_up, tp_down),
            (whole, tp_down, sibling),
            (whole, tp_up, sibling),
            (first, tp_far, sibling),
            (second, tp_far, sibling),
        )[kind]
        block = g.at[pl.ds(start, size), pl.ds(pl.multiple_of(shard * FEAT, FEAT), FEAT)]
        return pltpu.make_async_remote_copy(
            src_ref=block,
            dst_ref=block,
            send_sem=ag_send.at[step, kind],
            recv_sem=ag_recv.at[step, kind],
            device_id={"tp": target},
            device_id_type=MESH,
        )

    def send_own(step):
        for kind in (0, 1, 2):
            ag_copy(step, kind).start()

    send_own(0)

    def ss_copy(k):
        return pltpu.make_async_remote_copy(
            src_ref=ss_send,
            dst_ref=ss_recv.at[tp],
            send_sem=ss_ssem.at[k],
            recv_sem=ss_rsem.at[k],
            device_id={"tp": (tp + k) % NTP},
            device_id_type=MESH,
        )

    @pl.loop(1, NTP)
    def _(k):
        ss_copy(k).start()

    ss_recv[tp] = ss_send[...]
    send_own(1)

    loads[0].wait()
    o256, i256 = iota((256, 256), 0), iota((256, 256), 1)
    pick = jnp.where(i256 == (o256 % 32) * 8 + o256 // 32, 1.0, 0.0).astype(BF16)

    @pl.loop(0, 64)
    def _(b):
        at = pl.multiple_of(b * 512, 512)
        k0 = pl.multiple_of(b * 64, 64)
        both = jnp.concatenate([gx_raw[pl.ds(at, 256), :], gx_raw[pl.ds(at + 256, 256), :]], axis=1)
        sorted_rows = dot(pick, both).astype(BF16)
        for m in range(8):
            column = (m % 2) * 512 + (m // 2) * 128
            rows = sorted_rows[m * 32 : (m + 1) * 32, :]
            w[pl.ds(k0, 32), column : column + 128] = rows[:, :128]
            w[pl.ds(k0 + 32, 32), column : column + 128] = rows[:, 128:]

    loads[1].wait()
    pick_state = jnp.where(i256 == (o256 % 128) * 2 + o256 // 128, 1.0, 0.0).astype(BF16)

    @pl.loop(0, 16)
    def _(b):
        at = pl.multiple_of(b * 512, 512)
        k0 = pl.multiple_of(b * 256, 256)
        both = jnp.concatenate([sw_raw[pl.ds(at, 256), :], sw_raw[pl.ds(at + 256, 256), :]], axis=1)
        sorted_rows = dot(pick_state, both).astype(BF16)
        for m in range(2):
            column = 1024 + m * 128
            rows = sorted_rows[m * 128 : (m + 1) * 128, :]
            w[pl.ds(k0, 128), column : column + 128] = rows[:, :128]
            w[pl.ds(k0 + 128, 128), column : column + 128] = rows[:, 128:]

    @pl.loop(0, 32)
    def _(b):
        at = pl.multiple_of(b * 128, 128)
        rows = stepw_ref[:, pl.ds(at, 128)].astype(F32)
        square = jnp.concatenate([rows, jnp.zeros((120, 128), F32)], axis=0)
        w[pl.ds(at, 128), 1280:1408] = square.T.astype(BF16)

    for j in range(4):
        init_t[:, j * 128 : (j + 1) * 128] = init_ref[j * 128 : (j + 1) * 128, :].T

    lane512 = iota((1, 512), 1)
    row8 = iota((8, 128), 0)
    bias = jnp.zeros((8, 128), F32)
    rate = jnp.zeros((8, 128), F32)
    skip = jnp.zeros((1, 512), F32)
    for h in range(HEADS):
        bias = jnp.where(row8 == h, bias_ref[h], bias)
        rate = jnp.where(row8 == h, decay_ref[h], rate)
        skip = jnp.where(lane512 // WIDTH == h, skip_ref[h], skip)
    rate = jnp.exp(rate)
    r128, c128 = iota((128, 128), 0), iota((128, 128), 1)
    causal = r128 >= c128
    upper = jnp.where(r128 <= c128, 1.0, 0.0)
    s_row, s_lane = iota((128, 512), 0), iota((128, 512), 1)
    spread_decay = jnp.where(s_row == HEADS + s_lane // WIDTH, 1.0, 0.0).astype(BF16)
    spread_step = jnp.where(s_row == 2 * HEADS + s_lane // WIDTH, 1.0, 0.0).astype(BF16)

    state[...] = jnp.zeros((STATE, FEAT), F32)
    total_log[...] = jnp.zeros((8, 128), F32)

    halo_copy = pltpu.make_async_remote_copy(
        src_ref=halo_send,
        dst_ref=halo_recv,
        send_sem=halo_ssem,
        recv_sem=halo_rsem,
        device_id={"seq": (seq + 1) % NSEQ},
        device_id_type=MESH,
    )

    def project(step):
        row = pl.multiple_of(((step + NCHUNK - 1) % NCHUNK) * CHUNK, CHUNK)
        rows = pl.ds(row, CHUNK)
        r = rfull[rows, :]
        r2 = jnp.concatenate([r, r], axis=1)

        @pl.loop(0, 2)
        def _(n):
            cols = pl.ds(pl.multiple_of(n * 256, 256), 256)
            z = (dot(g[rows, :], w[:, cols]) * r2).astype(BF16).astype(F32)
            sz[rows, cols] = silu(z)

        @pl.loop(0, 3)
        def _(n):
            at = pl.multiple_of(n * 256, 256)
            raw = (dot(g[rows, :], w[:, pl.ds(pl.multiple_of(at + 512, 256), 256)]) * r2).astype(BF16)
            xf[pl.ds(pl.multiple_of(row + 16, 16), CHUNK), pl.ds(at, 256)] = raw.astype(F32)

        raw_step = (dot(g[rows, :], w[:, 1280:1408]) * r).astype(BF16).astype(F32)
        steps[:, rows] = raw_step.T[0:HEADS, :]

    def scan_chunk(c):
        row = pl.multiple_of(c * CHUNK, CHUNK)
        rows = pl.ds(row, CHUNK)

        def filtered(cols, taps):
            padded = xf[pl.ds(pl.multiple_of(row + 8, 8), CHUNK + 8), cols]
            summed = taps[0] * padded[5 : 5 + CHUNK]
            for k in range(1, 4):
                summed = summed + taps[k] * padded[5 + k : 5 + k + CHUNK]
            return silu(summed).astype(BF16)

        taps_x = tap_x[...].astype(F32)
        taps_s = tap_s[...].astype(F32)
        values = jnp.concatenate(
            [
                filtered(
                    slice(j * 128, (j + 1) * 128),
                    [taps_x[k : k + 1, j * 128 : (j + 1) * 128] for k in range(4)],
                )
                for j in range(4)
            ],
            axis=1,
        )
        in_map, out_map = (
            filtered(
                slice(512 + m * 128, 640 + m * 128),
                [taps_s[2 * k + m : 2 * k + m + 1, :] for k in range(4)],
            )
            for m in range(2)
        )
        cmap[rows, :] = out_map
        in_map_t = in_map.astype(F32).T.astype(BF16)
        step = softplus(steps[:, rows] + bias)
        cum = dot(-step * rate, upper, HIGHEST)
        last = jnp.broadcast_to(cum[:, 127:128], (8, 128))
        kept = step * jnp.exp(last - cum)
        columns = jnp.concatenate(
            [cum, jnp.exp(cum), kept, jnp.zeros((104, 128), F32)], axis=0
        ).T
        high = columns.astype(BF16)
        low = (columns - high.astype(F32)).astype(BF16)
        decay_exp = dot(high, spread_decay) + dot(low, spread_decay)
        step_exp = dot(high, spread_step) + dot(low, spread_step)
        ec[rows, :] = decay_exp
        wide = values.astype(F32)
        weighted = (wide * step_exp).astype(BF16)
        before = state[...]
        sloc[c] = before
        pre[c] = jnp.broadcast_to(jnp.exp(across_heads(total_log[...])), (8, FEAT))
        total_log[...] += last
        state[...] = jnp.exp(across_heads(last)) * before + dot(in_map_t, weighted)

        scores = dot(out_map, in_map_t)
        lane = iota((CHUNK, 128), 1)
        for j in range(4):
            pair = values[:, j * 128 : (j + 1) * 128]
            both = []
            for h in (2 * j, 2 * j + 1):
                spread = columns[:, h : h + 1] - cum[h : h + 1, :]
                weights = jnp.exp(jnp.where(causal, spread, -1e30))
                both.append(dot((scores * weights * step[h : h + 1, :]).astype(BF16), pair))
            cols = slice(j * 128, (j + 1) * 128)
            y[rows, cols] = jnp.where(lane < WIDTH, both[0], both[1]) + skip[:, cols] * wide[:, cols]

    @pl.loop(0, NCHUNK + 2)
    def _(i):
        @pl.when(i < NCHUNK)
        def _():
            ag_copy(i, 0).wait_recv()
            ag_copy(i, 3).start()
            ag_copy(i, 5).start()
            ag_copy(i, 1).wait_recv()
            ag_copy(i, 4).start()
            ag_copy(i, 6).start()

        @pl.when(i < NCHUNK - 2)
        def _():
            send_own(i + 2)

        @pl.when(i == 1)
        def _():
            @pl.loop(1, NTP)
            def _(k):
                ss_copy(k).wait_recv()

            summed = ss_recv[0]
            for k in range(1, NTP):
                summed = summed + ss_recv[k]
            r = lax.rsqrt(summed * (1.0 / MODEL) + EPSILON)
            for c in range(NCHUNK):
                rfull[c * CHUNK : (c + 1) * CHUNK, :] = jnp.broadcast_to(
                    r[c : c + 1, :], (CHUNK, 128)
                ).T

        @pl.when((i >= 1) & (i <= NCHUNK))
        def _():
            step = i - 1
            for kind in (2, 5, 6, 7, 8):
                ag_copy(step, kind).wait_recv()
            project(step)

        @pl.when(i == 1)
        def _():
            halo_send[...] = xf[ROWS : ROWS + 16, :].astype(BF16)
            halo_copy.start()

        @pl.when(i == 2)
        def _():
            halo_copy.wait_recv()
            xf[0:16, :] = jnp.where(seq > 0, halo_recv[...].astype(F32), 0.0)

        @pl.when(i >= 2)
        def _():
            scan_chunk(i - 2)

        @pl.when(i < NCHUNK)
        def _():
            ag_copy(i, 3).wait_recv()
            ag_copy(i, 7).start()
            ag_copy(i, 4).wait_recv()
            ag_copy(i, 8).start()

    logs = across_heads(total_log[...])
    high = logs.astype(BF16)
    rest = logs - high.astype(F32)
    middle = rest.astype(BF16)
    bits = [high.astype(F32), middle.astype(F32), rest - middle.astype(F32)]
    row16 = iota((16, 128), 0)
    for half in range(2):
        block = jnp.zeros((16, 128), F32)
        for part_at in range(2):
            at = half * 256 + part_at * 128
            for n in range(3):
                block = jnp.where(row16 == part_at * 8 + n, bits[n][:, at : at + 128], block)
        block = block.astype(BF16)
        for n in range(8):
            piece_send[2 * n + half, :, 0:256] = state[
                n * 16 : (n + 1) * 16, half * 256 : (half + 1) * 256
            ].astype(BF16)
            piece_send[2 * n + half, :, 256:384] = block

    def piece_copy(k):
        target = (seq + k) % NSEQ
        return pltpu.make_async_remote_copy(
            src_ref=piece_send.at[target],
            dst_ref=piece_recv.at[seq],
            send_sem=p_ssem.at[k],
            recv_sem=p_rsem.at[k],
            device_id={"seq": target},
            device_id_type=MESH,
        )

    def enter_copy(k):
        target = (seq + k) % NSEQ
        return pltpu.make_async_remote_copy(
            src_ref=enter_send.at[target],
            dst_ref=enter_recv.at[seq],
            send_sem=e_ssem.at[k],
            recv_sem=e_rsem.at[k],
            device_id={"seq": target},
            device_id_type=MESH,
        )

    @pl.loop(1, NSEQ)
    def _(k):
        piece_copy(k).start()

    piece_recv[seq] = piece_send[seq]
    carried = init_t[
        pl.ds(pl.multiple_of((seq // 2) * 16, 16), 16),
        pl.ds(pl.multiple_of((seq % 2) * 256, 256), 256),
    ]

    @pl.loop(1, NSEQ)
    def _(k):
        piece_copy(k).wait_recv()

    def combine(s, carried):
        enter_send[s] = carried.astype(BF16)
        codes = piece_recv[s, :, 256:384].astype(F32)
        log = jnp.concatenate(
            [codes[0:1] + codes[1:2] + codes[2:3], codes[8:9] + codes[9:10] + codes[10:11]], axis=1
        )
        return jnp.exp(log) * carried + piece_recv[s, :, 0:256].astype(F32)

    lax.fori_loop(0, NSEQ, combine, carried)

    @pl.loop(1, NSEQ)
    def _(k):
        enter_copy(k).start()

    enter_recv[seq] = enter_send[seq]
    loads[2].wait()

    @pl.loop(1, NSEQ)
    def _(k):
        enter_copy(k).wait_recv()

    for q in range(NSEQ):
        n, half = q // 2, q % 2
        entering[n * 16 : (n + 1) * 16, half * 256 : (half + 1) * 256] = enter_recv[q].astype(F32)

    igain_rows = igain_ref[...].astype(F32)
    igain = jnp.concatenate([igain_rows[j : j + 1, :] for j in range(4)], axis=1)

    def rs_copy(i, kind):
        src, dst, target = (
            (xs.at[i, 0], xr.at[i, 0], sibling),
            (xs.at[i, 1], xr.at[i, 1], sibling),
            (xs.at[i, 2], xr.at[i, 2], sibling),
            (xs.at[i, 3], xr.at[i, 3], sibling),
            (far_send.at[i, 0], far_recv.at[i, 0], tp_up),
            (far_send.at[i, 1], far_recv.at[i, 1], tp_down),
            (near_send.at[i, 0], near_recv.at[i, 0], tp_up),
            (near_send.at[i, 1], near_recv.at[i, 1], tp_down),
        )[kind]
        return pltpu.make_async_remote_copy(
            src_ref=src,
            dst_ref=dst,
            send_sem=rs_ssem.at[i, kind],
            recv_sem=rs_rsem.at[i, kind],
            device_id={"tp": target},
            device_id_type=MESH,
        )

    @pl.loop(0, NCHUNK + 2)
    def _(i):
        @pl.when(i < NCHUNK)
        def _():
            rows = pl.ds(pl.multiple_of(i * CHUNK, CHUNK), CHUNK)
            memory = (sloc[i] + pre[i][0:1, :] * entering[...]).astype(BF16)
            mixer = y[rows, :] + ec[rows, :] * dot(cmap[rows, :], memory)
            gated = mixer * sz[rows, :]
            scale = lax.rsqrt(jnp.mean(gated * gated, axis=1, keepdims=True) + EPSILON)
            mixed = (gated * scale * igain).astype(BF16)
            for d, z in enumerate((far, up, down, chip)):
                at = pl.multiple_of((z * 2 + 1 - core) * FEAT, FEAT)
                xs[i, d] = dot(mixed, wo[:, pl.ds(at, FEAT)]).astype(BF16)
                rs_copy(i, d).start()
            for d, z in enumerate((far, up, down, chip)):
                at = pl.multiple_of((z * 2 + core) * FEAT, FEAT)
                part[i, d] = dot(mixed, wo[:, pl.ds(at, FEAT)])
            rs_copy(i, 0).wait_recv()
            whole = (part[i, 0] + xr[i, 0].astype(F32)).astype(BF16)
            far_send[i, 0] = whole[:HALF]
            rs_copy(i, 4).start()
            far_send[i, 1] = whole[HALF:]
            rs_copy(i, 5).start()

        @pl.when((i >= 1) & (i <= NCHUNK))
        def _():
            c = i - 1
            rs_copy(c, 1).wait_recv()
            rs_copy(c, 4).wait_recv()
            whole = part[c, 1] + xr[c, 1].astype(F32)
            near_send[c, 0, 0:HALF] = (whole[:HALF] + far_recv[c, 0].astype(F32)).astype(BF16)
            near_send[c, 0, HALF:CHUNK] = whole[HALF:].astype(BF16)
            rs_copy(c, 6).start()
            rs_copy(c, 2).wait_recv()
            rs_copy(c, 5).wait_recv()
            whole = part[c, 2] + xr[c, 2].astype(F32)
            near_send[c, 1, 0:HALF] = whole[:HALF].astype(BF16)
            near_send[c, 1, HALF:CHUNK] = (whole[HALF:] + far_recv[c, 1].astype(F32)).astype(BF16)
            rs_copy(c, 7).start()

        @pl.when(i >= 2)
        def _():
            c = i - 2
            rows = pl.ds(pl.multiple_of(c * CHUNK, CHUNK), CHUNK)
            rs_copy(c, 3).wait_recv()
            summed = hidden[rows, :].astype(F32) + (part[c, 3] + xr[c, 3].astype(F32))
            rs_copy(c, 6).wait_recv()
            summed = summed + near_recv[c, 0].astype(F32)
            rs_copy(c, 7).wait_recv()
            out_ref[rows, :] = (summed + near_recv[c, 1].astype(F32)).astype(BF16)

    @pl.loop(0, NCHUNK)
    def _(i):
        for kind in range(RING_AG):
            ag_copy(i, kind).wait_send()
        for kind in range(RING_RS):
            rs_copy(i, kind).wait_send()

    @pl.loop(1, NTP)
    def _(k):
        ss_copy(k).wait_send()

    halo_copy.wait_send()

    @pl.loop(1, NSEQ)
    def _(k):
        piece_copy(k).wait_send()
        enter_copy(k).wait_send()


def on_device(
    hidden,
    norm_gain,
    gate_x_weight,
    state_weight,
    step_weight,
    conv_inner,
    conv_state,
    step_bias,
    decay_log,
    skip_gain,
    inner_gain,
    out_weight,
    initial_state,
):
    gx = gate_x_weight.reshape(MODEL, 2, 4, 128).transpose(0, 2, 1, 3).reshape(MODEL * 8, 128)
    sw = state_weight.reshape(MODEL * 2, 128)
    vmem = pl.BlockSpec(memory_space=pltpu.VMEM)
    smem = pl.BlockSpec(memory_space=pltpu.SMEM)
    anywhere = pl.BlockSpec(memory_space=pl.ANY)
    V = pltpu.VMEM
    dma = pltpu.SemaphoreType.DMA
    return pl.pallas_call(
        kernel,
        out_shape=jax.ShapeDtypeStruct((ROWS, FEAT), BF16),
        in_specs=[
            vmem, vmem, anywhere, anywhere, vmem, vmem, vmem, smem, smem, smem, vmem, anywhere, vmem,
        ],
        out_specs=vmem,
        scratch_shapes=[
            V((MODEL * 8, 128), BF16),
            V((MODEL * 2, 128), BF16),
            V((MODEL, COLS), BF16),
            V((FEAT, MODEL), BF16),
            V((ROWS, MODEL), BF16),
            V((8, 128), F32),
            V((NTP, 8, 128), F32),
            V((ROWS, 128), F32),
            V((ROWS + 16, 768), F32),
            V((8, ROWS), F32),
            V((ROWS, FEAT), F32),
            V((ROWS, FEAT), F32),
            V((ROWS, FEAT), F32),
            V((NCHUNK, STATE, FEAT), F32),
            V((NCHUNK, 8, FEAT), F32),
            V((STATE, FEAT), F32),
            V((8, 128), F32),
            V((ROWS, STATE), BF16),
            V((16, 768), BF16),
            V((16, 768), BF16),
            V((NSEQ, 16, 384), BF16),
            V((NSEQ, 16, 384), BF16),
            V((NSEQ, 16, 256), BF16),
            V((NSEQ, 16, 256), BF16),
            V((STATE, FEAT), F32),
            V((STATE, FEAT), F32),
            V((NCHUNK, 4, CHUNK, FEAT), BF16),
            V((NCHUNK, 4, CHUNK, FEAT), BF16),
            V((NCHUNK, 4, CHUNK, FEAT), F32),
            V((NCHUNK, 2, HALF, FEAT), BF16),
            V((NCHUNK, 2, CHUNK, FEAT), BF16),
            V((NCHUNK, 2, HALF, FEAT), BF16),
            V((NCHUNK, 2, CHUNK, FEAT), BF16),
            dma((3,)),
            dma((NCHUNK, RING_AG)),
            dma((NCHUNK, RING_AG)),
            dma((NTP,)),
            dma((NTP,)),
            dma,
            dma,
            dma((NSEQ,)),
            dma((NSEQ,)),
            dma((NSEQ,)),
            dma((NSEQ,)),
            dma((NCHUNK, RING_RS)),
            dma((NCHUNK, RING_RS)),
        ],
        compiler_params=pltpu.CompilerParams(
            collective_id=0, has_side_effects=True, vmem_limit_bytes=61 << 20
        ),
    )(
        hidden,
        norm_gain.reshape(MODEL // 128, 128),
        gx,
        sw,
        step_weight.T,
        conv_inner,
        conv_state.reshape(8, 128),
        step_bias,
        decay_log,
        skip_gain,
        inner_gain.reshape(4, 128),
        out_weight,
        initial_state.reshape(HEADS * WIDTH, STATE),
    )


def solution(mesh):
    return jax.shard_map(
        on_device,
        mesh=mesh,
        in_specs=(
            P("seq", "tp"),
            P(),
            P(None, None, "tp"),
            P(None, None, "tp"),
            P(None, "tp"),
            P(None, "tp"),
            P(None, None, "tp"),
            P("tp"),
            P("tp"),
            P("tp"),
            P("tp"),
            P("tp", None),
            P("tp", None, None),
        ),
        out_specs=P("seq", "tp"),
        check_vma=False,
    )
```

```python
import functools

import jax
import jax.numpy as jnp
from jax import lax
from jax.experimental import pallas as pl
from jax.experimental.pallas import tpu as pltpu
from jax.sharding import PartitionSpec as P

F32 = jnp.float32
BF16 = jnp.bfloat16
EPSILON = 1e-05
MESH = pl.DeviceIdType.MESH
HIGHEST = lax.Precision.HIGHEST

ROWS = 512
FEAT = 512
MODEL = 4096
HEADS = 8
WIDTH = 64
STATE = 128
CHUNK = 128
NCHUNK = ROWS // CHUNK
HALF = CHUNK // 2
NSEQ = 16
NTP = 8
NCHIP = 4
COLS = 1408
RING_AG = 9
RING_RS = 8


def silu(v):
    return v / (1.0 + jnp.exp(-v))


def softplus(v):
    return jnp.maximum(v, 0.0) + jnp.log1p(jnp.exp(-jnp.abs(v)))


def dot(a, b, precision=None):
    return jnp.dot(a, b, preferred_element_type=F32, precision=precision)


def iota(shape, dim):
    return lax.broadcasted_iota(jnp.int32, shape, dim)


def across_heads(rows):
    lane = iota((1, 128), 1)
    parts = [
        jnp.where(lane < WIDTH, rows[2 * j : 2 * j + 1, :], rows[2 * j + 1 : 2 * j + 2, :])
        for j in range(4)
    ]
    return jnp.concatenate(parts, axis=1)


def kernel(
    hidden,
    gain_ref,
    gx_hbm,
    sw_hbm,
    stepw_ref,
    tap_x,
    tap_s,
    bias_ref,
    decay_ref,
    skip_ref,
    igain_ref,
    wo_hbm,
    init_ref,
    out_ref,
    gx_raw,
    sw_raw,
    w,
    wo,
    g,
    ss_send,
    ss_recv,
    rfull,
    xf,
    steps,
    sz,
    y,
    ec,
    sloc,
    pre,
    state,
    total_log,
    cmap,
    vals,
    bmap_t,
    cols_t,
    cum_rows,
    step_rows,
    mx,
    halo_send,
    halo_recv,
    piece_send,
    piece_recv,
    enter_send,
    enter_recv,
    init_t,
    entering,
    xs,
    xr,
    part,
    far_send,
    near_send,
    far_recv,
    near_recv,
    load_sem,
    ag_send,
    ag_recv,
    ss_ssem,
    ss_rsem,
    halo_ssem,
    halo_rsem,
    p_ssem,
    p_rsem,
    e_ssem,
    e_rsem,
    rs_ssem,
    rs_rsem,
):
    seq = lax.axis_index("seq")
    tp = lax.axis_index("tp")
    chip = tp // 2
    core = tp % 2
    up = (chip + 1) % NCHIP
    down = (chip + 3) % NCHIP
    far = (chip + 2) % NCHIP
    tp_up = up * 2 + core
    tp_down = down * 2 + core
    tp_far = far * 2 + core
    sibling = chip * 2 + (1 - core)

    loads = [
        pltpu.make_async_copy(gx_hbm, gx_raw, load_sem.at[0]),
        pltpu.make_async_copy(sw_hbm, sw_raw, load_sem.at[1]),
        pltpu.make_async_copy(wo_hbm, wo, load_sem.at[2]),
    ]
    loads[0].start()
    loads[1].start()

    barrier = pltpu.get_barrier_semaphore()

    @pl.loop(1, NTP)
    def _(k):
        pl.semaphore_signal(
            barrier, inc=1, device_id={"tp": (tp + k) % NTP}, device_id_type=MESH
        )

    @pl.loop(1, NSEQ)
    def _(k):
        pl.semaphore_signal(
            barrier, inc=1, device_id={"seq": (seq + k) % NSEQ}, device_id_type=MESH
        )

    gain_rows = gain_ref[...].astype(F32)
    gain_at = iota((MODEL // 128, 128), 0)
    gain = jnp.concatenate(
        [
            jnp.sum(jnp.where(gain_at == tp * 4 + j, gain_rows, 0.0), axis=0, keepdims=True)
            for j in range(4)
        ],
        axis=1,
    )
    own = pl.ds(pl.multiple_of(tp * FEAT, FEAT), FEAT)
    squares = []
    for c in range(NCHUNK):
        rows = slice(c * CHUNK, (c + 1) * CHUNK)
        h = hidden[rows, :].astype(F32)
        g[rows, own] = (h * gain).astype(BF16)
        summed = jnp.sum(h * h, axis=1, keepdims=True)
        squares.append(jnp.broadcast_to(summed, (CHUNK, 128)).T[0:1, :])
    ss_send[...] = jnp.concatenate(squares + [jnp.zeros((4, 128), F32)], axis=0)

    pl.semaphore_wait(barrier, NTP - 1 + NSEQ - 1)

    def ag_copy(step, kind):
        row = pl.multiple_of(((step + NCHUNK - 1) % NCHUNK) * CHUNK, CHUNK)
        whole, first, second = (row, CHUNK), (row, HALF), (pl.multiple_of(row + HALF, HALF), HALF)
        (start, size), shard, target = (
            (whole, tp, tp_up),
            (whole, tp, tp_down),
            (whole, tp, sibling),
            (first, tp_down, tp_up),
            (second, tp_up, tp_down),
            (whole, tp_down, sibling),
            (whole, tp_up, sibling),
            (first, tp_far, sibling),
            (second, tp_far, sibling),
        )[kind]
        block = g.at[pl.ds(start, size), pl.ds(pl.multiple_of(shard * FEAT, FEAT), FEAT)]
        return pltpu.make_async_remote_copy(
            src_ref=block,
            dst_ref=block,
            send_sem=ag_send.at[step, kind],
            recv_sem=ag_recv.at[step, kind],
            device_id={"tp": target},
            device_id_type=MESH,
        )

    def send_own(step):
        for kind in (0, 1, 2):
            ag_copy(step, kind).start()

    send_own(0)

    def ss_copy(k):
        return pltpu.make_async_remote_copy(
            src_ref=ss_send,
            dst_ref=ss_recv.at[tp],
            send_sem=ss_ssem.at[k],
            recv_sem=ss_rsem.at[k],
            device_id={"tp": (tp + k) % NTP},
            device_id_type=MESH,
        )

    @pl.loop(1, NTP)
    def _(k):
        ss_copy(k).start()

    ss_recv[tp] = ss_send[...]
    send_own(1)

    loads[0].wait()
    o256, i256 = iota((256, 256), 0), iota((256, 256), 1)
    pick = jnp.where(i256 == (o256 % 32) * 8 + o256 // 32, 1.0, 0.0).astype(BF16)

    @pl.loop(0, 64, unroll=16)
    def _(b):
        at = pl.multiple_of(b * 512, 512)
        k0 = pl.multiple_of(b * 64, 64)
        both = jnp.concatenate([gx_raw[pl.ds(at, 256), :], gx_raw[pl.ds(at + 256, 256), :]], axis=1)
        sorted_rows = dot(pick, both).astype(BF16)
        for m in range(8):
            column = (m % 2) * 512 + (m // 2) * 128
            rows = sorted_rows[m * 32 : (m + 1) * 32, :]
            w[pl.ds(k0, 32), column : column + 128] = rows[:, :128]
            w[pl.ds(k0 + 32, 32), column : column + 128] = rows[:, 128:]

    loads[1].wait()
    loads[2].start()
    pick_state = jnp.where(i256 == (o256 % 128) * 2 + o256 // 128, 1.0, 0.0).astype(BF16)

    @pl.loop(0, 16, unroll=8)
    def _(b):
        at = pl.multiple_of(b * 512, 512)
        k0 = pl.multiple_of(b * 256, 256)
        both = jnp.concatenate([sw_raw[pl.ds(at, 256), :], sw_raw[pl.ds(at + 256, 256), :]], axis=1)
        sorted_rows = dot(pick_state, both).astype(BF16)
        for m in range(2):
            column = 1024 + m * 128
            rows = sorted_rows[m * 128 : (m + 1) * 128, :]
            w[pl.ds(k0, 128), column : column + 128] = rows[:, :128]
            w[pl.ds(k0 + 128, 128), column : column + 128] = rows[:, 128:]

    @pl.loop(0, 32, unroll=8)
    def _(b):
        at = pl.multiple_of(b * 128, 128)
        rows = stepw_ref[:, pl.ds(at, 128)].astype(F32)
        square = jnp.concatenate([rows, jnp.zeros((120, 128), F32)], axis=0)
        w[pl.ds(at, 128), 1280:1408] = square.T.astype(BF16)

    for j in range(4):
        init_t[:, j * 128 : (j + 1) * 128] = init_ref[j * 128 : (j + 1) * 128, :].T

    lane512 = iota((1, 512), 1)
    row8 = iota((8, 128), 0)
    bias = jnp.zeros((8, 128), F32)
    rate = jnp.zeros((8, 128), F32)
    skip = jnp.zeros((1, 512), F32)
    for h in range(HEADS):
        bias = jnp.where(row8 == h, bias_ref[h], bias)
        rate = jnp.where(row8 == h, decay_ref[h], rate)
        skip = jnp.where(lane512 // WIDTH == h, skip_ref[h], skip)
    rate = jnp.exp(rate)
    r128, c128 = iota((128, 128), 0), iota((128, 128), 1)
    causal = r128 >= c128
    upper = jnp.where(r128 <= c128, 1.0, 0.0)
    s_row, s_lane = iota((128, 512), 0), iota((128, 512), 1)
    spread_decay = jnp.where(s_row == HEADS + s_lane // WIDTH, 1.0, 0.0).astype(BF16)
    spread_step = jnp.where(s_row == 2 * HEADS + s_lane // WIDTH, 1.0, 0.0).astype(BF16)

    state[...] = jnp.zeros((STATE, FEAT), F32)
    total_log[...] = jnp.zeros((8, 128), F32)

    halo_copy = pltpu.make_async_remote_copy(
        src_ref=halo_send,
        dst_ref=halo_recv,
        send_sem=halo_ssem,
        recv_sem=halo_rsem,
        device_id={"seq": (seq + 1) % NSEQ},
        device_id_type=MESH,
    )

    def chunk_of(step):
        return (step + NCHUNK - 1) % NCHUNK

    def project(c):
        row = pl.multiple_of(c * CHUNK, CHUNK)
        rows = pl.ds(row, CHUNK)
        r = rfull[rows, :]
        product = dot(g[rows, :], w[:, 512:COLS])
        for n in range(6):
            raw = (product[:, n * 128 : (n + 1) * 128] * r).astype(BF16).astype(F32)
            xf[pl.ds(pl.multiple_of(row + 16, 16), CHUNK), n * 128 : (n + 1) * 128] = raw
        raw_step = (product[:, 768:896] * r).astype(BF16).astype(F32)
        steps[:, rows] = raw_step.T[0:HEADS, :]

    def project_gate(c):
        rows = pl.ds(pl.multiple_of(c * CHUNK, CHUNK), CHUNK)
        r = rfull[rows, :]
        product = dot(g[rows, :], w[:, 0:512])
        for n in range(4):
            z = (product[:, n * 128 : (n + 1) * 128] * r).astype(BF16).astype(F32)
            sz[rows, n * 128 : (n + 1) * 128] = silu(z)

    def scan_chunk(c):
        row = pl.multiple_of(c * CHUNK, CHUNK)
        rows = pl.ds(row, CHUNK)

        def filtered(cols, taps):
            padded = xf[pl.ds(pl.multiple_of(row + 8, 8), CHUNK + 8), cols]
            summed = taps[0] * padded[5 : 5 + CHUNK]
            for k in range(1, 4):
                summed = summed + taps[k] * padded[5 + k : 5 + k + CHUNK]
            return silu(summed).astype(BF16)

        taps_x = tap_x[...].astype(F32)
        taps_s = tap_s[...].astype(F32)
        values = jnp.concatenate(
            [
                filtered(
                    slice(j * 128, (j + 1) * 128),
                    [taps_x[k : k + 1, j * 128 : (j + 1) * 128] for k in range(4)],
                )
                for j in range(4)
            ],
            axis=1,
        )
        in_map, out_map = (
            filtered(
                slice(512 + m * 128, 640 + m * 128),
                [taps_s[2 * k + m : 2 * k + m + 1, :] for k in range(4)],
            )
            for m in range(2)
        )
        cmap[rows, :] = out_map
        vals[rows, :] = values
        in_map_t = in_map.astype(F32).T.astype(BF16)
        step = softplus(steps[:, rows] + bias)
        cum = dot(-step * rate, upper, HIGHEST)
        last = jnp.broadcast_to(cum[:, 127:128], (8, 128))
        kept = step * jnp.exp(last - cum)
        columns = jnp.concatenate(
            [cum, jnp.exp(cum), kept, jnp.zeros((104, 128), F32)], axis=0
        ).T
        bmap_t[c] = in_map_t
        cols_t[c] = columns
        cum_rows[c] = cum
        step_rows[c] = step
        high = columns.astype(BF16)
        low = (columns - high.astype(F32)).astype(BF16)
        step_exp = dot(high, spread_step) + dot(low, spread_step)
        wide = values.astype(F32)
        weighted = (wide * step_exp).astype(BF16)
        before = state[...]
        sloc[c] = before
        pre[c] = jnp.broadcast_to(jnp.exp(across_heads(total_log[...])), (8, FEAT))
        total_log[...] += last
        state[...] = jnp.exp(across_heads(last)) * before + dot(in_map_t, weighted)

    def outputs_of(c):
        rows = pl.ds(pl.multiple_of(c * CHUNK, CHUNK), CHUNK)
        columns, cum, step = cols_t[c], cum_rows[c], step_rows[c]
        high = columns.astype(BF16)
        low = (columns - high.astype(F32)).astype(BF16)
        ec[rows, :] = dot(high, spread_decay) + dot(low, spread_decay)
        scores = dot(cmap[rows, :], bmap_t[c])
        lane = iota((CHUNK, 128), 1)
        for j in range(4):
            cols = slice(j * 128, (j + 1) * 128)
            pair = vals[rows, cols]
            both = []
            for h in (2 * j, 2 * j + 1):
                spread = columns[:, h : h + 1] - cum[h : h + 1, :]
                weights = jnp.exp(jnp.where(causal, spread, -1e30))
                both.append(dot((scores * weights * step[h : h + 1, :]).astype(BF16), pair))
            y[rows, cols] = (
                jnp.where(lane < WIDTH, both[0], both[1]) + skip[:, cols] * pair.astype(F32)
            )

    @pl.loop(0, NCHUNK + 1)
    def _(i):
        @pl.when(i < NCHUNK)
        def _():
            ag_copy(i, 0).wait_recv()
            ag_copy(i, 3).start()
            ag_copy(i, 5).start()
            ag_copy(i, 1).wait_recv()
            ag_copy(i, 4).start()
            ag_copy(i, 6).start()

        @pl.when(i < NCHUNK - 2)
        def _():
            send_own(i + 2)

        @pl.when(i == 1)
        def _():
            @pl.loop(1, NTP)
            def _(k):
                ss_copy(k).wait_recv()

            summed = ss_recv[0]
            for k in range(1, NTP):
                summed = summed + ss_recv[k]
            r = lax.rsqrt(summed * (1.0 / MODEL) + EPSILON)
            for c in range(NCHUNK):
                rfull[c * CHUNK : (c + 1) * CHUNK, :] = jnp.broadcast_to(
                    r[c : c + 1, :], (CHUNK, 128)
                ).T

        @pl.when(i >= 1)
        def _():
            for kind in (2, 5, 6, 7, 8):
                ag_copy(i - 1, kind).wait_recv()
            project(chunk_of(i - 1))

        @pl.when(i == 1)
        def _():
            halo_send[...] = xf[ROWS : ROWS + 16, :].astype(BF16)
            halo_copy.start()

        @pl.when(i < NCHUNK)
        def _():
            ag_copy(i, 3).wait_recv()
            ag_copy(i, 7).start()
            ag_copy(i, 4).wait_recv()
            ag_copy(i, 8).start()

        @pl.when(i == 2)
        def _():
            halo_copy.wait_recv()
            xf[0:16, :] = jnp.where(seq > 0, halo_recv[...].astype(F32), 0.0)

        @pl.when(i >= 2)
        def _():
            scan_chunk(i - 2)

        @pl.when((i >= 1) & (i < NCHUNK))
        def _():
            project_gate(chunk_of(i - 1))

        @pl.when((i >= 2) & (i < NCHUNK))
        def _():
            outputs_of(i - 2)

    scan_chunk(NCHUNK - 1)

    logs = across_heads(total_log[...])
    high = logs.astype(BF16)
    rest = logs - high.astype(F32)
    middle = rest.astype(BF16)
    bits = [high.astype(F32), middle.astype(F32), rest - middle.astype(F32)]
    row16 = iota((16, 128), 0)
    for half in range(2):
        block = jnp.zeros((16, 128), F32)
        for part_at in range(2):
            at = half * 256 + part_at * 128
            for n in range(3):
                block = jnp.where(row16 == part_at * 8 + n, bits[n][:, at : at + 128], block)
        block = block.astype(BF16)
        for n in range(8):
            piece_send[2 * n + half, :, 0:256] = state[
                n * 16 : (n + 1) * 16, half * 256 : (half + 1) * 256
            ].astype(BF16)
            piece_send[2 * n + half, :, 256:384] = block

    def piece_copy(k):
        target = (seq + k) % NSEQ
        return pltpu.make_async_remote_copy(
            src_ref=piece_send.at[target],
            dst_ref=piece_recv.at[seq],
            send_sem=p_ssem.at[k],
            recv_sem=p_rsem.at[k],
            device_id={"seq": target},
            device_id_type=MESH,
        )

    def enter_copy(k):
        target = (seq + k) % NSEQ
        return pltpu.make_async_remote_copy(
            src_ref=enter_send.at[target],
            dst_ref=enter_recv.at[seq],
            send_sem=e_ssem.at[k],
            recv_sem=e_rsem.at[k],
            device_id={"seq": target},
            device_id_type=MESH,
        )

    @pl.loop(1, NSEQ)
    def _(k):
        piece_copy(k).start()

    piece_recv[seq] = piece_send[seq]
    project_gate(chunk_of(NCHUNK - 1))
    outputs_of(NCHUNK - 2)
    carried = init_t[
        pl.ds(pl.multiple_of((seq // 2) * 16, 16), 16),
        pl.ds(pl.multiple_of((seq % 2) * 256, 256), 256),
    ]

    @pl.loop(1, NSEQ)
    def _(k):
        piece_copy(k).wait_recv()

    for s in range(NSEQ):
        enter_send[s] = carried.astype(BF16)
        codes = piece_recv[s, :, 256:384].astype(F32)
        log = jnp.concatenate(
            [codes[0:1] + codes[1:2] + codes[2:3], codes[8:9] + codes[9:10] + codes[10:11]], axis=1
        )
        carried = jnp.exp(log) * carried + piece_recv[s, :, 0:256].astype(F32)

    @pl.loop(1, NSEQ)
    def _(k):
        enter_copy(k).start()

    enter_recv[seq] = enter_send[seq]
    outputs_of(NCHUNK - 1)
    loads[2].wait()

    @pl.loop(1, NSEQ)
    def _(k):
        enter_copy(k).wait_recv()

    for q in range(NSEQ):
        n, half = q // 2, q % 2
        entering[n * 16 : (n + 1) * 16, half * 256 : (half + 1) * 256] = enter_recv[q].astype(F32)

    igain_rows = igain_ref[...].astype(F32)
    igain = jnp.concatenate([igain_rows[j : j + 1, :] for j in range(4)], axis=1)

    def rs_copy(i, kind):
        src, dst, target = (
            (xs.at[i, 0], xr.at[i, 0], sibling),
            (xs.at[i, 1], xr.at[i, 1], sibling),
            (xs.at[i, 2], xr.at[i, 2], sibling),
            (xs.at[i, 3], xr.at[i, 3], sibling),
            (far_send.at[i, 0], far_recv.at[i, 0], tp_up),
            (far_send.at[i, 1], far_recv.at[i, 1], tp_down),
            (near_send.at[i, 0], near_recv.at[i, 0], tp_up),
            (near_send.at[i, 1], near_recv.at[i, 1], tp_down),
        )[kind]
        return pltpu.make_async_remote_copy(
            src_ref=src,
            dst_ref=dst,
            send_sem=rs_ssem.at[i, kind],
            recv_sem=rs_rsem.at[i, kind],
            device_id={"tp": target},
            device_id_type=MESH,
        )

    def out_block(rows, z, to_core):
        at = pl.multiple_of((z * 2 + to_core) * FEAT, FEAT)
        return dot(mx[rows, :], wo[:, pl.ds(at, FEAT)])

    def project_out(c, d, z):
        rows = pl.ds(pl.multiple_of(c * CHUNK, CHUNK), CHUNK)
        xs[c, d] = out_block(rows, z, 1 - core).astype(BF16)
        rs_copy(c, d).start()
        part[c, d] = out_block(rows, z, core)

    @pl.loop(0, NCHUNK + 1)
    def _(i):
        @pl.when(i < NCHUNK)
        def _():
            rows = pl.ds(pl.multiple_of(i * CHUNK, CHUNK), CHUNK)
            memory = (sloc[i] + pre[i][0:1, :] * entering[...]).astype(BF16)
            mixer = y[rows, :] + ec[rows, :] * dot(cmap[rows, :], memory)
            gated = mixer * sz[rows, :]
            scale = lax.rsqrt(jnp.mean(gated * gated, axis=1, keepdims=True) + EPSILON)
            mx[rows, :] = (gated * scale * igain).astype(BF16)
            project_out(i, 0, far)

        @pl.when(i >= 1)
        def _():
            c = i - 1
            rs_copy(c, 0).wait_recv()
            whole = (part[c, 0] + xr[c, 0].astype(F32)).astype(BF16)
            far_send[c, 0] = whole[:HALF]
            rs_copy(c, 4).start()
            far_send[c, 1] = whole[HALF:]
            rs_copy(c, 5).start()

    @pl.loop(0, NCHUNK + 1)
    def _(i):
        @pl.when(i < NCHUNK)
        def _():
            project_out(i, 1, up)
            project_out(i, 2, down)

        @pl.when(i >= 1)
        def _():
            c = i - 1
            rs_copy(c, 1).wait_recv()
            rs_copy(c, 4).wait_recv()
            whole = part[c, 1] + xr[c, 1].astype(F32)
            near_send[c, 0, 0:HALF] = (whole[:HALF] + far_recv[c, 0].astype(F32)).astype(BF16)
            near_send[c, 0, HALF:CHUNK] = whole[HALF:].astype(BF16)
            rs_copy(c, 6).start()
            rs_copy(c, 2).wait_recv()
            rs_copy(c, 5).wait_recv()
            whole = part[c, 2] + xr[c, 2].astype(F32)
            near_send[c, 1, 0:HALF] = whole[:HALF].astype(BF16)
            near_send[c, 1, HALF:CHUNK] = (whole[HALF:] + far_recv[c, 1].astype(F32)).astype(BF16)
            rs_copy(c, 7).start()

    @pl.loop(0, NCHUNK)
    def _(c):
        project_out(c, 3, chip)

    @pl.loop(0, NCHUNK)
    def _(c):
        rows = pl.ds(pl.multiple_of(c * CHUNK, CHUNK), CHUNK)
        rs_copy(c, 3).wait_recv()
        summed = hidden[rows, :].astype(F32) + (part[c, 3] + xr[c, 3].astype(F32))
        rs_copy(c, 6).wait_recv()
        summed = summed + near_recv[c, 0].astype(F32)
        rs_copy(c, 7).wait_recv()
        out_ref[rows, :] = (summed + near_recv[c, 1].astype(F32)).astype(BF16)

    @pl.loop(0, NCHUNK)
    def _(i):
        for kind in range(RING_AG):
            ag_copy(i, kind).wait_send()
        for kind in range(RING_RS):
            rs_copy(i, kind).wait_send()

    @pl.loop(1, NTP)
    def _(k):
        ss_copy(k).wait_send()

    halo_copy.wait_send()

    @pl.loop(1, NSEQ)
    def _(k):
        piece_copy(k).wait_send()
        enter_copy(k).wait_send()


def on_device(
    hidden,
    norm_gain,
    gate_x_weight,
    state_weight,
    step_weight,
    conv_inner,
    conv_state,
    step_bias,
    decay_log,
    skip_gain,
    inner_gain,
    out_weight,
    initial_state,
):
    gx = gate_x_weight.reshape(MODEL, 2, 4, 128).transpose(0, 2, 1, 3).reshape(MODEL * 8, 128)
    sw = state_weight.reshape(MODEL * 2, 128)
    vmem = pl.BlockSpec(memory_space=pltpu.VMEM)
    smem = pl.BlockSpec(memory_space=pltpu.SMEM)
    anywhere = pl.BlockSpec(memory_space=pl.ANY)
    V = pltpu.VMEM
    dma = pltpu.SemaphoreType.DMA
    return pl.pallas_call(
        kernel,
        out_shape=jax.ShapeDtypeStruct((ROWS, FEAT), BF16),
        in_specs=[
            vmem, vmem, anywhere, anywhere, vmem, vmem, vmem, smem, smem, smem, vmem, anywhere, vmem,
        ],
        out_specs=vmem,
        scratch_shapes=[
            V((MODEL * 8, 128), BF16),
            V((MODEL * 2, 128), BF16),
            V((MODEL, COLS), BF16),
            V((FEAT, MODEL), BF16),
            V((ROWS, MODEL), BF16),
            V((8, 128), F32),
            V((NTP, 8, 128), F32),
            V((ROWS, 128), F32),
            V((ROWS + 16, 768), F32),
            V((8, ROWS), F32),
            V((ROWS, FEAT), F32),
            V((ROWS, FEAT), F32),
            V((ROWS, FEAT), F32),
            V((NCHUNK, STATE, FEAT), F32),
            V((NCHUNK, 8, FEAT), F32),
            V((STATE, FEAT), F32),
            V((8, 128), F32),
            V((ROWS, STATE), BF16),
            V((ROWS, FEAT), BF16),
            V((NCHUNK, STATE, CHUNK), BF16),
            V((NCHUNK, CHUNK, 128), F32),
            V((NCHUNK, HEADS, CHUNK), F32),
            V((NCHUNK, HEADS, CHUNK), F32),
            V((ROWS, FEAT), BF16),
            V((16, 768), BF16),
            V((16, 768), BF16),
            V((NSEQ, 16, 384), BF16),
            V((NSEQ, 16, 384), BF16),
            V((NSEQ, 16, 256), BF16),
            V((NSEQ, 16, 256), BF16),
            V((STATE, FEAT), F32),
            V((STATE, FEAT), F32),
            V((NCHUNK, 4, CHUNK, FEAT), BF16),
            V((NCHUNK, 4, CHUNK, FEAT), BF16),
            V((NCHUNK, 4, CHUNK, FEAT), F32),
            V((NCHUNK, 2, HALF, FEAT), BF16),
            V((NCHUNK, 2, CHUNK, FEAT), BF16),
            V((NCHUNK, 2, HALF, FEAT), BF16),
            V((NCHUNK, 2, CHUNK, FEAT), BF16),
            dma((3,)),
            dma((NCHUNK, RING_AG)),
            dma((NCHUNK, RING_AG)),
            dma((NTP,)),
            dma((NTP,)),
            dma,
            dma,
            dma((NSEQ,)),
            dma((NSEQ,)),
            dma((NSEQ,)),
            dma((NSEQ,)),
            dma((NCHUNK, RING_RS)),
            dma((NCHUNK, RING_RS)),
        ],
        compiler_params=pltpu.CompilerParams(
            collective_id=0, has_side_effects=True, vmem_limit_bytes=61 << 20
        ),
    )(
        hidden,
        norm_gain.reshape(MODEL // 128, 128),
        gx,
        sw,
        step_weight.T,
        conv_inner,
        conv_state.reshape(8, 128),
        step_bias,
        decay_log,
        skip_gain,
        inner_gain.reshape(4, 128),
        out_weight,
        initial_state.reshape(HEADS * WIDTH, STATE),
    )


def solution(mesh):
    return jax.shard_map(
        on_device,
        mesh=mesh,
        in_specs=(
            P("seq", "tp"),
            P(),
            P(None, None, "tp"),
            P(None, None, "tp"),
            P(None, "tp"),
            P(None, "tp"),
            P(None, None, "tp"),
            P("tp"),
            P("tp"),
            P("tp"),
            P("tp"),
            P("tp", None),
            P("tp", None, None),
        ),
        out_specs=P("seq", "tp"),
        check_vma=False,
    )
```

```python
import functools

import jax
import jax.numpy as jnp
from jax import lax
from jax.experimental import pallas as pl
from jax.experimental.pallas import tpu as pltpu
from jax.sharding import PartitionSpec as P

F32 = jnp.float32
BF16 = jnp.bfloat16
EPSILON = 1e-05
MESH = pl.DeviceIdType.MESH
HIGHEST = lax.Precision.HIGHEST

ROWS = 512
FEAT = 512
MODEL = 4096
HEADS = 8
WIDTH = 64
STATE = 128
CHUNK = 128
NCHUNK = ROWS // CHUNK
HALF = CHUNK // 2
NSEQ = 16
NTP = 8
NCHIP = 4
COLS = 1408
RING_AG = 9
RING_RS = 8


def silu(v):
    return v / (1.0 + jnp.exp(-v))


def softplus(v):
    return jnp.maximum(v, 0.0) + jnp.log1p(jnp.exp(-jnp.abs(v)))


def dot(a, b, precision=None):
    return jnp.dot(a, b, preferred_element_type=F32, precision=precision)


def iota(shape, dim):
    return lax.broadcasted_iota(jnp.int32, shape, dim)


def across_heads(rows):
    lane = iota((1, 128), 1)
    parts = [
        jnp.where(lane < WIDTH, rows[2 * j : 2 * j + 1, :], rows[2 * j + 1 : 2 * j + 2, :])
        for j in range(4)
    ]
    return jnp.concatenate(parts, axis=1)


def kernel(
    hidden,
    gain_ref,
    gx_hbm,
    sw_hbm,
    stepw_ref,
    tap_x,
    tap_s,
    bias_ref,
    decay_ref,
    skip_ref,
    igain_ref,
    wo_hbm,
    init_ref,
    out_ref,
    gx_raw,
    sw_raw,
    w,
    wo,
    g,
    ss_send,
    ss_recv,
    rfull,
    xf,
    steps,
    sz,
    y,
    ec,
    sloc,
    pre,
    state,
    total_log,
    cmap,
    vals,
    bmap_t,
    cols_t,
    cum_rows,
    step_rows,
    mx,
    halo_send,
    halo_recv,
    piece_send,
    piece_recv,
    enter_send,
    enter_recv,
    init_t,
    entering,
    xs,
    xr,
    part,
    far_send,
    near_send,
    far_recv,
    near_recv,
    load_sem,
    ag_send,
    ag_recv,
    ss_ssem,
    ss_rsem,
    halo_ssem,
    halo_rsem,
    p_ssem,
    p_rsem,
    e_ssem,
    e_rsem,
    rs_ssem,
    rs_rsem,
):
    seq = lax.axis_index("seq")
    tp = lax.axis_index("tp")
    chip = tp // 2
    core = tp % 2
    up = (chip + 1) % NCHIP
    down = (chip + 3) % NCHIP
    far = (chip + 2) % NCHIP
    tp_up = up * 2 + core
    tp_down = down * 2 + core
    tp_far = far * 2 + core
    sibling = chip * 2 + (1 - core)

    loads = [
        pltpu.make_async_copy(gx_hbm, gx_raw, load_sem.at[0]),
        pltpu.make_async_copy(sw_hbm, sw_raw, load_sem.at[1]),
        pltpu.make_async_copy(wo_hbm, wo, load_sem.at[2]),
    ]
    loads[0].start()
    loads[1].start()

    barrier = pltpu.get_barrier_semaphore()

    @pl.loop(1, NTP)
    def _(k):
        pl.semaphore_signal(
            barrier, inc=1, device_id={"tp": (tp + k) % NTP}, device_id_type=MESH
        )

    @pl.loop(1, NSEQ)
    def _(k):
        pl.semaphore_signal(
            barrier, inc=1, device_id={"seq": (seq + k) % NSEQ}, device_id_type=MESH
        )

    gain_rows = gain_ref[...].astype(F32)
    gain_at = iota((MODEL // 128, 128), 0)
    gain = jnp.concatenate(
        [
            jnp.sum(jnp.where(gain_at == tp * 4 + j, gain_rows, 0.0), axis=0, keepdims=True)
            for j in range(4)
        ],
        axis=1,
    )
    own = pl.ds(pl.multiple_of(tp * FEAT, FEAT), FEAT)
    squares = []
    for c in range(NCHUNK):
        rows = slice(c * CHUNK, (c + 1) * CHUNK)
        h = hidden[rows, :].astype(F32)
        g[rows, own] = (h * gain).astype(BF16)
        summed = jnp.sum(h * h, axis=1, keepdims=True)
        squares.append(jnp.broadcast_to(summed, (CHUNK, 128)).T[0:1, :])
    ss_send[...] = jnp.concatenate(squares + [jnp.zeros((4, 128), F32)], axis=0)

    pl.semaphore_wait(barrier, NTP - 1 + NSEQ - 1)

    def ag_copy(step, kind):
        row = pl.multiple_of(((step + NCHUNK - 1) % NCHUNK) * CHUNK, CHUNK)
        whole, first, second = (row, CHUNK), (row, HALF), (pl.multiple_of(row + HALF, HALF), HALF)
        (start, size), shard, target = (
            (whole, tp, tp_up),
            (whole, tp, tp_down),
            (whole, tp, sibling),
            (first, tp_down, tp_up),
            (second, tp_up, tp_down),
            (whole, tp_down, sibling),
            (whole, tp_up, sibling),
            (first, tp_far, sibling),
            (second, tp_far, sibling),
        )[kind]
        block = g.at[pl.ds(start, size), pl.ds(pl.multiple_of(shard * FEAT, FEAT), FEAT)]
        return pltpu.make_async_remote_copy(
            src_ref=block,
            dst_ref=block,
            send_sem=ag_send.at[step, kind],
            recv_sem=ag_recv.at[step, kind],
            device_id={"tp": target},
            device_id_type=MESH,
        )

    def send_own(step):
        for kind in (0, 1, 2):
            ag_copy(step, kind).start()

    send_own(0)

    def ss_copy(k):
        return pltpu.make_async_remote_copy(
            src_ref=ss_send,
            dst_ref=ss_recv.at[tp],
            send_sem=ss_ssem.at[k],
            recv_sem=ss_rsem.at[k],
            device_id={"tp": (tp + k) % NTP},
            device_id_type=MESH,
        )

    @pl.loop(1, NTP)
    def _(k):
        ss_copy(k).start()

    ss_recv[tp] = ss_send[...]

    loads[0].wait()
    o256, i256 = iota((256, 256), 0), iota((256, 256), 1)
    pick = jnp.where(i256 == (o256 % 32) * 8 + o256 // 32, 1.0, 0.0).astype(BF16)

    def sort_gate_x(b):
        at = pl.multiple_of(b * 512, 512)
        k0 = pl.multiple_of(b * 64, 64)
        both = jnp.concatenate([gx_raw[pl.ds(at, 256), :], gx_raw[pl.ds(at + 256, 256), :]], axis=1)
        sorted_rows = dot(pick, both).astype(BF16)
        for m in range(8):
            column = (m % 2) * 512 + (m // 2) * 128
            rows = sorted_rows[m * 32 : (m + 1) * 32, :]
            w[pl.ds(k0, 32), column : column + 128] = rows[:, :128]
            w[pl.ds(k0 + 32, 32), column : column + 128] = rows[:, 128:]

    pl.loop(0, 32, unroll=16)(sort_gate_x)
    send_own(1)
    pl.loop(32, 64, unroll=16)(sort_gate_x)
    loads[1].wait()
    loads[2].start()
    pick_state = jnp.where(i256 == (o256 % 128) * 2 + o256 // 128, 1.0, 0.0).astype(BF16)

    @pl.loop(0, 16, unroll=8)
    def _(b):
        at = pl.multiple_of(b * 512, 512)
        k0 = pl.multiple_of(b * 256, 256)
        both = jnp.concatenate([sw_raw[pl.ds(at, 256), :], sw_raw[pl.ds(at + 256, 256), :]], axis=1)
        sorted_rows = dot(pick_state, both).astype(BF16)
        for m in range(2):
            column = 1024 + m * 128
            rows = sorted_rows[m * 128 : (m + 1) * 128, :]
            w[pl.ds(k0, 128), column : column + 128] = rows[:, :128]
            w[pl.ds(k0 + 128, 128), column : column + 128] = rows[:, 128:]

    @pl.loop(0, 32, unroll=8)
    def _(b):
        at = pl.multiple_of(b * 128, 128)
        rows = stepw_ref[:, pl.ds(at, 128)].astype(F32)
        square = jnp.concatenate([rows, jnp.zeros((120, 128), F32)], axis=0)
        w[pl.ds(at, 128), 1280:1408] = square.T.astype(BF16)

    for j in range(4):
        init_t[:, j * 128 : (j + 1) * 128] = init_ref[j * 128 : (j + 1) * 128, :].T

    lane512 = iota((1, 512), 1)
    row8 = iota((8, 128), 0)
    bias = jnp.zeros((8, 128), F32)
    rate = jnp.zeros((8, 128), F32)
    skip = jnp.zeros((1, 512), F32)
    for h in range(HEADS):
        bias = jnp.where(row8 == h, bias_ref[h], bias)
        rate = jnp.where(row8 == h, decay_ref[h], rate)
        skip = jnp.where(lane512 // WIDTH == h, skip_ref[h], skip)
    rate = jnp.exp(rate)
    r128, c128 = iota((128, 128), 0), iota((128, 128), 1)
    causal = r128 >= c128
    upper = jnp.where(r128 <= c128, 1.0, 0.0)
    s_row, s_lane = iota((128, 512), 0), iota((128, 512), 1)
    spread_decay = jnp.where(s_row == HEADS + s_lane // WIDTH, 1.0, 0.0).astype(BF16)
    spread_step = jnp.where(s_row == 2 * HEADS + s_lane // WIDTH, 1.0, 0.0).astype(BF16)

    state[...] = jnp.zeros((STATE, FEAT), F32)
    total_log[...] = jnp.zeros((8, 128), F32)

    halo_copy = pltpu.make_async_remote_copy(
        src_ref=halo_send,
        dst_ref=halo_recv,
        send_sem=halo_ssem,
        recv_sem=halo_rsem,
        device_id={"seq": (seq + 1) % NSEQ},
        device_id_type=MESH,
    )

    def chunk_of(step):
        return (step + NCHUNK - 1) % NCHUNK

    def project(c):
        row = pl.multiple_of(c * CHUNK, CHUNK)
        rows = pl.ds(row, CHUNK)
        r = rfull[rows, :]
        product = dot(g[rows, :], w[:, 512:COLS])
        for n in range(6):
            raw = (product[:, n * 128 : (n + 1) * 128] * r).astype(BF16).astype(F32)
            xf[pl.ds(pl.multiple_of(row + 16, 16), CHUNK), n * 128 : (n + 1) * 128] = raw
        raw_step = (product[:, 768:896] * r).astype(BF16).astype(F32)
        steps[:, rows] = raw_step.T[0:HEADS, :]

    def project_gate(c):
        rows = pl.ds(pl.multiple_of(c * CHUNK, CHUNK), CHUNK)
        r = rfull[rows, :]
        product = dot(g[rows, :], w[:, 0:512])
        for n in range(4):
            z = (product[:, n * 128 : (n + 1) * 128] * r).astype(BF16).astype(F32)
            sz[rows, n * 128 : (n + 1) * 128] = silu(z)

    def scan_chunk(c):
        row = pl.multiple_of(c * CHUNK, CHUNK)
        rows = pl.ds(row, CHUNK)

        def filtered(cols, taps):
            padded = xf[pl.ds(pl.multiple_of(row + 8, 8), CHUNK + 8), cols]
            summed = taps[0] * padded[5 : 5 + CHUNK]
            for k in range(1, 4):
                summed = summed + taps[k] * padded[5 + k : 5 + k + CHUNK]
            return silu(summed).astype(BF16)

        taps_x = tap_x[...].astype(F32)
        taps_s = tap_s[...].astype(F32)
        values = jnp.concatenate(
            [
                filtered(
                    slice(j * 128, (j + 1) * 128),
                    [taps_x[k : k + 1, j * 128 : (j + 1) * 128] for k in range(4)],
                )
                for j in range(4)
            ],
            axis=1,
        )
        in_map, out_map = (
            filtered(
                slice(512 + m * 128, 640 + m * 128),
                [taps_s[2 * k + m : 2 * k + m + 1, :] for k in range(4)],
            )
            for m in range(2)
        )
        cmap[rows, :] = out_map
        vals[rows, :] = values
        in_map_t = in_map.astype(F32).T.astype(BF16)
        step = softplus(steps[:, rows] + bias)
        cum = dot(-step * rate, upper, HIGHEST)
        last = jnp.broadcast_to(cum[:, 127:128], (8, 128))
        kept = step * jnp.exp(last - cum)
        columns = jnp.concatenate(
            [cum, jnp.exp(cum), kept, jnp.zeros((104, 128), F32)], axis=0
        ).T
        bmap_t[c] = in_map_t
        cols_t[c] = columns
        cum_rows[c] = cum
        step_rows[c] = step
        high = columns.astype(BF16)
        low = (columns - high.astype(F32)).astype(BF16)
        step_exp = dot(high, spread_step) + dot(low, spread_step)
        wide = values.astype(F32)
        weighted = (wide * step_exp).astype(BF16)
        before = state[...]
        sloc[c] = before
        pre[c] = jnp.broadcast_to(jnp.exp(across_heads(total_log[...])), (8, FEAT))
        total_log[...] += last
        state[...] = jnp.exp(across_heads(last)) * before + dot(in_map_t, weighted)

    def outputs_of(c):
        rows = pl.ds(pl.multiple_of(c * CHUNK, CHUNK), CHUNK)
        columns, cum, step = cols_t[c], cum_rows[c], step_rows[c]
        high = columns.astype(BF16)
        low = (columns - high.astype(F32)).astype(BF16)
        ec[rows, :] = dot(high, spread_decay) + dot(low, spread_decay)
        scores = dot(cmap[rows, :], bmap_t[c])
        lane = iota((CHUNK, 128), 1)
        for j in range(4):
            cols = slice(j * 128, (j + 1) * 128)
            pair = vals[rows, cols]
            both = []
            for h in (2 * j, 2 * j + 1):
                spread = columns[:, h : h + 1] - cum[h : h + 1, :]
                weights = jnp.exp(jnp.where(causal, spread, -1e30))
                both.append(dot((scores * weights * step[h : h + 1, :]).astype(BF16), pair))
            y[rows, cols] = (
                jnp.where(lane < WIDTH, both[0], both[1]) + skip[:, cols] * pair.astype(F32)
            )

    @pl.loop(0, NCHUNK + 2)
    def _(i):
        @pl.when(i == 2)
        def _():
            @pl.loop(1, NTP)
            def _(k):
                ss_copy(k).wait_recv()

            summed = ss_recv[0]
            for k in range(1, NTP):
                summed = summed + ss_recv[k]
            r = lax.rsqrt(summed * (1.0 / MODEL) + EPSILON)
            for c in range(NCHUNK):
                rfull[c * CHUNK : (c + 1) * CHUNK, :] = jnp.broadcast_to(
                    r[c : c + 1, :], (CHUNK, 128)
                ).T

        @pl.when(i >= 2)
        def _():
            for kind in (2, 5, 6, 7, 8):
                ag_copy(i - 2, kind).wait_recv()
            project(chunk_of(i - 2))

        @pl.when(i == 2)
        def _():
            halo_send[...] = xf[ROWS : ROWS + 16, :].astype(BF16)
            halo_copy.start()

        @pl.when(i < NCHUNK)
        def _():
            ag_copy(i, 0).wait_recv()
            ag_copy(i, 3).start()
            ag_copy(i, 5).start()
            ag_copy(i, 1).wait_recv()
            ag_copy(i, 4).start()
            ag_copy(i, 6).start()

        @pl.when(i < NCHUNK - 2)
        def _():
            send_own(i + 2)

        @pl.when((i >= 1) & (i <= NCHUNK))
        def _():
            ag_copy(i - 1, 3).wait_recv()
            ag_copy(i - 1, 7).start()
            ag_copy(i - 1, 4).wait_recv()
            ag_copy(i - 1, 8).start()

        @pl.when(i == 3)
        def _():
            halo_copy.wait_recv()
            xf[0:16, :] = jnp.where(seq > 0, halo_recv[...].astype(F32), 0.0)

        @pl.when(i >= 3)
        def _():
            scan_chunk(i - 3)

        @pl.when((i >= 2) & (i <= NCHUNK))
        def _():
            project_gate(chunk_of(i - 2))

    scan_chunk(NCHUNK - 1)

    logs = across_heads(total_log[...])
    high = logs.astype(BF16)
    rest = logs - high.astype(F32)
    middle = rest.astype(BF16)
    bits = [high.astype(F32), middle.astype(F32), rest - middle.astype(F32)]
    row16 = iota((16, 128), 0)
    for half in range(2):
        block = jnp.zeros((16, 128), F32)
        for part_at in range(2):
            at = half * 256 + part_at * 128
            for n in range(3):
                block = jnp.where(row16 == part_at * 8 + n, bits[n][:, at : at + 128], block)
        block = block.astype(BF16)
        for n in range(8):
            piece_send[2 * n + half, :, 0:256] = state[
                n * 16 : (n + 1) * 16, half * 256 : (half + 1) * 256
            ].astype(BF16)
            piece_send[2 * n + half, :, 256:384] = block

    def piece_copy(k):
        target = (seq + k) % NSEQ
        return pltpu.make_async_remote_copy(
            src_ref=piece_send.at[target],
            dst_ref=piece_recv.at[seq],
            send_sem=p_ssem.at[k],
            recv_sem=p_rsem.at[k],
            device_id={"seq": target},
            device_id_type=MESH,
        )

    def enter_copy(k):
        target = (seq + k) % NSEQ
        return pltpu.make_async_remote_copy(
            src_ref=enter_send.at[target],
            dst_ref=enter_recv.at[seq],
            send_sem=e_ssem.at[k],
            recv_sem=e_rsem.at[k],
            device_id={"seq": target},
            device_id_type=MESH,
        )

    @pl.loop(1, NSEQ)
    def _(k):
        piece_copy(k).start()

    piece_recv[seq] = piece_send[seq]
    project_gate(chunk_of(NCHUNK - 1))
    outputs_of(0)
    outputs_of(1)
    carried = init_t[
        pl.ds(pl.multiple_of((seq // 2) * 16, 16), 16),
        pl.ds(pl.multiple_of((seq % 2) * 256, 256), 256),
    ]

    @pl.loop(1, NSEQ)
    def _(k):
        piece_copy(k).wait_recv()

    for s in range(NSEQ):
        enter_send[s] = carried.astype(BF16)
        codes = piece_recv[s, :, 256:384].astype(F32)
        log = jnp.concatenate(
            [codes[0:1] + codes[1:2] + codes[2:3], codes[8:9] + codes[9:10] + codes[10:11]], axis=1
        )
        carried = jnp.exp(log) * carried + piece_recv[s, :, 0:256].astype(F32)

    @pl.loop(1, NSEQ)
    def _(k):
        enter_copy(k).start()

    enter_recv[seq] = enter_send[seq]
    outputs_of(2)
    outputs_of(3)
    loads[2].wait()

    @pl.loop(1, NSEQ)
    def _(k):
        enter_copy(k).wait_recv()

    for q in range(NSEQ):
        n, half = q // 2, q % 2
        entering[n * 16 : (n + 1) * 16, half * 256 : (half + 1) * 256] = enter_recv[q].astype(F32)

    igain_rows = igain_ref[...].astype(F32)
    igain = jnp.concatenate([igain_rows[j : j + 1, :] for j in range(4)], axis=1)

    def rs_copy(i, kind):
        src, dst, target = (
            (xs.at[i, 0], xr.at[i, 0], sibling),
            (xs.at[i, 1], xr.at[i, 1], sibling),
            (xs.at[i, 2], xr.at[i, 2], sibling),
            (xs.at[i, 3], xr.at[i, 3], sibling),
            (far_send.at[i, 0], far_recv.at[i, 0], tp_up),
            (far_send.at[i, 1], far_recv.at[i, 1], tp_down),
            (near_send.at[i, 0], near_recv.at[i, 0], tp_up),
            (near_send.at[i, 1], near_recv.at[i, 1], tp_down),
        )[kind]
        return pltpu.make_async_remote_copy(
            src_ref=src,
            dst_ref=dst,
            send_sem=rs_ssem.at[i, kind],
            recv_sem=rs_rsem.at[i, kind],
            device_id={"tp": target},
            device_id_type=MESH,
        )

    def out_block(rows, z, to_core):
        at = pl.multiple_of((z * 2 + to_core) * FEAT, FEAT)
        return dot(mx[rows, :], wo[:, pl.ds(at, FEAT)])

    def project_out(c, d, z):
        rows = pl.ds(pl.multiple_of(c * CHUNK, CHUNK), CHUNK)
        xs[c, d] = out_block(rows, z, 1 - core).astype(BF16)
        rs_copy(c, d).start()
        part[c, d] = out_block(rows, z, core)

    @pl.loop(0, NCHUNK + 1)
    def _(i):
        @pl.when(i < NCHUNK)
        def _():
            rows = pl.ds(pl.multiple_of(i * CHUNK, CHUNK), CHUNK)
            memory = (sloc[i] + pre[i][0:1, :] * entering[...]).astype(BF16)
            mixer = y[rows, :] + ec[rows, :] * dot(cmap[rows, :], memory)
            gated = mixer * sz[rows, :]
            scale = lax.rsqrt(jnp.mean(gated * gated, axis=1, keepdims=True) + EPSILON)
            mx[rows, :] = (gated * scale * igain).astype(BF16)
            project_out(i, 0, far)

        @pl.when(i >= 1)
        def _():
            c = i - 1
            rs_copy(c, 0).wait_recv()
            whole = (part[c, 0] + xr[c, 0].astype(F32)).astype(BF16)
            far_send[c, 0] = whole[:HALF]
            rs_copy(c, 4).start()
            far_send[c, 1] = whole[HALF:]
            rs_copy(c, 5).start()

    @pl.loop(0, NCHUNK + 1)
    def _(i):
        @pl.when(i < NCHUNK)
        def _():
            project_out(i, 1, up)
            project_out(i, 2, down)

        @pl.when(i >= 1)
        def _():
            c = i - 1
            rs_copy(c, 1).wait_recv()
            rs_copy(c, 4).wait_recv()
            whole = part[c, 1] + xr[c, 1].astype(F32)
            near_send[c, 0, 0:HALF] = (whole[:HALF] + far_recv[c, 0].astype(F32)).astype(BF16)
            near_send[c, 0, HALF:CHUNK] = whole[HALF:].astype(BF16)
            rs_copy(c, 6).start()
            rs_copy(c, 2).wait_recv()
            rs_copy(c, 5).wait_recv()
            whole = part[c, 2] + xr[c, 2].astype(F32)
            near_send[c, 1, 0:HALF] = whole[:HALF].astype(BF16)
            near_send[c, 1, HALF:CHUNK] = (whole[HALF:] + far_recv[c, 1].astype(F32)).astype(BF16)
            rs_copy(c, 7).start()

    @pl.loop(0, NCHUNK)
    def _(c):
        project_out(c, 3, chip)

    @pl.loop(0, NCHUNK)
    def _(c):
        rows = pl.ds(pl.multiple_of(c * CHUNK, CHUNK), CHUNK)
        rs_copy(c, 3).wait_recv()
        summed = hidden[rows, :].astype(F32) + (part[c, 3] + xr[c, 3].astype(F32))
        rs_copy(c, 6).wait_recv()
        summed = summed + near_recv[c, 0].astype(F32)
        rs_copy(c, 7).wait_recv()
        out_ref[rows, :] = (summed + near_recv[c, 1].astype(F32)).astype(BF16)

    @pl.loop(0, NCHUNK)
    def _(i):
        for kind in range(RING_AG):
            ag_copy(i, kind).wait_send()
        for kind in range(RING_RS):
            rs_copy(i, kind).wait_send()

    @pl.loop(1, NTP)
    def _(k):
        ss_copy(k).wait_send()

    halo_copy.wait_send()

    @pl.loop(1, NSEQ)
    def _(k):
        piece_copy(k).wait_send()
        enter_copy(k).wait_send()


def on_device(
    hidden,
    norm_gain,
    gate_x_weight,
    state_weight,
    step_weight,
    conv_inner,
    conv_state,
    step_bias,
    decay_log,
    skip_gain,
    inner_gain,
    out_weight,
    initial_state,
):
    gx = gate_x_weight.reshape(MODEL, 2, 4, 128).transpose(0, 2, 1, 3).reshape(MODEL * 8, 128)
    sw = state_weight.reshape(MODEL * 2, 128)
    vmem = pl.BlockSpec(memory_space=pltpu.VMEM)
    smem = pl.BlockSpec(memory_space=pltpu.SMEM)
    anywhere = pl.BlockSpec(memory_space=pl.ANY)
    V = pltpu.VMEM
    dma = pltpu.SemaphoreType.DMA
    return pl.pallas_call(
        kernel,
        out_shape=jax.ShapeDtypeStruct((ROWS, FEAT), BF16),
        in_specs=[
            vmem, vmem, anywhere, anywhere, vmem, vmem, vmem, smem, smem, smem, vmem, anywhere, vmem,
        ],
        out_specs=vmem,
        scratch_shapes=[
            V((MODEL * 8, 128), BF16),
            V((MODEL * 2, 128), BF16),
            V((MODEL, COLS), BF16),
            V((FEAT, MODEL), BF16),
            V((ROWS, MODEL), BF16),
            V((8, 128), F32),
            V((NTP, 8, 128), F32),
            V((ROWS, 128), F32),
            V((ROWS + 16, 768), F32),
            V((8, ROWS), F32),
            V((ROWS, FEAT), F32),
            V((ROWS, FEAT), F32),
            V((ROWS, FEAT), F32),
            V((NCHUNK, STATE, FEAT), F32),
            V((NCHUNK, 8, FEAT), F32),
            V((STATE, FEAT), F32),
            V((8, 128), F32),
            V((ROWS, STATE), BF16),
            V((ROWS, FEAT), BF16),
            V((NCHUNK, STATE, CHUNK), BF16),
            V((NCHUNK, CHUNK, 128), F32),
            V((NCHUNK, HEADS, CHUNK), F32),
            V((NCHUNK, HEADS, CHUNK), F32),
            V((ROWS, FEAT), BF16),
            V((16, 768), BF16),
            V((16, 768), BF16),
            V((NSEQ, 16, 384), BF16),
            V((NSEQ, 16, 384), BF16),
            V((NSEQ, 16, 256), BF16),
            V((NSEQ, 16, 256), BF16),
            V((STATE, FEAT), F32),
            V((STATE, FEAT), F32),
            V((NCHUNK, 4, CHUNK, FEAT), BF16),
            V((NCHUNK, 4, CHUNK, FEAT), BF16),
            V((NCHUNK, 4, CHUNK, FEAT), F32),
            V((NCHUNK, 2, HALF, FEAT), BF16),
            V((NCHUNK, 2, CHUNK, FEAT), BF16),
            V((NCHUNK, 2, HALF, FEAT), BF16),
            V((NCHUNK, 2, CHUNK, FEAT), BF16),
            dma((3,)),
            dma((NCHUNK, RING_AG)),
            dma((NCHUNK, RING_AG)),
            dma((NTP,)),
            dma((NTP,)),
            dma,
            dma,
            dma((NSEQ,)),
            dma((NSEQ,)),
            dma((NSEQ,)),
            dma((NSEQ,)),
            dma((NCHUNK, RING_RS)),
            dma((NCHUNK, RING_RS)),
        ],
        compiler_params=pltpu.CompilerParams(
            collective_id=0, has_side_effects=True, vmem_limit_bytes=61 << 20
        ),
    )(
        hidden,
        norm_gain.reshape(MODEL // 128, 128),
        gx,
        sw,
        step_weight.T,
        conv_inner,
        conv_state.reshape(8, 128),
        step_bias,
        decay_log,
        skip_gain,
        inner_gain.reshape(4, 128),
        out_weight,
        initial_state.reshape(HEADS * WIDTH, STATE),
    )


def solution(mesh):
    return jax.shard_map(
        on_device,
        mesh=mesh,
        in_specs=(
            P("seq", "tp"),
            P(),
            P(None, None, "tp"),
            P(None, None, "tp"),
            P(None, "tp"),
            P(None, "tp"),
            P(None, None, "tp"),
            P("tp"),
            P("tp"),
            P("tp"),
            P("tp"),
            P("tp", None),
            P("tp", None, None),
        ),
        out_specs=P("seq", "tp"),
        check_vma=False,
    )
```

```python
import functools

import jax
import jax.numpy as jnp
from jax import lax
from jax.experimental import pallas as pl
from jax.experimental.pallas import tpu as pltpu
from jax.sharding import PartitionSpec as P

F32 = jnp.float32
BF16 = jnp.bfloat16
EPSILON = 1e-05
MESH = pl.DeviceIdType.MESH
HIGHEST = lax.Precision.HIGHEST

ROWS = 512
FEAT = 512
MODEL = 4096
HEADS = 8
WIDTH = 64
STATE = 128
CHUNK = 128
NCHUNK = ROWS // CHUNK
HALF = CHUNK // 2
NSEQ = 16
NTP = 8
NCHIP = 4
COLS = 1408
RING_AG = 9
RING_RS = 8


def silu(v):
    return v / (1.0 + jnp.exp(-v))


def softplus(v):
    return jnp.maximum(v, 0.0) + jnp.log1p(jnp.exp(-jnp.abs(v)))


def dot(a, b, precision=None):
    return jnp.dot(a, b, preferred_element_type=F32, precision=precision)


def iota(shape, dim):
    return lax.broadcasted_iota(jnp.int32, shape, dim)


def across_heads(rows):
    lane = iota((1, 128), 1)
    parts = [
        jnp.where(lane < WIDTH, rows[2 * j : 2 * j + 1, :], rows[2 * j + 1 : 2 * j + 2, :])
        for j in range(4)
    ]
    return jnp.concatenate(parts, axis=1)


def kernel(
    hidden_hbm,
    gain_hbm,
    gx_hbm,
    sw_hbm,
    stepw_hbm,
    tap_x_hbm,
    tap_s_hbm,
    bias_hbm,
    decay_hbm,
    skip_hbm,
    igain_hbm,
    wo_hbm,
    init_hbm,
    out_hbm,
    hidden,
    gain_ref,
    stepw_ref,
    tap_x,
    tap_s,
    bias_ref,
    decay_ref,
    skip_ref,
    igain_ref,
    init_ref,
    out_ref,
    gx_raw,
    sw_raw,
    w,
    wo,
    g,
    ss_send,
    ss_recv,
    rfull,
    xf,
    steps,
    sz,
    y,
    ec,
    sloc,
    pre,
    state,
    total_log,
    cmap,
    vals,
    bmap_t,
    cols_t,
    cum_rows,
    step_rows,
    mx,
    halo_send,
    halo_recv,
    piece_send,
    piece_recv,
    enter_send,
    enter_recv,
    init_t,
    entering,
    xs,
    xr,
    part,
    far_send,
    near_send,
    far_recv,
    near_recv,
    load_sem,
    out_sem,
    ag_send,
    ag_recv,
    ss_ssem,
    ss_rsem,
    halo_ssem,
    halo_rsem,
    p_ssem,
    p_rsem,
    e_ssem,
    e_rsem,
    rs_ssem,
    rs_rsem,
):
    seq = lax.axis_index("seq")
    tp = lax.axis_index("tp")
    chip = tp // 2
    core = tp % 2
    up = (chip + 1) % NCHIP
    down = (chip + 3) % NCHIP
    far = (chip + 2) % NCHIP
    tp_up = up * 2 + core
    tp_down = down * 2 + core
    tp_far = far * 2 + core
    sibling = chip * 2 + (1 - core)

    loads = [
        pltpu.make_async_copy(gx_hbm, gx_raw, load_sem.at[0]),
        pltpu.make_async_copy(sw_hbm, sw_raw, load_sem.at[1]),
        pltpu.make_async_copy(wo_hbm, wo, load_sem.at[2]),
        pltpu.make_async_copy(hidden_hbm, hidden, load_sem.at[3]),
        pltpu.make_async_copy(gain_hbm, gain_ref, load_sem.at[4]),
        pltpu.make_async_copy(stepw_hbm, stepw_ref, load_sem.at[5]),
        pltpu.make_async_copy(tap_x_hbm, tap_x, load_sem.at[6]),
        pltpu.make_async_copy(tap_s_hbm, tap_s, load_sem.at[7]),
        pltpu.make_async_copy(bias_hbm, bias_ref, load_sem.at[8]),
        pltpu.make_async_copy(decay_hbm, decay_ref, load_sem.at[9]),
        pltpu.make_async_copy(skip_hbm, skip_ref, load_sem.at[10]),
        pltpu.make_async_copy(igain_hbm, igain_ref, load_sem.at[11]),
        pltpu.make_async_copy(init_hbm, init_ref, load_sem.at[12]),
    ]
    loads[3].start()
    loads[4].start()

    barrier = pltpu.get_barrier_semaphore()

    @pl.loop(0, NSEQ - 1)
    def _(k):
        pl.semaphore_signal(
            barrier, inc=1, device_id={"seq": (seq + 1 + (k + 5) % (NSEQ - 1)) % NSEQ}, device_id_type=MESH
        )

    @pl.loop(1, NTP)
    def _(k):
        pl.semaphore_signal(
            barrier, inc=1, device_id={"tp": (tp + k) % NTP}, device_id_type=MESH
        )

    for n in (0, 1, 5, 6, 7, 8, 9, 10, 11, 12):
        loads[n].start()
    loads[3].wait()
    loads[4].wait()

    gain_rows = gain_ref[...].astype(F32)
    gain_at = iota((MODEL // 128, 128), 0)
    gain = jnp.concatenate(
        [
            jnp.sum(jnp.where(gain_at == tp * 4 + j, gain_rows, 0.0), axis=0, keepdims=True)
            for j in range(4)
        ],
        axis=1,
    )
    own = pl.ds(pl.multiple_of(tp * FEAT, FEAT), FEAT)
    squares = []
    for c in range(NCHUNK):
        rows = slice(c * CHUNK, (c + 1) * CHUNK)
        h = hidden[rows, :].astype(F32)
        g[rows, own] = (h * gain).astype(BF16)
        summed = jnp.sum(h * h, axis=1, keepdims=True)
        squares.append(jnp.broadcast_to(summed, (CHUNK, 128)).T[0:1, :])
    ss_send[...] = jnp.concatenate(squares + [jnp.zeros((4, 128), F32)], axis=0)

    pl.semaphore_wait(barrier, NTP - 1 + NSEQ - 1)

    def ag_copy(step, kind):
        row = pl.multiple_of(((step + NCHUNK - 1) % NCHUNK) * CHUNK, CHUNK)
        whole, first, second = (row, CHUNK), (row, HALF), (pl.multiple_of(row + HALF, HALF), HALF)
        (start, size), shard, target = (
            (whole, tp, tp_up),
            (whole, tp, tp_down),
            (whole, tp, sibling),
            (first, tp_down, tp_up),
            (second, tp_up, tp_down),
            (whole, tp_down, sibling),
            (whole, tp_up, sibling),
            (first, tp_far, sibling),
            (second, tp_far, sibling),
        )[kind]
        block = g.at[pl.ds(start, size), pl.ds(pl.multiple_of(shard * FEAT, FEAT), FEAT)]
        return pltpu.make_async_remote_copy(
            src_ref=block,
            dst_ref=block,
            send_sem=ag_send.at[step, kind],
            recv_sem=ag_recv.at[step, kind],
            device_id={"tp": target},
            device_id_type=MESH,
        )

    def send_own(step):
        for kind in (0, 1, 2):
            ag_copy(step, kind).start()

    send_own(0)

    def ss_copy(k):
        return pltpu.make_async_remote_copy(
            src_ref=ss_send,
            dst_ref=ss_recv.at[tp],
            send_sem=ss_ssem.at[k],
            recv_sem=ss_rsem.at[k],
            device_id={"tp": (tp + k) % NTP},
            device_id_type=MESH,
        )

    @pl.loop(1, NTP)
    def _(k):
        ss_copy(k).start()

    ss_recv[tp] = ss_send[...]

    loads[0].wait()
    o256, i256 = iota((256, 256), 0), iota((256, 256), 1)
    pick = jnp.where(i256 == (o256 % 32) * 8 + o256 // 32, 1.0, 0.0).astype(BF16)

    def sort_gate_x(b):
        at = pl.multiple_of(b * 512, 512)
        k0 = pl.multiple_of(b * 64, 64)
        both = jnp.concatenate([gx_raw[pl.ds(at, 256), :], gx_raw[pl.ds(at + 256, 256), :]], axis=1)
        sorted_rows = dot(pick, both).astype(BF16)
        for m in range(8):
            column = (m % 2) * 512 + (m // 2) * 128
            rows = sorted_rows[m * 32 : (m + 1) * 32, :]
            w[pl.ds(k0, 32), column : column + 128] = rows[:, :128]
            w[pl.ds(k0 + 32, 32), column : column + 128] = rows[:, 128:]

    pl.loop(0, 32, unroll=16)(sort_gate_x)
    send_own(1)
    pl.loop(32, 64, unroll=16)(sort_gate_x)
    loads[1].wait()
    loads[2].start()
    pick_state = jnp.where(i256 == (o256 % 128) * 2 + o256 // 128, 1.0, 0.0).astype(BF16)

    @pl.loop(0, 16, unroll=8)
    def _(b):
        at = pl.multiple_of(b * 512, 512)
        k0 = pl.multiple_of(b * 256, 256)
        both = jnp.concatenate([sw_raw[pl.ds(at, 256), :], sw_raw[pl.ds(at + 256, 256), :]], axis=1)
        sorted_rows = dot(pick_state, both).astype(BF16)
        for m in range(2):
            column = 1024 + m * 128
            rows = sorted_rows[m * 128 : (m + 1) * 128, :]
            w[pl.ds(k0, 128), column : column + 128] = rows[:, :128]
            w[pl.ds(k0 + 128, 128), column : column + 128] = rows[:, 128:]

    for n in range(5, 13):
        loads[n].wait()

    @pl.loop(0, 32, unroll=8)
    def _(b):
        at = pl.multiple_of(b * 128, 128)
        rows = stepw_ref[:, pl.ds(at, 128)].astype(F32)
        square = jnp.concatenate([rows, jnp.zeros((120, 128), F32)], axis=0)
        w[pl.ds(at, 128), 1280:1408] = square.T.astype(BF16)

    for j in range(4):
        init_t[:, j * 128 : (j + 1) * 128] = init_ref[j * 128 : (j + 1) * 128, :].T

    lane512 = iota((1, 512), 1)
    row8 = iota((8, 128), 0)
    bias = jnp.zeros((8, 128), F32)
    rate = jnp.zeros((8, 128), F32)
    skip = jnp.zeros((1, 512), F32)
    for h in range(HEADS):
        bias = jnp.where(row8 == h, bias_ref[h], bias)
        rate = jnp.where(row8 == h, decay_ref[h], rate)
        skip = jnp.where(lane512 // WIDTH == h, skip_ref[h], skip)
    rate = jnp.exp(rate)
    r128, c128 = iota((128, 128), 0), iota((128, 128), 1)
    causal = r128 >= c128
    upper = jnp.where(r128 <= c128, 1.0, 0.0)
    s_row, s_lane = iota((128, 512), 0), iota((128, 512), 1)
    spread_decay = jnp.where(s_row == HEADS + s_lane // WIDTH, 1.0, 0.0).astype(BF16)
    spread_step = jnp.where(s_row == 2 * HEADS + s_lane // WIDTH, 1.0, 0.0).astype(BF16)

    state[...] = jnp.zeros((STATE, FEAT), F32)
    total_log[...] = jnp.zeros((8, 128), F32)

    halo_copy = pltpu.make_async_remote_copy(
        src_ref=halo_send,
        dst_ref=halo_recv,
        send_sem=halo_ssem,
        recv_sem=halo_rsem,
        device_id={"seq": (seq + 1) % NSEQ},
        device_id_type=MESH,
    )

    def chunk_of(step):
        return (step + NCHUNK - 1) % NCHUNK

    def project(c):
        row = pl.multiple_of(c * CHUNK, CHUNK)
        rows = pl.ds(row, CHUNK)
        r = rfull[rows, :]
        product = dot(g[rows, :], w[:, 512:COLS])
        for n in range(6):
            raw = (product[:, n * 128 : (n + 1) * 128] * r).astype(BF16).astype(F32)
            xf[pl.ds(pl.multiple_of(row + 16, 16), CHUNK), n * 128 : (n + 1) * 128] = raw
        raw_step = (product[:, 768:896] * r).astype(BF16).astype(F32)
        steps[:, rows] = raw_step.T[0:HEADS, :]

    def project_gate(c):
        rows = pl.ds(pl.multiple_of(c * CHUNK, CHUNK), CHUNK)
        r = rfull[rows, :]
        product = dot(g[rows, :], w[:, 0:512])
        for n in range(4):
            z = (product[:, n * 128 : (n + 1) * 128] * r).astype(BF16).astype(F32)
            sz[rows, n * 128 : (n + 1) * 128] = silu(z)

    def scan_chunk(c):
        row = pl.multiple_of(c * CHUNK, CHUNK)
        rows = pl.ds(row, CHUNK)

        def filtered(cols, taps):
            padded = xf[pl.ds(pl.multiple_of(row + 8, 8), CHUNK + 8), cols]
            summed = taps[0] * padded[5 : 5 + CHUNK]
            for k in range(1, 4):
                summed = summed + taps[k] * padded[5 + k : 5 + k + CHUNK]
            return silu(summed).astype(BF16)

        taps_x = tap_x[...].astype(F32)
        taps_s = tap_s[...].astype(F32)
        values = jnp.concatenate(
            [
                filtered(
                    slice(j * 128, (j + 1) * 128),
                    [taps_x[k : k + 1, j * 128 : (j + 1) * 128] for k in range(4)],
                )
                for j in range(4)
            ],
            axis=1,
        )
        in_map, out_map = (
            filtered(
                slice(512 + m * 128, 640 + m * 128),
                [taps_s[2 * k + m : 2 * k + m + 1, :] for k in range(4)],
            )
            for m in range(2)
        )
        cmap[rows, :] = out_map
        vals[rows, :] = values
        in_map_t = in_map.astype(F32).T.astype(BF16)
        step = softplus(steps[:, rows] + bias)
        cum = dot(-step * rate, upper, HIGHEST)
        last = jnp.broadcast_to(cum[:, 127:128], (8, 128))
        kept = step * jnp.exp(last - cum)
        columns = jnp.concatenate(
            [cum, jnp.exp(cum), kept, jnp.zeros((104, 128), F32)], axis=0
        ).T
        bmap_t[c] = in_map_t
        cols_t[c] = columns
        cum_rows[c] = cum
        step_rows[c] = step
        high = columns.astype(BF16)
        low = (columns - high.astype(F32)).astype(BF16)
        step_exp = dot(high, spread_step) + dot(low, spread_step)
        wide = values.astype(F32)
        weighted = (wide * step_exp).astype(BF16)
        before = state[...]
        sloc[c] = before
        pre[c] = jnp.broadcast_to(jnp.exp(across_heads(total_log[...])), (8, FEAT))
        total_log[...] += last
        state[...] = jnp.exp(across_heads(last)) * before + dot(in_map_t, weighted)

    def outputs_of(c):
        rows = pl.ds(pl.multiple_of(c * CHUNK, CHUNK), CHUNK)
        columns, cum, step = cols_t[c], cum_rows[c], step_rows[c]
        high = columns.astype(BF16)
        low = (columns - high.astype(F32)).astype(BF16)
        ec[rows, :] = dot(high, spread_decay) + dot(low, spread_decay)
        scores = dot(cmap[rows, :], bmap_t[c])
        lane = iota((CHUNK, 128), 1)
        for j in range(4):
            cols = slice(j * 128, (j + 1) * 128)
            pair = vals[rows, cols]
            both = []
            for h in (2 * j, 2 * j + 1):
                spread = columns[:, h : h + 1] - cum[h : h + 1, :]
                weights = jnp.exp(jnp.where(causal, spread, -1e30))
                both.append(dot((scores * weights * step[h : h + 1, :]).astype(BF16), pair))
            y[rows, cols] = (
                jnp.where(lane < WIDTH, both[0], both[1]) + skip[:, cols] * pair.astype(F32)
            )

    @pl.loop(0, NCHUNK + 2)
    def _(i):
        @pl.when(i == 2)
        def _():
            @pl.loop(1, NTP)
            def _(k):
                ss_copy(k).wait_recv()

            summed = ss_recv[0]
            for k in range(1, NTP):
                summed = summed + ss_recv[k]
            r = lax.rsqrt(summed * (1.0 / MODEL) + EPSILON)
            for c in range(NCHUNK):
                rfull[c * CHUNK : (c + 1) * CHUNK, :] = jnp.broadcast_to(
                    r[c : c + 1, :], (CHUNK, 128)
                ).T

        @pl.when(i >= 2)
        def _():
            for kind in (2, 5, 6, 7, 8):
                ag_copy(i - 2, kind).wait_recv()
            project(chunk_of(i - 2))

        @pl.when(i == 2)
        def _():
            halo_send[...] = xf[ROWS : ROWS + 16, :].astype(BF16)
            halo_copy.start()

        @pl.when(i < NCHUNK)
        def _():
            ag_copy(i, 0).wait_recv()
            ag_copy(i, 3).start()
            ag_copy(i, 5).start()
            ag_copy(i, 1).wait_recv()
            ag_copy(i, 4).start()
            ag_copy(i, 6).start()

        @pl.when(i < NCHUNK - 2)
        def _():
            send_own(i + 2)

        @pl.when((i >= 1) & (i <= NCHUNK))
        def _():
            ag_copy(i - 1, 3).wait_recv()
            ag_copy(i - 1, 7).start()
            ag_copy(i - 1, 4).wait_recv()
            ag_copy(i - 1, 8).start()

        @pl.when(i == 3)
        def _():
            halo_copy.wait_recv()
            xf[0:16, :] = jnp.where(seq > 0, halo_recv[...].astype(F32), 0.0)

        @pl.when(i >= 3)
        def _():
            scan_chunk(i - 3)

        @pl.when((i >= 2) & (i <= NCHUNK))
        def _():
            project_gate(chunk_of(i - 2))

    scan_chunk(NCHUNK - 1)

    logs = across_heads(total_log[...])
    high = logs.astype(BF16)
    rest = logs - high.astype(F32)
    middle = rest.astype(BF16)
    bits = [high.astype(F32), middle.astype(F32), rest - middle.astype(F32)]
    row16 = iota((16, 128), 0)
    for half in range(2):
        block = jnp.zeros((16, 128), F32)
        for part_at in range(2):
            at = half * 256 + part_at * 128
            for n in range(3):
                block = jnp.where(row16 == part_at * 8 + n, bits[n][:, at : at + 128], block)
        block = block.astype(BF16)
        for n in range(8):
            piece_send[2 * n + half, :, 0:256] = state[
                n * 16 : (n + 1) * 16, half * 256 : (half + 1) * 256
            ].astype(BF16)
            piece_send[2 * n + half, :, 256:384] = block

    def piece_copy(k):
        target = (seq + k) % NSEQ
        return pltpu.make_async_remote_copy(
            src_ref=piece_send.at[target],
            dst_ref=piece_recv.at[seq],
            send_sem=p_ssem.at[k],
            recv_sem=p_rsem.at[k],
            device_id={"seq": target},
            device_id_type=MESH,
        )

    def enter_copy(k):
        target = (seq + k) % NSEQ
        return pltpu.make_async_remote_copy(
            src_ref=enter_send.at[target],
            dst_ref=enter_recv.at[seq],
            send_sem=e_ssem.at[k],
            recv_sem=e_rsem.at[k],
            device_id={"seq": target},
            device_id_type=MESH,
        )

    @pl.loop(1, NSEQ)
    def _(k):
        piece_copy(k).start()

    piece_recv[seq] = piece_send[seq]
    project_gate(chunk_of(NCHUNK - 1))
    outputs_of(0)
    outputs_of(1)
    carried = init_t[
        pl.ds(pl.multiple_of((seq // 2) * 16, 16), 16),
        pl.ds(pl.multiple_of((seq % 2) * 256, 256), 256),
    ]

    @pl.loop(1, NSEQ)
    def _(k):
        piece_copy(k).wait_recv()

    for s in range(NSEQ):
        enter_send[s] = carried.astype(BF16)
        codes = piece_recv[s, :, 256:384].astype(F32)
        log = jnp.concatenate(
            [codes[0:1] + codes[1:2] + codes[2:3], codes[8:9] + codes[9:10] + codes[10:11]], axis=1
        )
        carried = jnp.exp(log) * carried + piece_recv[s, :, 0:256].astype(F32)

    @pl.loop(1, NSEQ)
    def _(k):
        enter_copy(k).start()

    enter_recv[seq] = enter_send[seq]
    outputs_of(2)
    outputs_of(3)
    loads[2].wait()

    @pl.loop(1, NSEQ)
    def _(k):
        enter_copy(k).wait_recv()

    for q in range(NSEQ):
        n, half = q // 2, q % 2
        entering[n * 16 : (n + 1) * 16, half * 256 : (half + 1) * 256] = enter_recv[q].astype(F32)

    igain_rows = igain_ref[...].astype(F32)
    igain = jnp.concatenate([igain_rows[j : j + 1, :] for j in range(4)], axis=1)

    def rs_copy(i, kind):
        src, dst, target = (
            (xs.at[i, 0], xr.at[i, 0], sibling),
            (xs.at[i, 1], xr.at[i, 1], sibling),
            (xs.at[i, 2], xr.at[i, 2], sibling),
            (xs.at[i, 3], xr.at[i, 3], sibling),
            (far_send.at[i, 0], far_recv.at[i, 0], tp_up),
            (far_send.at[i, 1], far_recv.at[i, 1], tp_down),
            (near_send.at[i, 0], near_recv.at[i, 0], tp_up),
            (near_send.at[i, 1], near_recv.at[i, 1], tp_down),
        )[kind]
        return pltpu.make_async_remote_copy(
            src_ref=src,
            dst_ref=dst,
            send_sem=rs_ssem.at[i, kind],
            recv_sem=rs_rsem.at[i, kind],
            device_id={"tp": target},
            device_id_type=MESH,
        )

    def out_block(rows, z, to_core):
        at = pl.multiple_of((z * 2 + to_core) * FEAT, FEAT)
        return dot(mx[rows, :], wo[:, pl.ds(at, FEAT)])

    def project_out(c, d, z):
        rows = pl.ds(pl.multiple_of(c * CHUNK, CHUNK), CHUNK)
        xs[c, d] = out_block(rows, z, 1 - core).astype(BF16)
        rs_copy(c, d).start()
        part[c, d] = out_block(rows, z, core)

    @pl.loop(0, NCHUNK + 1)
    def _(i):
        @pl.when(i < NCHUNK)
        def _():
            rows = pl.ds(pl.multiple_of(i * CHUNK, CHUNK), CHUNK)
            memory = (sloc[i] + pre[i][0:1, :] * entering[...]).astype(BF16)
            mixer = y[rows, :] + ec[rows, :] * dot(cmap[rows, :], memory)
            gated = mixer * sz[rows, :]
            scale = lax.rsqrt(jnp.mean(gated * gated, axis=1, keepdims=True) + EPSILON)
            mx[rows, :] = (gated * scale * igain).astype(BF16)
            project_out(i, 0, far)

        @pl.when(i >= 1)
        def _():
            c = i - 1
            rs_copy(c, 0).wait_recv()
            whole = (part[c, 0] + xr[c, 0].astype(F32)).astype(BF16)
            far_send[c, 0] = whole[:HALF]
            rs_copy(c, 4).start()
            far_send[c, 1] = whole[HALF:]
            rs_copy(c, 5).start()

    @pl.loop(0, NCHUNK + 1)
    def _(i):
        @pl.when(i < NCHUNK)
        def _():
            project_out(i, 1, up)
            project_out(i, 2, down)

        @pl.when(i >= 1)
        def _():
            c = i - 1
            rs_copy(c, 1).wait_recv()
            rs_copy(c, 4).wait_recv()
            whole = part[c, 1] + xr[c, 1].astype(F32)
            near_send[c, 0, 0:HALF] = (whole[:HALF] + far_recv[c, 0].astype(F32)).astype(BF16)
            near_send[c, 0, HALF:CHUNK] = whole[HALF:].astype(BF16)
            rs_copy(c, 6).start()
            rs_copy(c, 2).wait_recv()
            rs_copy(c, 5).wait_recv()
            whole = part[c, 2] + xr[c, 2].astype(F32)
            near_send[c, 1, 0:HALF] = whole[:HALF].astype(BF16)
            near_send[c, 1, HALF:CHUNK] = (whole[HALF:] + far_recv[c, 1].astype(F32)).astype(BF16)
            rs_copy(c, 7).start()

    @pl.loop(0, NCHUNK)
    def _(c):
        project_out(c, 3, chip)

    @pl.loop(0, NCHUNK)
    def _(i):
        for kind in range(RING_AG):
            ag_copy(i, kind).wait_send()
        for kind in (0, 1, 2, 4, 5):
            rs_copy(i, kind).wait_send()

    @pl.loop(1, NTP)
    def _(k):
        ss_copy(k).wait_send()

    halo_copy.wait_send()

    @pl.loop(1, NSEQ)
    def _(k):
        piece_copy(k).wait_send()
        enter_copy(k).wait_send()

    def out_copy(c):
        rows = pl.ds(pl.multiple_of(c * CHUNK, CHUNK), CHUNK)
        return pltpu.make_async_copy(out_ref.at[rows, :], out_hbm.at[rows, :], out_sem.at[c])

    @pl.loop(0, NCHUNK)
    def _(c):
        rows = pl.ds(pl.multiple_of(c * CHUNK, CHUNK), CHUNK)
        rs_copy(c, 3).wait_recv()
        summed = hidden[rows, :].astype(F32) + (part[c, 3] + xr[c, 3].astype(F32))
        rs_copy(c, 6).wait_recv()
        summed = summed + near_recv[c, 0].astype(F32)
        rs_copy(c, 7).wait_recv()
        out_ref[rows, :] = (summed + near_recv[c, 1].astype(F32)).astype(BF16)
        out_copy(c).start()

    @pl.loop(0, NCHUNK)
    def _(c):
        rs_copy(c, 3).wait_send()
        rs_copy(c, 6).wait_send()
        rs_copy(c, 7).wait_send()
        out_copy(c).wait()


def on_device(
    hidden,
    norm_gain,
    gate_x_weight,
    state_weight,
    step_weight,
    conv_inner,
    conv_state,
    step_bias,
    decay_log,
    skip_gain,
    inner_gain,
    out_weight,
    initial_state,
):
    gx = gate_x_weight.reshape(MODEL, 2, 4, 128).transpose(0, 2, 1, 3).reshape(MODEL * 8, 128)
    sw = state_weight.reshape(MODEL * 2, 128)
    anywhere = pl.BlockSpec(memory_space=pl.ANY)
    V = pltpu.VMEM
    dma = pltpu.SemaphoreType.DMA
    return pl.pallas_call(
        kernel,
        out_shape=jax.ShapeDtypeStruct((ROWS, FEAT), BF16),
        in_specs=[anywhere] * 13,
        out_specs=anywhere,
        scratch_shapes=[
            V((ROWS, FEAT), BF16),
            V((MODEL // 128, 128), BF16),
            V((HEADS, MODEL), BF16),
            V((4, FEAT), BF16),
            V((8, 128), BF16),
            pltpu.SMEM((HEADS,), F32),
            pltpu.SMEM((HEADS,), F32),
            pltpu.SMEM((HEADS,), F32),
            V((4, 128), BF16),
            V((HEADS * WIDTH, STATE), F32),
            V((ROWS, FEAT), BF16),
            V((MODEL * 8, 128), BF16),
            V((MODEL * 2, 128), BF16),
            V((MODEL, COLS), BF16),
            V((FEAT, MODEL), BF16),
            V((ROWS, MODEL), BF16),
            V((8, 128), F32),
            V((NTP, 8, 128), F32),
            V((ROWS, 128), F32),
            V((ROWS + 16, 768), F32),
            V((8, ROWS), F32),
            V((ROWS, FEAT), F32),
            V((ROWS, FEAT), F32),
            V((ROWS, FEAT), F32),
            V((NCHUNK, STATE, FEAT), F32),
            V((NCHUNK, 8, FEAT), F32),
            V((STATE, FEAT), F32),
            V((8, 128), F32),
            V((ROWS, STATE), BF16),
            V((ROWS, FEAT), BF16),
            V((NCHUNK, STATE, CHUNK), BF16),
            V((NCHUNK, CHUNK, 128), F32),
            V((NCHUNK, HEADS, CHUNK), F32),
            V((NCHUNK, HEADS, CHUNK), F32),
            V((ROWS, FEAT), BF16),
            V((16, 768), BF16),
            V((16, 768), BF16),
            V((NSEQ, 16, 384), BF16),
            V((NSEQ, 16, 384), BF16),
            V((NSEQ, 16, 256), BF16),
            V((NSEQ, 16, 256), BF16),
            V((STATE, FEAT), F32),
            V((STATE, FEAT), F32),
            V((NCHUNK, 4, CHUNK, FEAT), BF16),
            V((NCHUNK, 4, CHUNK, FEAT), BF16),
            V((NCHUNK, 4, CHUNK, FEAT), F32),
            V((NCHUNK, 2, HALF, FEAT), BF16),
            V((NCHUNK, 2, CHUNK, FEAT), BF16),
            V((NCHUNK, 2, HALF, FEAT), BF16),
            V((NCHUNK, 2, CHUNK, FEAT), BF16),
            dma((13,)),
            dma((NCHUNK,)),
            dma((NCHUNK, RING_AG)),
            dma((NCHUNK, RING_AG)),
            dma((NTP,)),
            dma((NTP,)),
            dma,
            dma,
            dma((NSEQ,)),
            dma((NSEQ,)),
            dma((NSEQ,)),
            dma((NSEQ,)),
            dma((NCHUNK, RING_RS)),
            dma((NCHUNK, RING_RS)),
        ],
        compiler_params=pltpu.CompilerParams(
            collective_id=0, has_side_effects=True, vmem_limit_bytes=61 << 20
        ),
    )(
        hidden,
        norm_gain.reshape(MODEL // 128, 128),
        gx,
        sw,
        step_weight.T,
        conv_inner,
        conv_state.reshape(8, 128),
        step_bias,
        decay_log,
        skip_gain,
        inner_gain.reshape(4, 128),
        out_weight,
        initial_state.reshape(HEADS * WIDTH, STATE),
    )


def solution(mesh):
    return jax.shard_map(
        on_device,
        mesh=mesh,
        in_specs=(
            P("seq", "tp"),
            P(),
            P(None, None, "tp"),
            P(None, None, "tp"),
            P(None, "tp"),
            P(None, "tp"),
            P(None, None, "tp"),
            P("tp"),
            P("tp"),
            P("tp"),
            P("tp"),
            P("tp", None),
            P("tp", None, None),
        ),
        out_specs=P("seq", "tp"),
        check_vma=False,
    )
```

```python
import functools

import jax
import jax.numpy as jnp
from jax import lax
from jax.experimental import pallas as pl
from jax.experimental.pallas import tpu as pltpu
from jax.sharding import PartitionSpec as P

F32 = jnp.float32
BF16 = jnp.bfloat16
EPSILON = 1e-05
MESH = pl.DeviceIdType.MESH
HIGHEST = lax.Precision.HIGHEST

ROWS = 512
FEAT = 512
MODEL = 4096
HEADS = 8
WIDTH = 64
STATE = 128
CHUNK = 128
NCHUNK = ROWS // CHUNK
HALF = CHUNK // 2
NSEQ = 16
NTP = 8
NCHIP = 4
COLS = 1408
RING_AG = 9
RING_RS = 8


def silu(v):
    return v / (1.0 + jnp.exp(-v))


def softplus(v):
    return jnp.maximum(v, 0.0) + jnp.log1p(jnp.exp(-jnp.abs(v)))


def dot(a, b, precision=None):
    return jnp.dot(a, b, preferred_element_type=F32, precision=precision)


def iota(shape, dim):
    return lax.broadcasted_iota(jnp.int32, shape, dim)


def across_heads(rows):
    lane = iota((1, 128), 1)
    parts = [
        jnp.where(lane < WIDTH, rows[2 * j : 2 * j + 1, :], rows[2 * j + 1 : 2 * j + 2, :])
        for j in range(4)
    ]
    return jnp.concatenate(parts, axis=1)


def kernel(
    hidden_hbm,
    gain_hbm,
    gx_hbm,
    sw_hbm,
    stepw_hbm,
    tap_x_hbm,
    tap_s_hbm,
    bias_hbm,
    decay_hbm,
    skip_hbm,
    igain_hbm,
    wo_hbm,
    init_hbm,
    out_hbm,
    hidden,
    gain_ref,
    stepw_ref,
    tap_x,
    tap_s,
    bias_ref,
    decay_ref,
    skip_ref,
    igain_ref,
    init_ref,
    out_ref,
    gx_raw,
    sw_raw,
    w,
    wo,
    g,
    ss_send,
    ss_recv,
    rfull,
    xf,
    steps,
    sz,
    y,
    ec,
    sloc,
    pre,
    state,
    total_log,
    cmap,
    vals,
    bmap_t,
    cols_t,
    cum_rows,
    step_rows,
    mx,
    early,
    halo_send,
    halo_recv,
    piece_send,
    piece_recv,
    enter_send,
    enter_recv,
    init_t,
    entering,
    xs,
    xr,
    part,
    far_send,
    near_send,
    far_recv,
    near_recv,
    load_sem,
    out_sem,
    ag_send,
    ag_recv,
    ss_ssem,
    ss_rsem,
    halo_ssem,
    halo_rsem,
    p_ssem,
    p_rsem,
    e_ssem,
    e_rsem,
    rs_ssem,
    rs_rsem,
):
    seq = lax.axis_index("seq")
    tp = lax.axis_index("tp")
    chip = tp // 2
    core = tp % 2
    up = (chip + 1) % NCHIP
    down = (chip + 3) % NCHIP
    far = (chip + 2) % NCHIP
    tp_up = up * 2 + core
    tp_down = down * 2 + core
    tp_far = far * 2 + core
    sibling = chip * 2 + (1 - core)

    loads = [
        pltpu.make_async_copy(gx_hbm, gx_raw, load_sem.at[0]),
        pltpu.make_async_copy(sw_hbm, sw_raw, load_sem.at[1]),
        pltpu.make_async_copy(wo_hbm, wo, load_sem.at[2]),
        pltpu.make_async_copy(hidden_hbm, hidden, load_sem.at[3]),
        pltpu.make_async_copy(gain_hbm, gain_ref, load_sem.at[4]),
        pltpu.make_async_copy(stepw_hbm, stepw_ref, load_sem.at[5]),
        pltpu.make_async_copy(tap_x_hbm, tap_x, load_sem.at[6]),
        pltpu.make_async_copy(tap_s_hbm, tap_s, load_sem.at[7]),
        pltpu.make_async_copy(bias_hbm, bias_ref, load_sem.at[8]),
        pltpu.make_async_copy(decay_hbm, decay_ref, load_sem.at[9]),
        pltpu.make_async_copy(skip_hbm, skip_ref, load_sem.at[10]),
        pltpu.make_async_copy(igain_hbm, igain_ref, load_sem.at[11]),
        pltpu.make_async_copy(init_hbm, init_ref, load_sem.at[12]),
    ]
    loads[3].start()
    loads[4].start()

    barrier = pltpu.get_barrier_semaphore()

    @pl.loop(0, NSEQ - 1)
    def _(k):
        pl.semaphore_signal(
            barrier, inc=1, device_id={"seq": (seq + 1 + (k + 5) % (NSEQ - 1)) % NSEQ}, device_id_type=MESH
        )

    @pl.loop(1, NTP)
    def _(k):
        pl.semaphore_signal(
            barrier, inc=1, device_id={"tp": (tp + k) % NTP}, device_id_type=MESH
        )

    for n in (0, 1, 5, 6, 7, 8, 9, 10, 11, 12):
        loads[n].start()
    loads[3].wait()
    loads[4].wait()

    gain_rows = gain_ref[...].astype(F32)
    gain_at = iota((MODEL // 128, 128), 0)
    gain = jnp.concatenate(
        [
            jnp.sum(jnp.where(gain_at == tp * 4 + j, gain_rows, 0.0), axis=0, keepdims=True)
            for j in range(4)
        ],
        axis=1,
    )
    own = pl.ds(pl.multiple_of(tp * FEAT, FEAT), FEAT)
    squares = []
    for c in range(NCHUNK):
        rows = slice(c * CHUNK, (c + 1) * CHUNK)
        h = hidden[rows, :].astype(F32)
        g[rows, own] = (h * gain).astype(BF16)
        summed = jnp.sum(h * h, axis=1, keepdims=True)
        squares.append(jnp.broadcast_to(summed, (CHUNK, 128)).T[0:1, :])
    ss_send[...] = jnp.concatenate(squares + [jnp.zeros((4, 128), F32)], axis=0)

    pl.semaphore_wait(barrier, NTP - 1 + NSEQ - 1)

    def ag_copy(step, kind):
        row = pl.multiple_of(((step + NCHUNK - 1) % NCHUNK) * CHUNK, CHUNK)
        whole, first, second = (row, CHUNK), (row, HALF), (pl.multiple_of(row + HALF, HALF), HALF)
        (start, size), shard, target = (
            (whole, tp, tp_up),
            (whole, tp, tp_down),
            (whole, tp, sibling),
            (first, tp_down, tp_up),
            (second, tp_up, tp_down),
            (whole, tp_down, sibling),
            (whole, tp_up, sibling),
            (first, tp_far, sibling),
            (second, tp_far, sibling),
        )[kind]
        block = g.at[pl.ds(start, size), pl.ds(pl.multiple_of(shard * FEAT, FEAT), FEAT)]
        return pltpu.make_async_remote_copy(
            src_ref=block,
            dst_ref=block,
            send_sem=ag_send.at[step, kind],
            recv_sem=ag_recv.at[step, kind],
            device_id={"tp": target},
            device_id_type=MESH,
        )

    def send_own(step):
        for kind in (0, 1, 2):
            ag_copy(step, kind).start()

    send_own(0)

    def ss_copy(k):
        return pltpu.make_async_remote_copy(
            src_ref=ss_send,
            dst_ref=ss_recv.at[tp],
            send_sem=ss_ssem.at[k],
            recv_sem=ss_rsem.at[k],
            device_id={"tp": (tp + k) % NTP},
            device_id_type=MESH,
        )

    @pl.loop(1, NTP)
    def _(k):
        ss_copy(k).start()

    ss_recv[tp] = ss_send[...]

    loads[0].wait()
    o256, i256 = iota((256, 256), 0), iota((256, 256), 1)
    pick = jnp.where(i256 == (o256 % 32) * 8 + o256 // 32, 1.0, 0.0).astype(BF16)

    def sort_gate_x(b):
        at = pl.multiple_of(b * 512, 512)
        k0 = pl.multiple_of(b * 64, 64)
        both = jnp.concatenate([gx_raw[pl.ds(at, 256), :], gx_raw[pl.ds(at + 256, 256), :]], axis=1)
        sorted_rows = dot(pick, both).astype(BF16)
        for m in range(8):
            column = (m % 2) * 512 + (m // 2) * 128
            rows = sorted_rows[m * 32 : (m + 1) * 32, :]
            w[pl.ds(k0, 32), column : column + 128] = rows[:, :128]
            w[pl.ds(k0 + 32, 32), column : column + 128] = rows[:, 128:]

    pl.loop(0, 32, unroll=16)(sort_gate_x)
    send_own(1)
    pl.loop(32, 64, unroll=16)(sort_gate_x)
    loads[1].wait()
    loads[2].start()
    pick_state = jnp.where(i256 == (o256 % 128) * 2 + o256 // 128, 1.0, 0.0).astype(BF16)

    @pl.loop(0, 16, unroll=8)
    def _(b):
        at = pl.multiple_of(b * 512, 512)
        k0 = pl.multiple_of(b * 256, 256)
        both = jnp.concatenate([sw_raw[pl.ds(at, 256), :], sw_raw[pl.ds(at + 256, 256), :]], axis=1)
        sorted_rows = dot(pick_state, both).astype(BF16)
        for m in range(2):
            column = 1024 + m * 128
            rows = sorted_rows[m * 128 : (m + 1) * 128, :]
            w[pl.ds(k0, 128), column : column + 128] = rows[:, :128]
            w[pl.ds(k0 + 128, 128), column : column + 128] = rows[:, 128:]

    for n in range(5, 13):
        loads[n].wait()

    @pl.loop(0, 32, unroll=8)
    def _(b):
        at = pl.multiple_of(b * 128, 128)
        rows = stepw_ref[:, pl.ds(at, 128)].astype(F32)
        square = jnp.concatenate([rows, jnp.zeros((120, 128), F32)], axis=0)
        w[pl.ds(at, 128), 1280:1408] = square.T.astype(BF16)

    for j in range(4):
        init_t[:, j * 128 : (j + 1) * 128] = init_ref[j * 128 : (j + 1) * 128, :].T

    lane512 = iota((1, 512), 1)
    row8 = iota((8, 128), 0)
    bias = jnp.zeros((8, 128), F32)
    rate = jnp.zeros((8, 128), F32)
    skip = jnp.zeros((1, 512), F32)
    for h in range(HEADS):
        bias = jnp.where(row8 == h, bias_ref[h], bias)
        rate = jnp.where(row8 == h, decay_ref[h], rate)
        skip = jnp.where(lane512 // WIDTH == h, skip_ref[h], skip)
    rate = jnp.exp(rate)
    r128, c128 = iota((128, 128), 0), iota((128, 128), 1)
    causal = r128 >= c128
    upper = jnp.where(r128 <= c128, 1.0, 0.0)
    s_row, s_lane = iota((128, 512), 0), iota((128, 512), 1)
    spread_decay = jnp.where(s_row == HEADS + s_lane // WIDTH, 1.0, 0.0).astype(BF16)
    spread_step = jnp.where(s_row == 2 * HEADS + s_lane // WIDTH, 1.0, 0.0).astype(BF16)

    state[...] = jnp.zeros((STATE, FEAT), F32)
    total_log[...] = jnp.zeros((8, 128), F32)

    halo_copy = pltpu.make_async_remote_copy(
        src_ref=halo_send,
        dst_ref=halo_recv,
        send_sem=halo_ssem,
        recv_sem=halo_rsem,
        device_id={"seq": (seq + 1) % NSEQ},
        device_id_type=MESH,
    )

    def chunk_of(step):
        return (step + NCHUNK - 1) % NCHUNK

    def product_with(rows, z):
        features = pl.ds(pl.multiple_of(z * 2 * FEAT, 2 * FEAT), 2 * FEAT)
        return dot(g[rows, features], w[features, 512:COLS])

    def project_near(c):
        rows = pl.ds(pl.multiple_of(c * CHUNK, CHUNK), CHUNK)
        early[...] = product_with(rows, chip) + product_with(rows, up) + product_with(rows, down)

    def project(c):
        row = pl.multiple_of(c * CHUNK, CHUNK)
        rows = pl.ds(row, CHUNK)
        r = rfull[rows, :]
        product = early[...] + product_with(rows, far)
        for n in range(6):
            raw = (product[:, n * 128 : (n + 1) * 128] * r).astype(BF16).astype(F32)
            xf[pl.ds(pl.multiple_of(row + 16, 16), CHUNK), n * 128 : (n + 1) * 128] = raw
        raw_step = (product[:, 768:896] * r).astype(BF16).astype(F32)
        steps[:, rows] = raw_step.T[0:HEADS, :]

    def project_gate(c):
        rows = pl.ds(pl.multiple_of(c * CHUNK, CHUNK), CHUNK)
        r = rfull[rows, :]
        product = dot(g[rows, :], w[:, 0:512])
        for n in range(4):
            z = (product[:, n * 128 : (n + 1) * 128] * r).astype(BF16).astype(F32)
            sz[rows, n * 128 : (n + 1) * 128] = silu(z)

    def scan_chunk(c):
        row = pl.multiple_of(c * CHUNK, CHUNK)
        rows = pl.ds(row, CHUNK)

        def filtered(cols, taps):
            padded = xf[pl.ds(pl.multiple_of(row + 8, 8), CHUNK + 8), cols]
            summed = taps[0] * padded[5 : 5 + CHUNK]
            for k in range(1, 4):
                summed = summed + taps[k] * padded[5 + k : 5 + k + CHUNK]
            return silu(summed).astype(BF16)

        taps_x = tap_x[...].astype(F32)
        taps_s = tap_s[...].astype(F32)
        values = jnp.concatenate(
            [
                filtered(
                    slice(j * 128, (j + 1) * 128),
                    [taps_x[k : k + 1, j * 128 : (j + 1) * 128] for k in range(4)],
                )
                for j in range(4)
            ],
            axis=1,
        )
        in_map, out_map = (
            filtered(
                slice(512 + m * 128, 640 + m * 128),
                [taps_s[2 * k + m : 2 * k + m + 1, :] for k in range(4)],
            )
            for m in range(2)
        )
        cmap[rows, :] = out_map
        vals[rows, :] = values
        in_map_t = in_map.astype(F32).T.astype(BF16)
        bmap_t[c] = in_map_t
        last = jnp.broadcast_to(cum_rows[c][:, 127:128], (8, 128))
        wide = values.astype(F32)
        weighted = (wide * y[rows, :]).astype(BF16)
        before = state[...]
        sloc[c] = before
        pre[c] = jnp.broadcast_to(jnp.exp(across_heads(total_log[...])), (8, FEAT))
        total_log[...] += last
        state[...] = jnp.exp(across_heads(last)) * before + dot(in_map_t, weighted)

    def scan_steps(c):
        rows = pl.ds(pl.multiple_of(c * CHUNK, CHUNK), CHUNK)
        step = softplus(steps[:, rows] + bias)
        cum = dot(-step * rate, upper, HIGHEST)
        last = jnp.broadcast_to(cum[:, 127:128], (8, 128))
        kept = step * jnp.exp(last - cum)
        columns = jnp.concatenate(
            [cum, jnp.exp(cum), kept, jnp.zeros((104, 128), F32)], axis=0
        ).T
        cols_t[c] = columns
        cum_rows[c] = cum
        step_rows[c] = step
        high = columns.astype(BF16)
        low = (columns - high.astype(F32)).astype(BF16)
        step_exp = dot(high, spread_step) + dot(low, spread_step)
        y[rows, :] = step_exp

    def outputs_of(c):
        rows = pl.ds(pl.multiple_of(c * CHUNK, CHUNK), CHUNK)
        columns, cum, step = cols_t[c], cum_rows[c], step_rows[c]
        high = columns.astype(BF16)
        low = (columns - high.astype(F32)).astype(BF16)
        ec[rows, :] = dot(high, spread_decay) + dot(low, spread_decay)
        scores = dot(cmap[rows, :], bmap_t[c])
        lane = iota((CHUNK, 128), 1)
        for j in range(4):
            cols = slice(j * 128, (j + 1) * 128)
            pair = vals[rows, cols]
            both = []
            for h in (2 * j, 2 * j + 1):
                spread = columns[:, h : h + 1] - cum[h : h + 1, :]
                weights = jnp.exp(jnp.where(causal, spread, -1e30))
                both.append(dot((scores * weights * step[h : h + 1, :]).astype(BF16), pair))
            y[rows, cols] = (
                jnp.where(lane < WIDTH, both[0], both[1]) + skip[:, cols] * pair.astype(F32)
            )

    @pl.loop(0, NCHUNK + 2)
    def _(i):
        @pl.when(i == 2)
        def _():
            @pl.loop(1, NTP)
            def _(k):
                ss_copy(k).wait_recv()

            summed = ss_recv[0]
            for k in range(1, NTP):
                summed = summed + ss_recv[k]
            r = lax.rsqrt(summed * (1.0 / MODEL) + EPSILON)
            for c in range(NCHUNK):
                rfull[c * CHUNK : (c + 1) * CHUNK, :] = jnp.broadcast_to(
                    r[c : c + 1, :], (CHUNK, 128)
                ).T

        @pl.when(i >= 2)
        def _():
            for kind in (7, 8):
                ag_copy(i - 2, kind).wait_recv()
            project(chunk_of(i - 2))
            scan_steps(chunk_of(i - 2))

        @pl.when(i == 2)
        def _():
            halo_send[...] = xf[ROWS : ROWS + 16, :].astype(BF16)
            halo_copy.start()

        @pl.when(i < NCHUNK)
        def _():
            ag_copy(i, 0).wait_recv()
            ag_copy(i, 3).start()
            ag_copy(i, 5).start()
            ag_copy(i, 1).wait_recv()
            ag_copy(i, 4).start()
            ag_copy(i, 6).start()

        @pl.when(i < NCHUNK - 2)
        def _():
            send_own(i + 2)

        @pl.when((i >= 1) & (i <= NCHUNK))
        def _():
            for kind in (2, 5, 6):
                ag_copy(i - 1, kind).wait_recv()
            project_near(chunk_of(i - 1))
            ag_copy(i - 1, 3).wait_recv()
            ag_copy(i - 1, 7).start()
            ag_copy(i - 1, 4).wait_recv()
            ag_copy(i - 1, 8).start()

        @pl.when(i == 3)
        def _():
            halo_copy.wait_recv()
            xf[0:16, :] = jnp.where(seq > 0, halo_recv[...].astype(F32), 0.0)

        @pl.when(i >= 3)
        def _():
            scan_chunk(i - 3)

    scan_chunk(NCHUNK - 1)

    logs = across_heads(total_log[...])
    high = logs.astype(BF16)
    rest = logs - high.astype(F32)
    middle = rest.astype(BF16)
    bits = [high.astype(F32), middle.astype(F32), rest - middle.astype(F32)]
    row16 = iota((16, 128), 0)
    for half in range(2):
        block = jnp.zeros((16, 128), F32)
        for part_at in range(2):
            at = half * 256 + part_at * 128
            for n in range(3):
                block = jnp.where(row16 == part_at * 8 + n, bits[n][:, at : at + 128], block)
        block = block.astype(BF16)
        for n in range(8):
            piece_send[2 * n + half, :, 0:256] = state[
                n * 16 : (n + 1) * 16, half * 256 : (half + 1) * 256
            ].astype(BF16)
            piece_send[2 * n + half, :, 256:384] = block

    def piece_copy(k):
        target = (seq + k) % NSEQ
        return pltpu.make_async_remote_copy(
            src_ref=piece_send.at[target],
            dst_ref=piece_recv.at[seq],
            send_sem=p_ssem.at[k],
            recv_sem=p_rsem.at[k],
            device_id={"seq": target},
            device_id_type=MESH,
        )

    def enter_copy(k):
        target = (seq + k) % NSEQ
        return pltpu.make_async_remote_copy(
            src_ref=enter_send.at[target],
            dst_ref=enter_recv.at[seq],
            send_sem=e_ssem.at[k],
            recv_sem=e_rsem.at[k],
            device_id={"seq": target},
            device_id_type=MESH,
        )

    @pl.loop(1, NSEQ)
    def _(k):
        piece_copy(k).start()

    piece_recv[seq] = piece_send[seq]

    @pl.loop(0, 2)
    def _(c):
        project_gate(c)
        outputs_of(c)

    carried = init_t[
        pl.ds(pl.multiple_of((seq // 2) * 16, 16), 16),
        pl.ds(pl.multiple_of((seq % 2) * 256, 256), 256),
    ]

    @pl.loop(1, NSEQ)
    def _(k):
        piece_copy(k).wait_recv()

    for s in range(NSEQ):
        enter_send[s] = carried.astype(BF16)
        codes = piece_recv[s, :, 256:384].astype(F32)
        log = jnp.concatenate(
            [codes[0:1] + codes[1:2] + codes[2:3], codes[8:9] + codes[9:10] + codes[10:11]], axis=1
        )
        carried = jnp.exp(log) * carried + piece_recv[s, :, 0:256].astype(F32)

    @pl.loop(1, NSEQ)
    def _(k):
        enter_copy(k).start()

    enter_recv[seq] = enter_send[seq]

    @pl.loop(2, 4)
    def _(c):
        project_gate(c)
        outputs_of(c)

    loads[2].wait()

    @pl.loop(1, NSEQ)
    def _(k):
        enter_copy(k).wait_recv()

    for q in range(NSEQ):
        n, half = q // 2, q % 2
        entering[n * 16 : (n + 1) * 16, half * 256 : (half + 1) * 256] = enter_recv[q].astype(F32)

    igain_rows = igain_ref[...].astype(F32)
    igain = jnp.concatenate([igain_rows[j : j + 1, :] for j in range(4)], axis=1)

    def rs_copy(i, kind):
        src, dst, target = (
            (xs.at[i, 0], xr.at[i, 0], sibling),
            (xs.at[i, 1], xr.at[i, 1], sibling),
            (xs.at[i, 2], xr.at[i, 2], sibling),
            (xs.at[i, 3], xr.at[i, 3], sibling),
            (far_send.at[i, 0], far_recv.at[i, 0], tp_up),
            (far_send.at[i, 1], far_recv.at[i, 1], tp_down),
            (near_send.at[i, 0], near_recv.at[i, 0], tp_up),
            (near_send.at[i, 1], near_recv.at[i, 1], tp_down),
        )[kind]
        return pltpu.make_async_remote_copy(
            src_ref=src,
            dst_ref=dst,
            send_sem=rs_ssem.at[i, kind],
            recv_sem=rs_rsem.at[i, kind],
            device_id={"tp": target},
            device_id_type=MESH,
        )

    def out_block(rows, z, to_core):
        at = pl.multiple_of((z * 2 + to_core) * FEAT, FEAT)
        return dot(mx[rows, :], wo[:, pl.ds(at, FEAT)])

    def project_out(c, d, z):
        rows = pl.ds(pl.multiple_of(c * CHUNK, CHUNK), CHUNK)
        xs[c, d] = out_block(rows, z, 1 - core).astype(BF16)
        rs_copy(c, d).start()
        part[c, d] = out_block(rows, z, core)

    @pl.loop(0, NCHUNK + 1)
    def _(i):
        @pl.when(i < NCHUNK)
        def _():
            rows = pl.ds(pl.multiple_of(i * CHUNK, CHUNK), CHUNK)
            memory = (sloc[i] + pre[i][0:1, :] * entering[...]).astype(BF16)
            mixer = y[rows, :] + ec[rows, :] * dot(cmap[rows, :], memory)
            gated = mixer * sz[rows, :]
            scale = lax.rsqrt(jnp.mean(gated * gated, axis=1, keepdims=True) + EPSILON)
            mx[rows, :] = (gated * scale * igain).astype(BF16)
            project_out(i, 0, far)

        @pl.when(i >= 1)
        def _():
            c = i - 1
            rs_copy(c, 0).wait_recv()
            whole = (part[c, 0] + xr[c, 0].astype(F32)).astype(BF16)
            far_send[c, 0] = whole[:HALF]
            rs_copy(c, 4).start()
            far_send[c, 1] = whole[HALF:]
            rs_copy(c, 5).start()

    @pl.loop(0, NCHUNK)
    def _(c):
        project_out(c, 1, up)
        project_out(c, 2, down)
        rs_copy(c, 1).wait_recv()
        rs_copy(c, 4).wait_recv()
        whole = part[c, 1] + xr[c, 1].astype(F32)
        near_send[c, 0, 0:HALF] = (whole[:HALF] + far_recv[c, 0].astype(F32)).astype(BF16)
        near_send[c, 0, HALF:CHUNK] = whole[HALF:].astype(BF16)
        rs_copy(c, 6).start()
        rs_copy(c, 2).wait_recv()
        rs_copy(c, 5).wait_recv()
        whole = part[c, 2] + xr[c, 2].astype(F32)
        near_send[c, 1, 0:HALF] = whole[:HALF].astype(BF16)
        near_send[c, 1, HALF:CHUNK] = (whole[HALF:] + far_recv[c, 1].astype(F32)).astype(BF16)
        rs_copy(c, 7).start()

    @pl.loop(0, NCHUNK)
    def _(c):
        project_out(c, 3, chip)

    @pl.loop(0, NCHUNK)
    def _(i):
        for kind in range(RING_AG):
            ag_copy(i, kind).wait_send()
        for kind in (0, 1, 2, 4, 5):
            rs_copy(i, kind).wait_send()

    @pl.loop(1, NTP)
    def _(k):
        ss_copy(k).wait_send()

    halo_copy.wait_send()

    @pl.loop(1, NSEQ)
    def _(k):
        piece_copy(k).wait_send()
        enter_copy(k).wait_send()

    @pl.loop(0, NCHUNK)
    def _(c):
        rows = pl.ds(pl.multiple_of(c * CHUNK, CHUNK), CHUNK)
        rs_copy(c, 3).wait_recv()
        part[c, 3] = hidden[rows, :].astype(F32) + (part[c, 3] + xr[c, 3].astype(F32))

    def out_copy(c):
        rows = pl.ds(pl.multiple_of(c * CHUNK, CHUNK), CHUNK)
        return pltpu.make_async_copy(out_ref.at[rows, :], out_hbm.at[rows, :], out_sem.at[c])

    @pl.loop(0, NCHUNK)
    def _(c):
        rows = pl.ds(pl.multiple_of(c * CHUNK, CHUNK), CHUNK)
        rs_copy(c, 6).wait_recv()
        summed = part[c, 3] + near_recv[c, 0].astype(F32)
        rs_copy(c, 7).wait_recv()
        out_ref[rows, :] = (summed + near_recv[c, 1].astype(F32)).astype(BF16)
        out_copy(c).start()

    @pl.loop(0, NCHUNK)
    def _(c):
        rs_copy(c, 3).wait_send()
        rs_copy(c, 6).wait_send()
        rs_copy(c, 7).wait_send()
        out_copy(c).wait()


def on_device(
    hidden,
    norm_gain,
    gate_x_weight,
    state_weight,
    step_weight,
    conv_inner,
    conv_state,
    step_bias,
    decay_log,
    skip_gain,
    inner_gain,
    out_weight,
    initial_state,
):
    gx = gate_x_weight.reshape(MODEL, 2, 4, 128).transpose(0, 2, 1, 3).reshape(MODEL * 8, 128)
    sw = state_weight.reshape(MODEL * 2, 128)
    anywhere = pl.BlockSpec(memory_space=pl.ANY)
    V = pltpu.VMEM
    dma = pltpu.SemaphoreType.DMA
    return pl.pallas_call(
        kernel,
        out_shape=jax.ShapeDtypeStruct((ROWS, FEAT), BF16),
        in_specs=[anywhere] * 13,
        out_specs=anywhere,
        scratch_shapes=[
            V((ROWS, FEAT), BF16),
            V((MODEL // 128, 128), BF16),
            V((HEADS, MODEL), BF16),
            V((4, FEAT), BF16),
            V((8, 128), BF16),
            pltpu.SMEM((HEADS,), F32),
            pltpu.SMEM((HEADS,), F32),
            pltpu.SMEM((HEADS,), F32),
            V((4, 128), BF16),
            V((HEADS * WIDTH, STATE), F32),
            V((ROWS, FEAT), BF16),
            V((MODEL * 8, 128), BF16),
            V((MODEL * 2, 128), BF16),
            V((MODEL, COLS), BF16),
            V((FEAT, MODEL), BF16),
            V((ROWS, MODEL), BF16),
            V((8, 128), F32),
            V((NTP, 8, 128), F32),
            V((ROWS, 128), F32),
            V((ROWS + 16, 768), F32),
            V((8, ROWS), F32),
            V((ROWS, FEAT), F32),
            V((ROWS, FEAT), F32),
            V((ROWS, FEAT), F32),
            V((NCHUNK, STATE, FEAT), F32),
            V((NCHUNK, 8, FEAT), F32),
            V((STATE, FEAT), F32),
            V((8, 128), F32),
            V((ROWS, STATE), BF16),
            V((ROWS, FEAT), BF16),
            V((NCHUNK, STATE, CHUNK), BF16),
            V((NCHUNK, CHUNK, 128), F32),
            V((NCHUNK, HEADS, CHUNK), F32),
            V((NCHUNK, HEADS, CHUNK), F32),
            V((ROWS, FEAT), BF16),
            V((CHUNK, COLS - 512), F32),
            V((16, 768), BF16),
            V((16, 768), BF16),
            V((NSEQ, 16, 384), BF16),
            V((NSEQ, 16, 384), BF16),
            V((NSEQ, 16, 256), BF16),
            V((NSEQ, 16, 256), BF16),
            V((STATE, FEAT), F32),
            V((STATE, FEAT), F32),
            V((NCHUNK, 4, CHUNK, FEAT), BF16),
            V((NCHUNK, 4, CHUNK, FEAT), BF16),
            V((NCHUNK, 4, CHUNK, FEAT), F32),
            V((NCHUNK, 2, HALF, FEAT), BF16),
            V((NCHUNK, 2, CHUNK, FEAT), BF16),
            V((NCHUNK, 2, HALF, FEAT), BF16),
            V((NCHUNK, 2, CHUNK, FEAT), BF16),
            dma((13,)),
            dma((NCHUNK,)),
            dma((NCHUNK, RING_AG)),
            dma((NCHUNK, RING_AG)),
            dma((NTP,)),
            dma((NTP,)),
            dma,
            dma,
            dma((NSEQ,)),
            dma((NSEQ,)),
            dma((NSEQ,)),
            dma((NSEQ,)),
            dma((NCHUNK, RING_RS)),
            dma((NCHUNK, RING_RS)),
        ],
        compiler_params=pltpu.CompilerParams(
            collective_id=0, has_side_effects=True, vmem_limit_bytes=61 << 20
        ),
    )(
        hidden,
        norm_gain.reshape(MODEL // 128, 128),
        gx,
        sw,
        step_weight.T,
        conv_inner,
        conv_state.reshape(8, 128),
        step_bias,
        decay_log,
        skip_gain,
        inner_gain.reshape(4, 128),
        out_weight,
        initial_state.reshape(HEADS * WIDTH, STATE),
    )


def solution(mesh):
    return jax.shard_map(
        on_device,
        mesh=mesh,
        in_specs=(
            P("seq", "tp"),
            P(),
            P(None, None, "tp"),
            P(None, None, "tp"),
            P(None, "tp"),
            P(None, "tp"),
            P(None, None, "tp"),
            P("tp"),
            P("tp"),
            P("tp"),
            P("tp"),
            P("tp", None),
            P("tp", None, None),
        ),
        out_specs=P("seq", "tp"),
        check_vma=False,
    )
```

```python
import functools

import jax
import jax.numpy as jnp
from jax import lax
from jax.experimental import pallas as pl
from jax.experimental.pallas import tpu as pltpu
from jax.sharding import PartitionSpec as P

F32 = jnp.float32
BF16 = jnp.bfloat16
EPSILON = 1e-05
MESH = pl.DeviceIdType.MESH
HIGHEST = lax.Precision.HIGHEST

ROWS = 512
FEAT = 512
MODEL = 4096
HEADS = 8
WIDTH = 64
STATE = 128
CHUNK = 128
NCHUNK = ROWS // CHUNK
HALF = CHUNK // 2
NSEQ = 16
NTP = 8
NCHIP = 4
COLS = 1408
RING_AG = 9
RING_RS = 8


def silu(v):
    return v / (1.0 + jnp.exp(-v))


def softplus(v):
    return jnp.maximum(v, 0.0) + jnp.log1p(jnp.exp(-jnp.abs(v)))


def dot(a, b, precision=None):
    return jnp.dot(a, b, preferred_element_type=F32, precision=precision)


def iota(shape, dim):
    return lax.broadcasted_iota(jnp.int32, shape, dim)


def across_heads(rows):
    lane = iota((1, 128), 1)
    parts = [
        jnp.where(lane < WIDTH, rows[2 * j : 2 * j + 1, :], rows[2 * j + 1 : 2 * j + 2, :])
        for j in range(4)
    ]
    return jnp.concatenate(parts, axis=1)


def kernel(
    hidden_hbm,
    gain_hbm,
    gx_hbm,
    sw_hbm,
    stepw_hbm,
    tap_x_hbm,
    tap_s_hbm,
    bias_hbm,
    decay_hbm,
    skip_hbm,
    igain_hbm,
    wo_hbm,
    init_hbm,
    out_hbm,
    hidden,
    gain_ref,
    stepw_ref,
    tap_x,
    tap_s,
    bias_ref,
    decay_ref,
    skip_ref,
    igain_ref,
    init_ref,
    out_ref,
    gx_raw,
    sw_raw,
    w,
    wo,
    g,
    ss_send,
    ss_recv,
    rfull,
    xf,
    steps,
    sz,
    y,
    ec,
    sloc,
    pre,
    state,
    total_log,
    cmap,
    vals,
    bmap_t,
    cols_t,
    cum_rows,
    step_rows,
    mx,
    early,
    halo_send,
    halo_recv,
    piece_send,
    piece_recv,
    enter_send,
    enter_recv,
    init_t,
    entering,
    xs,
    xr,
    part,
    far_send,
    near_send,
    far_recv,
    near_recv,
    load_sem,
    out_sem,
    ag_send,
    ag_recv,
    ss_ssem,
    ss_rsem,
    halo_ssem,
    halo_rsem,
    p_ssem,
    p_rsem,
    e_ssem,
    e_rsem,
    rs_ssem,
    rs_rsem,
):
    seq = lax.axis_index("seq")
    tp = lax.axis_index("tp")
    chip = tp // 2
    core = tp % 2
    up = (chip + 1) % NCHIP
    down = (chip + 3) % NCHIP
    far = (chip + 2) % NCHIP
    tp_up = up * 2 + core
    tp_down = down * 2 + core
    tp_far = far * 2 + core
    sibling = chip * 2 + (1 - core)

    loads = [
        pltpu.make_async_copy(gx_hbm, gx_raw, load_sem.at[0]),
        pltpu.make_async_copy(sw_hbm, sw_raw, load_sem.at[1]),
        pltpu.make_async_copy(wo_hbm, wo, load_sem.at[2]),
        pltpu.make_async_copy(hidden_hbm, hidden, load_sem.at[3]),
        pltpu.make_async_copy(gain_hbm, gain_ref, load_sem.at[4]),
        pltpu.make_async_copy(stepw_hbm, stepw_ref, load_sem.at[5]),
        pltpu.make_async_copy(tap_x_hbm, tap_x, load_sem.at[6]),
        pltpu.make_async_copy(tap_s_hbm, tap_s, load_sem.at[7]),
        pltpu.make_async_copy(bias_hbm, bias_ref, load_sem.at[8]),
        pltpu.make_async_copy(decay_hbm, decay_ref, load_sem.at[9]),
        pltpu.make_async_copy(skip_hbm, skip_ref, load_sem.at[10]),
        pltpu.make_async_copy(igain_hbm, igain_ref, load_sem.at[11]),
        pltpu.make_async_copy(init_hbm, init_ref, load_sem.at[12]),
    ]
    loads[3].start()
    loads[4].start()

    barrier = pltpu.get_barrier_semaphore()

    @pl.loop(0, NSEQ - 1)
    def _(k):
        pl.semaphore_signal(
            barrier, inc=1, device_id={"seq": (seq + 1 + (k + 5) % (NSEQ - 1)) % NSEQ}, device_id_type=MESH
        )

    @pl.loop(1, NTP)
    def _(k):
        pl.semaphore_signal(
            barrier, inc=1, device_id={"tp": (tp + k) % NTP}, device_id_type=MESH
        )

    for n in (0, 1, 5, 6, 7, 8, 9, 10, 11, 12):
        loads[n].start()
    loads[3].wait()
    loads[4].wait()

    gain_rows = gain_ref[...].astype(F32)
    gain_at = iota((MODEL // 128, 128), 0)
    gain = jnp.concatenate(
        [
            jnp.sum(jnp.where(gain_at == tp * 4 + j, gain_rows, 0.0), axis=0, keepdims=True)
            for j in range(4)
        ],
        axis=1,
    )
    own = pl.ds(pl.multiple_of(tp * FEAT, FEAT), FEAT)
    squares = []
    for c in range(NCHUNK):
        rows = slice(c * CHUNK, (c + 1) * CHUNK)
        h = hidden[rows, :].astype(F32)
        g[rows, own] = (h * gain).astype(BF16)
        summed = jnp.sum(h * h, axis=1, keepdims=True)
        squares.append(jnp.broadcast_to(summed, (CHUNK, 128)).T[0:1, :])
    ss_send[...] = jnp.concatenate(squares + [jnp.zeros((4, 128), F32)], axis=0)

    pl.semaphore_wait(barrier, NTP - 1 + NSEQ - 1)

    def ag_copy(step, kind):
        row = pl.multiple_of(((step + NCHUNK - 1) % NCHUNK) * CHUNK, CHUNK)
        whole, first, second = (row, CHUNK), (row, HALF), (pl.multiple_of(row + HALF, HALF), HALF)
        (start, size), shard, target = (
            (whole, tp, tp_up),
            (whole, tp, tp_down),
            (whole, tp, sibling),
            (first, tp_down, tp_up),
            (second, tp_up, tp_down),
            (whole, tp_down, sibling),
            (whole, tp_up, sibling),
            (first, tp_far, sibling),
            (second, tp_far, sibling),
        )[kind]
        block = g.at[pl.ds(start, size), pl.ds(pl.multiple_of(shard * FEAT, FEAT), FEAT)]
        return pltpu.make_async_remote_copy(
            src_ref=block,
            dst_ref=block,
            send_sem=ag_send.at[step, kind],
            recv_sem=ag_recv.at[step, kind],
            device_id={"tp": target},
            device_id_type=MESH,
        )

    def send_own(step):
        for kind in (0, 1, 2):
            ag_copy(step, kind).start()

    send_own(0)

    def ss_copy(k):
        return pltpu.make_async_remote_copy(
            src_ref=ss_send,
            dst_ref=ss_recv.at[tp],
            send_sem=ss_ssem.at[k],
            recv_sem=ss_rsem.at[k],
            device_id={"tp": (tp + k) % NTP},
            device_id_type=MESH,
        )

    @pl.loop(1, NTP)
    def _(k):
        ss_copy(k).start()

    ss_recv[tp] = ss_send[...]

    loads[0].wait()
    o256, i256 = iota((256, 256), 0), iota((256, 256), 1)
    pick = jnp.where(i256 == (o256 % 32) * 8 + o256 // 32, 1.0, 0.0).astype(BF16)

    def sort_gate_x(b):
        at = pl.multiple_of(b * 512, 512)
        k0 = pl.multiple_of(b * 64, 64)
        both = jnp.concatenate([gx_raw[pl.ds(at, 256), :], gx_raw[pl.ds(at + 256, 256), :]], axis=1)
        sorted_rows = dot(pick, both).astype(BF16)
        for m in range(8):
            column = (m % 2) * 512 + (m // 2) * 128
            rows = sorted_rows[m * 32 : (m + 1) * 32, :]
            w[pl.ds(k0, 32), column : column + 128] = rows[:, :128]
            w[pl.ds(k0 + 32, 32), column : column + 128] = rows[:, 128:]

    pl.loop(0, 32, unroll=16)(sort_gate_x)
    send_own(1)
    pl.loop(32, 64, unroll=16)(sort_gate_x)
    loads[1].wait()
    loads[2].start()
    pick_state = jnp.where(i256 == (o256 % 128) * 2 + o256 // 128, 1.0, 0.0).astype(BF16)

    @pl.loop(0, 16, unroll=8)
    def _(b):
        at = pl.multiple_of(b * 512, 512)
        k0 = pl.multiple_of(b * 256, 256)
        both = jnp.concatenate([sw_raw[pl.ds(at, 256), :], sw_raw[pl.ds(at + 256, 256), :]], axis=1)
        sorted_rows = dot(pick_state, both).astype(BF16)
        for m in range(2):
            column = 1024 + m * 128
            rows = sorted_rows[m * 128 : (m + 1) * 128, :]
            w[pl.ds(k0, 128), column : column + 128] = rows[:, :128]
            w[pl.ds(k0 + 128, 128), column : column + 128] = rows[:, 128:]

    for n in range(5, 13):
        loads[n].wait()

    @pl.loop(0, 32, unroll=8)
    def _(b):
        at = pl.multiple_of(b * 128, 128)
        rows = stepw_ref[:, pl.ds(at, 128)].astype(F32)
        square = jnp.concatenate([rows, jnp.zeros((120, 128), F32)], axis=0)
        w[pl.ds(at, 128), 1280:1408] = square.T.astype(BF16)

    for j in range(4):
        init_t[:, j * 128 : (j + 1) * 128] = init_ref[j * 128 : (j + 1) * 128, :].T

    lane512 = iota((1, 512), 1)
    row8 = iota((8, 128), 0)
    bias = jnp.zeros((8, 128), F32)
    rate = jnp.zeros((8, 128), F32)
    skip = jnp.zeros((1, 512), F32)
    for h in range(HEADS):
        bias = jnp.where(row8 == h, bias_ref[h], bias)
        rate = jnp.where(row8 == h, decay_ref[h], rate)
        skip = jnp.where(lane512 // WIDTH == h, skip_ref[h], skip)
    rate = jnp.exp(rate)
    r128, c128 = iota((128, 128), 0), iota((128, 128), 1)
    causal = r128 >= c128
    upper = jnp.where(r128 <= c128, 1.0, 0.0)
    s_row, s_lane = iota((128, 512), 0), iota((128, 512), 1)
    spread_decay = jnp.where(s_row == HEADS + s_lane // WIDTH, 1.0, 0.0).astype(BF16)
    spread_step = jnp.where(s_row == 2 * HEADS + s_lane // WIDTH, 1.0, 0.0).astype(BF16)

    state[...] = jnp.zeros((STATE, FEAT), F32)
    total_log[...] = jnp.zeros((8, 128), F32)

    halo_copy = pltpu.make_async_remote_copy(
        src_ref=halo_send,
        dst_ref=halo_recv,
        send_sem=halo_ssem,
        recv_sem=halo_rsem,
        device_id={"seq": (seq + 1) % NSEQ},
        device_id_type=MESH,
    )

    def chunk_of(step):
        return (step + NCHUNK - 1) % NCHUNK

    def product_with(rows, z):
        features = pl.ds(pl.multiple_of(z * 2 * FEAT, 2 * FEAT), 2 * FEAT)
        return dot(g[rows, features], w[features, 512:COLS])

    def project_near(c):
        rows = pl.ds(pl.multiple_of(c * CHUNK, CHUNK), CHUNK)
        early[...] = product_with(rows, chip) + product_with(rows, up) + product_with(rows, down)

    def project(c):
        row = pl.multiple_of(c * CHUNK, CHUNK)
        rows = pl.ds(row, CHUNK)
        r = rfull[rows, :]
        product = early[...] + product_with(rows, far)
        for n in range(6):
            raw = (product[:, n * 128 : (n + 1) * 128] * r).astype(BF16).astype(F32)
            xf[pl.ds(pl.multiple_of(row + 16, 16), CHUNK), n * 128 : (n + 1) * 128] = raw
        raw_step = (product[:, 768:896] * r).astype(BF16).astype(F32)
        steps[:, rows] = raw_step.T[0:HEADS, :]

    def project_gate(c):
        rows = pl.ds(pl.multiple_of(c * CHUNK, CHUNK), CHUNK)
        r = rfull[rows, :]
        product = dot(g[rows, :], w[:, 0:512])
        for n in range(4):
            z = (product[:, n * 128 : (n + 1) * 128] * r).astype(BF16).astype(F32)
            sz[rows, n * 128 : (n + 1) * 128] = silu(z)

    def scan_chunk(c):
        row = pl.multiple_of(c * CHUNK, CHUNK)
        rows = pl.ds(row, CHUNK)

        def filtered(cols, taps):
            padded = xf[pl.ds(pl.multiple_of(row + 8, 8), CHUNK + 8), cols]
            summed = taps[0] * padded[5 : 5 + CHUNK]
            for k in range(1, 4):
                summed = summed + taps[k] * padded[5 + k : 5 + k + CHUNK]
            return silu(summed).astype(BF16)

        taps_x = tap_x[...].astype(F32)
        taps_s = tap_s[...].astype(F32)
        values = jnp.concatenate(
            [
                filtered(
                    slice(j * 128, (j + 1) * 128),
                    [taps_x[k : k + 1, j * 128 : (j + 1) * 128] for k in range(4)],
                )
                for j in range(4)
            ],
            axis=1,
        )
        in_map, out_map = (
            filtered(
                slice(512 + m * 128, 640 + m * 128),
                [taps_s[2 * k + m : 2 * k + m + 1, :] for k in range(4)],
            )
            for m in range(2)
        )
        cmap[rows, :] = out_map
        vals[rows, :] = values
        in_map_t = in_map.astype(F32).T.astype(BF16)
        bmap_t[c] = in_map_t
        last = jnp.broadcast_to(cum_rows[c][:, 127:128], (8, 128))
        wide = values.astype(F32)
        weighted = (wide * y[rows, :]).astype(BF16)
        before = state[...]
        sloc[c] = before
        pre[c] = jnp.broadcast_to(jnp.exp(across_heads(total_log[...])), (8, FEAT))
        total_log[...] += last
        state[...] = jnp.exp(across_heads(last)) * before + dot(in_map_t, weighted)

    def scan_steps(c):
        rows = pl.ds(pl.multiple_of(c * CHUNK, CHUNK), CHUNK)
        step = softplus(steps[:, rows] + bias)
        cum = dot(-step * rate, upper, HIGHEST)
        last = jnp.broadcast_to(cum[:, 127:128], (8, 128))
        kept = step * jnp.exp(last - cum)
        columns = jnp.concatenate(
            [cum, jnp.exp(cum), kept, jnp.zeros((104, 128), F32)], axis=0
        ).T
        cols_t[c] = columns
        cum_rows[c] = cum
        step_rows[c] = step
        high = columns.astype(BF16)
        low = (columns - high.astype(F32)).astype(BF16)
        step_exp = dot(high, spread_step) + dot(low, spread_step)
        y[rows, :] = step_exp

    def outputs_of(c):
        rows = pl.ds(pl.multiple_of(c * CHUNK, CHUNK), CHUNK)
        columns, cum, step = cols_t[c], cum_rows[c], step_rows[c]
        high = columns.astype(BF16)
        low = (columns - high.astype(F32)).astype(BF16)
        ec[rows, :] = dot(high, spread_decay) + dot(low, spread_decay)
        scores = dot(cmap[rows, :], bmap_t[c])
        lane = iota((CHUNK, 128), 1)
        for j in range(4):
            cols = slice(j * 128, (j + 1) * 128)
            pair = vals[rows, cols]
            both = []
            for h in (2 * j, 2 * j + 1):
                spread = columns[:, h : h + 1] - cum[h : h + 1, :]
                weights = jnp.exp(jnp.where(causal, spread, -1e30))
                both.append(dot((scores * weights * step[h : h + 1, :]).astype(BF16), pair))
            y[rows, cols] = (
                jnp.where(lane < WIDTH, both[0], both[1]) + skip[:, cols] * pair.astype(F32)
            )

    @pl.loop(0, NCHUNK + 1)
    def _(i):
        @pl.when(i == 2)
        def _():
            @pl.loop(1, NTP)
            def _(k):
                ss_copy(k).wait_recv()

            summed = ss_recv[0]
            for k in range(1, NTP):
                summed = summed + ss_recv[k]
            r = lax.rsqrt(summed * (1.0 / MODEL) + EPSILON)
            for c in range(NCHUNK):
                rfull[c * CHUNK : (c + 1) * CHUNK, :] = jnp.broadcast_to(
                    r[c : c + 1, :], (CHUNK, 128)
                ).T

        @pl.when(i >= 2)
        def _():
            for kind in (7, 8):
                ag_copy(i - 2, kind).wait_recv()
            project(chunk_of(i - 2))
            scan_steps(chunk_of(i - 2))

        @pl.when(i == 2)
        def _():
            halo_send[...] = xf[ROWS : ROWS + 16, :].astype(BF16)
            halo_copy.start()

        @pl.when(i < NCHUNK)
        def _():
            ag_copy(i, 0).wait_recv()
            ag_copy(i, 3).start()
            ag_copy(i, 5).start()
            ag_copy(i, 1).wait_recv()
            ag_copy(i, 4).start()
            ag_copy(i, 6).start()

        @pl.when(i < NCHUNK - 2)
        def _():
            send_own(i + 2)

        @pl.when((i >= 1) & (i <= NCHUNK))
        def _():
            for kind in (2, 5, 6):
                ag_copy(i - 1, kind).wait_recv()
            project_near(chunk_of(i - 1))
            ag_copy(i - 1, 3).wait_recv()
            ag_copy(i - 1, 7).start()
            ag_copy(i - 1, 4).wait_recv()
            ag_copy(i - 1, 8).start()

        @pl.when(i == 3)
        def _():
            halo_copy.wait_recv()
            xf[0:16, :] = jnp.where(seq > 0, halo_recv[...].astype(F32), 0.0)

        @pl.when(i >= 3)
        def _():
            scan_chunk(i - 3)

    for kind in (7, 8):
        ag_copy(NCHUNK - 1, kind).wait_recv()
    project(NCHUNK - 2)
    scan_steps(NCHUNK - 2)
    scan_chunk(NCHUNK - 2)
    scan_chunk(NCHUNK - 1)

    logs = across_heads(total_log[...])
    high = logs.astype(BF16)
    rest = logs - high.astype(F32)
    middle = rest.astype(BF16)
    bits = [high.astype(F32), middle.astype(F32), rest - middle.astype(F32)]
    row16 = iota((16, 128), 0)
    for half in range(2):
        block = jnp.zeros((16, 128), F32)
        for part_at in range(2):
            at = half * 256 + part_at * 128
            for n in range(3):
                block = jnp.where(row16 == part_at * 8 + n, bits[n][:, at : at + 128], block)
        block = block.astype(BF16)
        for n in range(8):
            piece_send[2 * n + half, :, 0:256] = state[
                n * 16 : (n + 1) * 16, half * 256 : (half + 1) * 256
            ].astype(BF16)
            piece_send[2 * n + half, :, 256:384] = block

    def piece_copy(k):
        target = (seq + 1 + (k + 4) % (NSEQ - 1)) % NSEQ
        return pltpu.make_async_remote_copy(
            src_ref=piece_send.at[target],
            dst_ref=piece_recv.at[seq],
            send_sem=p_ssem.at[k],
            recv_sem=p_rsem.at[k],
            device_id={"seq": target},
            device_id_type=MESH,
        )

    def enter_copy(k):
        target = (seq + 1 + (k + 4) % (NSEQ - 1)) % NSEQ
        return pltpu.make_async_remote_copy(
            src_ref=enter_send.at[target],
            dst_ref=enter_recv.at[seq],
            send_sem=e_ssem.at[k],
            recv_sem=e_rsem.at[k],
            device_id={"seq": target},
            device_id_type=MESH,
        )

    @pl.loop(1, NSEQ)
    def _(k):
        piece_copy(k).start()

    piece_recv[seq] = piece_send[seq]

    @pl.loop(0, 2)
    def _(c):
        project_gate(c)
        outputs_of(c)

    carried = init_t[
        pl.ds(pl.multiple_of((seq // 2) * 16, 16), 16),
        pl.ds(pl.multiple_of((seq % 2) * 256, 256), 256),
    ]

    @pl.loop(1, NSEQ)
    def _(k):
        piece_copy(k).wait_recv()

    for s in range(NSEQ):
        enter_send[s] = carried.astype(BF16)
        codes = piece_recv[s, :, 256:384].astype(F32)
        log = jnp.concatenate(
            [codes[0:1] + codes[1:2] + codes[2:3], codes[8:9] + codes[9:10] + codes[10:11]], axis=1
        )
        carried = jnp.exp(log) * carried + piece_recv[s, :, 0:256].astype(F32)

    @pl.loop(1, NSEQ)
    def _(k):
        enter_copy(k).start()

    enter_recv[seq] = enter_send[seq]

    @pl.loop(2, 4)
    def _(c):
        project_gate(c)
        outputs_of(c)

    loads[2].wait()

    @pl.loop(1, NSEQ)
    def _(k):
        enter_copy(k).wait_recv()

    for q in range(NSEQ):
        n, half = q // 2, q % 2
        entering[n * 16 : (n + 1) * 16, half * 256 : (half + 1) * 256] = enter_recv[q].astype(F32)

    igain_rows = igain_ref[...].astype(F32)
    igain = jnp.concatenate([igain_rows[j : j + 1, :] for j in range(4)], axis=1)

    def rs_copy(i, kind):
        src, dst, target = (
            (xs.at[i, 0], xr.at[i, 0], sibling),
            (xs.at[i, 1], xr.at[i, 1], sibling),
            (xs.at[i, 2], xr.at[i, 2], sibling),
            (xs.at[i, 3], xr.at[i, 3], sibling),
            (far_send.at[i, 0], far_recv.at[i, 0], tp_up),
            (far_send.at[i, 1], far_recv.at[i, 1], tp_down),
            (near_send.at[i, 0], near_recv.at[i, 0], tp_up),
            (near_send.at[i, 1], near_recv.at[i, 1], tp_down),
        )[kind]
        return pltpu.make_async_remote_copy(
            src_ref=src,
            dst_ref=dst,
            send_sem=rs_ssem.at[i, kind],
            recv_sem=rs_rsem.at[i, kind],
            device_id={"tp": target},
            device_id_type=MESH,
        )

    def out_block(rows, z, to_core):
        at = pl.multiple_of((z * 2 + to_core) * FEAT, FEAT)
        return dot(mx[rows, :], wo[:, pl.ds(at, FEAT)])

    def project_out(c, d, z):
        rows = pl.ds(pl.multiple_of(c * CHUNK, CHUNK), CHUNK)
        xs[c, d] = out_block(rows, z, 1 - core).astype(BF16)
        rs_copy(c, d).start()
        part[c, d] = out_block(rows, z, core)

    @pl.loop(0, NCHUNK + 1)
    def _(i):
        @pl.when(i < NCHUNK)
        def _():
            rows = pl.ds(pl.multiple_of(i * CHUNK, CHUNK), CHUNK)
            memory = (sloc[i] + pre[i][0:1, :] * entering[...]).astype(BF16)
            mixer = y[rows, :] + ec[rows, :] * dot(cmap[rows, :], memory)
            gated = mixer * sz[rows, :]
            scale = lax.rsqrt(jnp.mean(gated * gated, axis=1, keepdims=True) + EPSILON)
            mx[rows, :] = (gated * scale * igain).astype(BF16)
            project_out(i, 0, far)

        @pl.when(i >= 1)
        def _():
            c = i - 1
            rs_copy(c, 0).wait_recv()
            whole = (part[c, 0] + xr[c, 0].astype(F32)).astype(BF16)
            far_send[c, 0] = whole[:HALF]
            rs_copy(c, 4).start()
            far_send[c, 1] = whole[HALF:]
            rs_copy(c, 5).start()

    @pl.loop(0, NCHUNK)
    def _(c):
        project_out(c, 1, up)
        project_out(c, 2, down)
        rs_copy(c, 1).wait_recv()
        rs_copy(c, 4).wait_recv()
        whole = part[c, 1] + xr[c, 1].astype(F32)
        near_send[c, 0, 0:HALF] = (whole[:HALF] + far_recv[c, 0].astype(F32)).astype(BF16)
        near_send[c, 0, HALF:CHUNK] = whole[HALF:].astype(BF16)
        rs_copy(c, 6).start()
        rs_copy(c, 2).wait_recv()
        rs_copy(c, 5).wait_recv()
        whole = part[c, 2] + xr[c, 2].astype(F32)
        near_send[c, 1, 0:HALF] = whole[:HALF].astype(BF16)
        near_send[c, 1, HALF:CHUNK] = (whole[HALF:] + far_recv[c, 1].astype(F32)).astype(BF16)
        rs_copy(c, 7).start()

    @pl.loop(0, NCHUNK)
    def _(c):
        project_out(c, 3, chip)

    @pl.loop(0, NCHUNK)
    def _(i):
        for kind in range(RING_AG):
            ag_copy(i, kind).wait_send()
        for kind in (0, 1, 2, 4, 5):
            rs_copy(i, kind).wait_send()

    @pl.loop(1, NTP)
    def _(k):
        ss_copy(k).wait_send()

    halo_copy.wait_send()

    @pl.loop(1, NSEQ)
    def _(k):
        piece_copy(k).wait_send()
        enter_copy(k).wait_send()

    @pl.loop(0, NCHUNK)
    def _(c):
        rows = pl.ds(pl.multiple_of(c * CHUNK, CHUNK), CHUNK)
        rs_copy(c, 3).wait_recv()
        part[c, 3] = hidden[rows, :].astype(F32) + (part[c, 3] + xr[c, 3].astype(F32))

    def out_copy(c):
        rows = pl.ds(pl.multiple_of(c * CHUNK, CHUNK), CHUNK)
        return pltpu.make_async_copy(out_ref.at[rows, :], out_hbm.at[rows, :], out_sem.at[c])

    @pl.loop(0, NCHUNK)
    def _(c):
        rows = pl.ds(pl.multiple_of(c * CHUNK, CHUNK), CHUNK)
        rs_copy(c, 6).wait_recv()
        summed = part[c, 3] + near_recv[c, 0].astype(F32)
        rs_copy(c, 7).wait_recv()
        out_ref[rows, :] = (summed + near_recv[c, 1].astype(F32)).astype(BF16)
        out_copy(c).start()

    @pl.loop(0, NCHUNK)
    def _(c):
        rs_copy(c, 3).wait_send()
        rs_copy(c, 6).wait_send()
        rs_copy(c, 7).wait_send()
        out_copy(c).wait()


def on_device(
    hidden,
    norm_gain,
    gate_x_weight,
    state_weight,
    step_weight,
    conv_inner,
    conv_state,
    step_bias,
    decay_log,
    skip_gain,
    inner_gain,
    out_weight,
    initial_state,
):
    gx = gate_x_weight.reshape(MODEL, 2, 4, 128).transpose(0, 2, 1, 3).reshape(MODEL * 8, 128)
    sw = state_weight.reshape(MODEL * 2, 128)
    anywhere = pl.BlockSpec(memory_space=pl.ANY)
    V = pltpu.VMEM
    dma = pltpu.SemaphoreType.DMA
    return pl.pallas_call(
        kernel,
        out_shape=jax.ShapeDtypeStruct((ROWS, FEAT), BF16),
        in_specs=[anywhere] * 13,
        out_specs=anywhere,
        scratch_shapes=[
            V((ROWS, FEAT), BF16),
            V((MODEL // 128, 128), BF16),
            V((HEADS, MODEL), BF16),
            V((4, FEAT), BF16),
            V((8, 128), BF16),
            pltpu.SMEM((HEADS,), F32),
            pltpu.SMEM((HEADS,), F32),
            pltpu.SMEM((HEADS,), F32),
            V((4, 128), BF16),
            V((HEADS * WIDTH, STATE), F32),
            V((ROWS, FEAT), BF16),
            V((MODEL * 8, 128), BF16),
            V((MODEL * 2, 128), BF16),
            V((MODEL, COLS), BF16),
            V((FEAT, MODEL), BF16),
            V((ROWS, MODEL), BF16),
            V((8, 128), F32),
            V((NTP, 8, 128), F32),
            V((ROWS, 128), F32),
            V((ROWS + 16, 768), F32),
            V((8, ROWS), F32),
            V((ROWS, FEAT), F32),
            V((ROWS, FEAT), F32),
            V((ROWS, FEAT), F32),
            V((NCHUNK, STATE, FEAT), F32),
            V((NCHUNK, 8, FEAT), F32),
            V((STATE, FEAT), F32),
            V((8, 128), F32),
            V((ROWS, STATE), BF16),
            V((ROWS, FEAT), BF16),
            V((NCHUNK, STATE, CHUNK), BF16),
            V((NCHUNK, CHUNK, 128), F32),
            V((NCHUNK, HEADS, CHUNK), F32),
            V((NCHUNK, HEADS, CHUNK), F32),
            V((ROWS, FEAT), BF16),
            V((CHUNK, COLS - 512), F32),
            V((16, 768), BF16),
            V((16, 768), BF16),
            V((NSEQ, 16, 384), BF16),
            V((NSEQ, 16, 384), BF16),
            V((NSEQ, 16, 256), BF16),
            V((NSEQ, 16, 256), BF16),
            V((STATE, FEAT), F32),
            V((STATE, FEAT), F32),
            V((NCHUNK, 4, CHUNK, FEAT), BF16),
            V((NCHUNK, 4, CHUNK, FEAT), BF16),
            V((NCHUNK, 4, CHUNK, FEAT), F32),
            V((NCHUNK, 2, HALF, FEAT), BF16),
            V((NCHUNK, 2, CHUNK, FEAT), BF16),
            V((NCHUNK, 2, HALF, FEAT), BF16),
            V((NCHUNK, 2, CHUNK, FEAT), BF16),
            dma((13,)),
            dma((NCHUNK,)),
            dma((NCHUNK, RING_AG)),
            dma((NCHUNK, RING_AG)),
            dma((NTP,)),
            dma((NTP,)),
            dma,
            dma,
            dma((NSEQ,)),
            dma((NSEQ,)),
            dma((NSEQ,)),
            dma((NSEQ,)),
            dma((NCHUNK, RING_RS)),
            dma((NCHUNK, RING_RS)),
        ],
        compiler_params=pltpu.CompilerParams(
            collective_id=0, has_side_effects=True, vmem_limit_bytes=61 << 20
        ),
    )(
        hidden,
        norm_gain.reshape(MODEL // 128, 128),
        gx,
        sw,
        step_weight.T,
        conv_inner,
        conv_state.reshape(8, 128),
        step_bias,
        decay_log,
        skip_gain,
        inner_gain.reshape(4, 128),
        out_weight,
        initial_state.reshape(HEADS * WIDTH, STATE),
    )


def solution(mesh):
    return jax.shard_map(
        on_device,
        mesh=mesh,
        in_specs=(
            P("seq", "tp"),
            P(),
            P(None, None, "tp"),
            P(None, None, "tp"),
            P(None, "tp"),
            P(None, "tp"),
            P(None, None, "tp"),
            P("tp"),
            P("tp"),
            P("tp"),
            P("tp"),
            P("tp", None),
            P("tp", None, None),
        ),
        out_specs=P("seq", "tp"),
        check_vma=False,
    )
```

```python
import functools

import jax
import jax.numpy as jnp
from jax import lax
from jax.experimental import pallas as pl
from jax.experimental.pallas import tpu as pltpu
from jax.sharding import PartitionSpec as P

F32 = jnp.float32
BF16 = jnp.bfloat16
EPSILON = 1e-05
MESH = pl.DeviceIdType.MESH
HIGHEST = lax.Precision.HIGHEST

ROWS = 512
FEAT = 512
MODEL = 4096
HEADS = 8
WIDTH = 64
STATE = 128
CHUNK = 128
NCHUNK = ROWS // CHUNK
HALF = CHUNK // 2
NSEQ = 16
NTP = 8
NCHIP = 4
COLS = 1408
RING_AG = 9
RING_RS = 8


def silu(v):
    return v / (1.0 + jnp.exp(-v))


def softplus(v):
    return jnp.maximum(v, 0.0) + jnp.log1p(jnp.exp(-jnp.abs(v)))


def dot(a, b, precision=None):
    return jnp.dot(a, b, preferred_element_type=F32, precision=precision)


def iota(shape, dim):
    return lax.broadcasted_iota(jnp.int32, shape, dim)


def across_heads(rows):
    lane = iota((1, 128), 1)
    parts = [
        jnp.where(lane < WIDTH, rows[2 * j : 2 * j + 1, :], rows[2 * j + 1 : 2 * j + 2, :])
        for j in range(4)
    ]
    return jnp.concatenate(parts, axis=1)


def kernel(
    hidden_hbm,
    gain_hbm,
    gx_hbm,
    sw_hbm,
    stepw_hbm,
    tap_x_hbm,
    tap_s_hbm,
    bias_hbm,
    decay_hbm,
    skip_hbm,
    igain_hbm,
    wo_hbm,
    init_hbm,
    out_hbm,
    hidden,
    gain_ref,
    stepw_ref,
    tap_x,
    tap_s,
    bias_ref,
    decay_ref,
    skip_ref,
    igain_ref,
    init_ref,
    out_ref,
    gx_raw,
    sw_raw,
    w,
    wo,
    g,
    ss_send,
    ss_recv,
    rfull,
    xf,
    steps,
    sz,
    y,
    ec,
    sloc,
    pre,
    state,
    total_log,
    cmap,
    vals,
    bmap_t,
    cols_t,
    cum_rows,
    step_rows,
    mx,
    early,
    halo_send,
    halo_recv,
    piece_send,
    piece_recv,
    enter_send,
    enter_recv,
    init_t,
    entering,
    xs,
    xr,
    part,
    far_send,
    near_send,
    far_recv,
    near_recv,
    load_sem,
    out_sem,
    ag_send,
    ag_recv,
    ss_ssem,
    ss_rsem,
    halo_ssem,
    halo_rsem,
    p_ssem,
    p_rsem,
    e_ssem,
    e_rsem,
    rs_ssem,
    rs_rsem,
):
    seq = lax.axis_index("seq")
    tp = lax.axis_index("tp")
    chip = tp // 2
    core = tp % 2
    up = (chip + 1) % NCHIP
    down = (chip + 3) % NCHIP
    far = (chip + 2) % NCHIP
    tp_up = up * 2 + core
    tp_down = down * 2 + core
    tp_far = far * 2 + core
    sibling = chip * 2 + (1 - core)

    loads = [
        pltpu.make_async_copy(gx_hbm, gx_raw, load_sem.at[0]),
        pltpu.make_async_copy(sw_hbm, sw_raw, load_sem.at[1]),
        pltpu.make_async_copy(wo_hbm, wo, load_sem.at[2]),
        pltpu.make_async_copy(hidden_hbm, hidden, load_sem.at[3]),
        pltpu.make_async_copy(gain_hbm, gain_ref, load_sem.at[4]),
        pltpu.make_async_copy(stepw_hbm, stepw_ref, load_sem.at[5]),
        pltpu.make_async_copy(tap_x_hbm, tap_x, load_sem.at[6]),
        pltpu.make_async_copy(tap_s_hbm, tap_s, load_sem.at[7]),
        pltpu.make_async_copy(bias_hbm, bias_ref, load_sem.at[8]),
        pltpu.make_async_copy(decay_hbm, decay_ref, load_sem.at[9]),
        pltpu.make_async_copy(skip_hbm, skip_ref, load_sem.at[10]),
        pltpu.make_async_copy(igain_hbm, igain_ref, load_sem.at[11]),
        pltpu.make_async_copy(init_hbm, init_ref, load_sem.at[12]),
    ]
    loads[3].start()
    loads[4].start()

    barrier = pltpu.get_barrier_semaphore()

    @pl.loop(0, NSEQ - 1)
    def _(k):
        pl.semaphore_signal(
            barrier, inc=1, device_id={"seq": (seq + 1 + (k + 5) % (NSEQ - 1)) % NSEQ}, device_id_type=MESH
        )

    @pl.loop(1, NTP)
    def _(k):
        pl.semaphore_signal(
            barrier, inc=1, device_id={"tp": (tp + k) % NTP}, device_id_type=MESH
        )

    for n in (0, 1, 5, 6, 7, 8, 9, 10, 11, 12):
        loads[n].start()
    loads[3].wait()
    loads[4].wait()

    gain_rows = gain_ref[...].astype(F32)
    gain_at = iota((MODEL // 128, 128), 0)
    gain = jnp.concatenate(
        [
            jnp.sum(jnp.where(gain_at == tp * 4 + j, gain_rows, 0.0), axis=0, keepdims=True)
            for j in range(4)
        ],
        axis=1,
    )
    own = pl.ds(pl.multiple_of(tp * FEAT, FEAT), FEAT)
    squares = []
    for c in range(NCHUNK):
        rows = slice(c * CHUNK, (c + 1) * CHUNK)
        h = hidden[rows, :].astype(F32)
        g[rows, own] = (h * gain).astype(BF16)
        summed = jnp.sum(h * h, axis=1, keepdims=True)
        squares.append(jnp.broadcast_to(summed, (CHUNK, 128)).T[0:1, :])
    ss_send[...] = jnp.concatenate(squares + [jnp.zeros((4, 128), F32)], axis=0)

    pl.semaphore_wait(barrier, NTP - 1 + NSEQ - 1)

    def ag_copy(step, kind):
        row = pl.multiple_of(((step + NCHUNK - 1) % NCHUNK) * CHUNK, CHUNK)
        whole, first, second = (row, CHUNK), (row, HALF), (pl.multiple_of(row + HALF, HALF), HALF)
        (start, size), shard, target = (
            (whole, tp, tp_up),
            (whole, tp, tp_down),
            (whole, tp, sibling),
            (first, tp_down, tp_up),
            (second, tp_up, tp_down),
            (whole, tp_down, sibling),
            (whole, tp_up, sibling),
            (first, tp_far, sibling),
            (second, tp_far, sibling),
        )[kind]
        block = g.at[pl.ds(start, size), pl.ds(pl.multiple_of(shard * FEAT, FEAT), FEAT)]
        return pltpu.make_async_remote_copy(
            src_ref=block,
            dst_ref=block,
            send_sem=ag_send.at[step, kind],
            recv_sem=ag_recv.at[step, kind],
            device_id={"tp": target},
            device_id_type=MESH,
        )

    def send_own(step):
        for kind in (0, 1, 2):
            ag_copy(step, kind).start()

    send_own(0)

    def ss_copy(k):
        return pltpu.make_async_remote_copy(
            src_ref=ss_send,
            dst_ref=ss_recv.at[tp],
            send_sem=ss_ssem.at[k],
            recv_sem=ss_rsem.at[k],
            device_id={"tp": (tp + k) % NTP},
            device_id_type=MESH,
        )

    @pl.loop(1, NTP)
    def _(k):
        ss_copy(k).start()

    ss_recv[tp] = ss_send[...]

    loads[0].wait()
    o256, i256 = iota((256, 256), 0), iota((256, 256), 1)
    pick = jnp.where(i256 == (o256 % 32) * 8 + o256 // 32, 1.0, 0.0).astype(BF16)

    def sort_gate_x(b):
        at = pl.multiple_of(b * 512, 512)
        k0 = pl.multiple_of(b * 64, 64)
        both = jnp.concatenate([gx_raw[pl.ds(at, 256), :], gx_raw[pl.ds(at + 256, 256), :]], axis=1)
        sorted_rows = dot(pick, both).astype(BF16)
        for m in range(8):
            column = (m % 2) * 512 + (m // 2) * 128
            rows = sorted_rows[m * 32 : (m + 1) * 32, :]
            w[pl.ds(k0, 32), column : column + 128] = rows[:, :128]
            w[pl.ds(k0 + 32, 32), column : column + 128] = rows[:, 128:]

    pl.loop(0, 32, unroll=16)(sort_gate_x)
    send_own(1)
    pl.loop(32, 64, unroll=16)(sort_gate_x)
    loads[1].wait()
    loads[2].start()
    pick_state = jnp.where(i256 == (o256 % 128) * 2 + o256 // 128, 1.0, 0.0).astype(BF16)

    @pl.loop(0, 16, unroll=8)
    def _(b):
        at = pl.multiple_of(b * 512, 512)
        k0 = pl.multiple_of(b * 256, 256)
        both = jnp.concatenate([sw_raw[pl.ds(at, 256), :], sw_raw[pl.ds(at + 256, 256), :]], axis=1)
        sorted_rows = dot(pick_state, both).astype(BF16)
        for m in range(2):
            column = 1024 + m * 128
            rows = sorted_rows[m * 128 : (m + 1) * 128, :]
            w[pl.ds(k0, 128), column : column + 128] = rows[:, :128]
            w[pl.ds(k0 + 128, 128), column : column + 128] = rows[:, 128:]

    for n in range(5, 13):
        loads[n].wait()

    @pl.loop(0, 32, unroll=8)
    def _(b):
        at = pl.multiple_of(b * 128, 128)
        rows = stepw_ref[:, pl.ds(at, 128)].astype(F32)
        square = jnp.concatenate([rows, jnp.zeros((120, 128), F32)], axis=0)
        w[pl.ds(at, 128), 1280:1408] = square.T.astype(BF16)

    for j in range(4):
        init_t[:, j * 128 : (j + 1) * 128] = init_ref[j * 128 : (j + 1) * 128, :].T

    lane512 = iota((1, 512), 1)
    row8 = iota((8, 128), 0)
    bias = jnp.zeros((8, 128), F32)
    rate = jnp.zeros((8, 128), F32)
    skip = jnp.zeros((1, 512), F32)
    for h in range(HEADS):
        bias = jnp.where(row8 == h, bias_ref[h], bias)
        rate = jnp.where(row8 == h, decay_ref[h], rate)
        skip = jnp.where(lane512 // WIDTH == h, skip_ref[h], skip)
    rate = jnp.exp(rate)
    r128, c128 = iota((128, 128), 0), iota((128, 128), 1)
    causal = r128 >= c128
    upper = jnp.where(r128 <= c128, 1.0, 0.0)
    s_row, s_lane = iota((128, 512), 0), iota((128, 512), 1)
    spread_decay = jnp.where(s_row == HEADS + s_lane // WIDTH, 1.0, 0.0).astype(BF16)
    spread_step = jnp.where(s_row == 2 * HEADS + s_lane // WIDTH, 1.0, 0.0).astype(BF16)

    state[...] = jnp.zeros((STATE, FEAT), F32)
    total_log[...] = jnp.zeros((8, 128), F32)

    halo_copy = pltpu.make_async_remote_copy(
        src_ref=halo_send,
        dst_ref=halo_recv,
        send_sem=halo_ssem,
        recv_sem=halo_rsem,
        device_id={"seq": (seq + 1) % NSEQ},
        device_id_type=MESH,
    )

    def chunk_of(step):
        return (step + NCHUNK - 1) % NCHUNK

    def product_with(rows, z):
        features = pl.ds(pl.multiple_of(z * 2 * FEAT, 2 * FEAT), 2 * FEAT)
        return dot(g[rows, features], w[features, 512:COLS])

    def project_near(c):
        rows = pl.ds(pl.multiple_of(c * CHUNK, CHUNK), CHUNK)
        early[...] = product_with(rows, chip) + product_with(rows, up) + product_with(rows, down)

    def project(c):
        row = pl.multiple_of(c * CHUNK, CHUNK)
        rows = pl.ds(row, CHUNK)
        r = rfull[rows, :]
        product = early[...] + product_with(rows, far)
        for n in range(6):
            raw = (product[:, n * 128 : (n + 1) * 128] * r).astype(BF16).astype(F32)
            xf[pl.ds(pl.multiple_of(row + 16, 16), CHUNK), n * 128 : (n + 1) * 128] = raw
        raw_step = (product[:, 768:896] * r).astype(BF16).astype(F32)
        steps[:, rows] = raw_step.T[0:HEADS, :]

    def project_gate(c):
        rows = pl.ds(pl.multiple_of(c * CHUNK, CHUNK), CHUNK)
        r = rfull[rows, :]
        product = dot(g[rows, :], w[:, 0:512])
        for n in range(4):
            z = (product[:, n * 128 : (n + 1) * 128] * r).astype(BF16).astype(F32)
            sz[rows, n * 128 : (n + 1) * 128] = silu(z)

    def scan_chunk(c):
        row = pl.multiple_of(c * CHUNK, CHUNK)
        rows = pl.ds(row, CHUNK)

        def filtered(cols, taps):
            padded = xf[pl.ds(pl.multiple_of(row + 8, 8), CHUNK + 8), cols]
            summed = taps[0] * padded[5 : 5 + CHUNK]
            for k in range(1, 4):
                summed = summed + taps[k] * padded[5 + k : 5 + k + CHUNK]
            return silu(summed).astype(BF16)

        taps_x = tap_x[...].astype(F32)
        taps_s = tap_s[...].astype(F32)
        values = jnp.concatenate(
            [
                filtered(
                    slice(j * 128, (j + 1) * 128),
                    [taps_x[k : k + 1, j * 128 : (j + 1) * 128] for k in range(4)],
                )
                for j in range(4)
            ],
            axis=1,
        )
        in_map, out_map = (
            filtered(
                slice(512 + m * 128, 640 + m * 128),
                [taps_s[2 * k + m : 2 * k + m + 1, :] for k in range(4)],
            )
            for m in range(2)
        )
        cmap[rows, :] = out_map
        vals[rows, :] = values
        in_map_t = in_map.astype(F32).T.astype(BF16)
        bmap_t[c] = in_map_t
        last = jnp.broadcast_to(cum_rows[c][:, 127:128], (8, 128))
        wide = values.astype(F32)
        weighted = (wide * y[rows, :]).astype(BF16)
        before = state[...]
        sloc[c] = before
        pre[c] = jnp.broadcast_to(jnp.exp(across_heads(total_log[...])), (8, FEAT))
        total_log[...] += last
        state[...] = jnp.exp(across_heads(last)) * before + dot(in_map_t, weighted)

    def scan_steps(c):
        rows = pl.ds(pl.multiple_of(c * CHUNK, CHUNK), CHUNK)
        step = softplus(steps[:, rows] + bias)
        cum = dot(-step * rate, upper, HIGHEST)
        last = jnp.broadcast_to(cum[:, 127:128], (8, 128))
        kept = step * jnp.exp(last - cum)
        columns = jnp.concatenate(
            [cum, jnp.exp(cum), kept, jnp.zeros((104, 128), F32)], axis=0
        ).T
        cols_t[c] = columns
        cum_rows[c] = cum
        step_rows[c] = step
        high = columns.astype(BF16)
        low = (columns - high.astype(F32)).astype(BF16)
        step_exp = dot(high, spread_step) + dot(low, spread_step)
        y[rows, :] = step_exp

    def outputs_of(c):
        rows = pl.ds(pl.multiple_of(c * CHUNK, CHUNK), CHUNK)
        columns, cum, step = cols_t[c], cum_rows[c], step_rows[c]
        high = columns.astype(BF16)
        low = (columns - high.astype(F32)).astype(BF16)
        ec[rows, :] = dot(high, spread_decay) + dot(low, spread_decay)
        scores = dot(cmap[rows, :], bmap_t[c])
        lane = iota((CHUNK, 128), 1)
        for j in range(4):
            cols = slice(j * 128, (j + 1) * 128)
            pair = vals[rows, cols]
            both = []
            for h in (2 * j, 2 * j + 1):
                spread = columns[:, h : h + 1] - cum[h : h + 1, :]
                weights = jnp.exp(jnp.where(causal, spread, -1e30))
                both.append(dot((scores * weights * step[h : h + 1, :]).astype(BF16), pair))
            y[rows, cols] = (
                jnp.where(lane < WIDTH, both[0], both[1]) + skip[:, cols] * pair.astype(F32)
            )

    @pl.loop(0, NCHUNK + 1)
    def _(i):
        @pl.when(i == 2)
        def _():
            @pl.loop(1, NTP)
            def _(k):
                ss_copy(k).wait_recv()

            summed = ss_recv[0]
            for k in range(1, NTP):
                summed = summed + ss_recv[k]
            r = lax.rsqrt(summed * (1.0 / MODEL) + EPSILON)
            for c in range(NCHUNK):
                rfull[c * CHUNK : (c + 1) * CHUNK, :] = jnp.broadcast_to(
                    r[c : c + 1, :], (CHUNK, 128)
                ).T

        @pl.when(i >= 2)
        def _():
            for kind in (7, 8):
                ag_copy(i - 2, kind).wait_recv()
            project(chunk_of(i - 2))
            scan_steps(chunk_of(i - 2))

        @pl.when(i == 2)
        def _():
            halo_send[...] = xf[ROWS : ROWS + 16, :].astype(BF16)
            halo_copy.start()

        @pl.when(i < NCHUNK)
        def _():
            ag_copy(i, 0).wait_recv()
            ag_copy(i, 3).start()
            ag_copy(i, 5).start()
            ag_copy(i, 1).wait_recv()
            ag_copy(i, 4).start()
            ag_copy(i, 6).start()

        @pl.when(i < NCHUNK - 2)
        def _():
            send_own(i + 2)

        @pl.when((i >= 1) & (i <= NCHUNK))
        def _():
            for kind in (2, 5, 6):
                ag_copy(i - 1, kind).wait_recv()
            project_near(chunk_of(i - 1))
            ag_copy(i - 1, 3).wait_recv()
            ag_copy(i - 1, 7).start()
            ag_copy(i - 1, 4).wait_recv()
            ag_copy(i - 1, 8).start()

        @pl.when(i == 3)
        def _():
            halo_copy.wait_recv()
            xf[0:16, :] = jnp.where(seq > 0, halo_recv[...].astype(F32), 0.0)

        @pl.when(i >= 3)
        def _():
            scan_chunk(i - 3)

    for kind in (7, 8):
        ag_copy(NCHUNK - 1, kind).wait_recv()
    project(NCHUNK - 2)
    scan_steps(NCHUNK - 2)
    scan_chunk(NCHUNK - 2)
    scan_chunk(NCHUNK - 1)

    logs = across_heads(total_log[...])
    high = logs.astype(BF16)
    rest = logs - high.astype(F32)
    middle = rest.astype(BF16)
    bits = [high.astype(F32), middle.astype(F32), rest - middle.astype(F32)]
    row16 = iota((16, 128), 0)
    for half in range(2):
        block = jnp.zeros((16, 128), F32)
        for part_at in range(2):
            at = half * 256 + part_at * 128
            for n in range(3):
                block = jnp.where(row16 == part_at * 8 + n, bits[n][:, at : at + 128], block)
        block = block.astype(BF16)
        for n in range(8):
            piece_send[2 * n + half, :, 0:256] = state[
                n * 16 : (n + 1) * 16, half * 256 : (half + 1) * 256
            ].astype(BF16)
            piece_send[2 * n + half, :, 256:384] = block

    def piece_copy(k):
        target = (seq + 1 + (k + 4) % (NSEQ - 1)) % NSEQ
        return pltpu.make_async_remote_copy(
            src_ref=piece_send.at[target],
            dst_ref=piece_recv.at[seq],
            send_sem=p_ssem.at[k],
            recv_sem=p_rsem.at[k],
            device_id={"seq": target},
            device_id_type=MESH,
        )

    def enter_copy(k):
        target = (seq + 1 + (k + 4) % (NSEQ - 1)) % NSEQ
        return pltpu.make_async_remote_copy(
            src_ref=enter_send.at[target],
            dst_ref=enter_recv.at[seq],
            send_sem=e_ssem.at[k],
            recv_sem=e_rsem.at[k],
            device_id={"seq": target},
            device_id_type=MESH,
        )

    @pl.loop(1, NSEQ)
    def _(k):
        piece_copy(k).start()

    piece_recv[seq] = piece_send[seq]

    @pl.loop(0, 2)
    def _(c):
        project_gate(c)
        outputs_of(c)

    carried = init_t[
        pl.ds(pl.multiple_of((seq // 2) * 16, 16), 16),
        pl.ds(pl.multiple_of((seq % 2) * 256, 256), 256),
    ]

    @pl.loop(1, NSEQ)
    def _(k):
        piece_copy(k).wait_recv()

    for s in range(NSEQ):
        enter_send[s] = carried.astype(BF16)
        codes = piece_recv[s, :, 256:384].astype(F32)
        log = jnp.concatenate(
            [codes[0:1] + codes[1:2] + codes[2:3], codes[8:9] + codes[9:10] + codes[10:11]], axis=1
        )
        carried = jnp.exp(log) * carried + piece_recv[s, :, 0:256].astype(F32)

        @pl.when(seq != s)
        def _():
            enter_copy(((s + NSEQ - seq) % NSEQ + 9) % (NSEQ - 1) + 1).start()

    enter_recv[seq] = enter_send[seq]

    @pl.loop(2, 4)
    def _(c):
        project_gate(c)
        outputs_of(c)

    loads[2].wait()

    @pl.loop(1, NSEQ)
    def _(k):
        enter_copy(k).wait_recv()

    for q in range(NSEQ):
        n, half = q // 2, q % 2
        entering[n * 16 : (n + 1) * 16, half * 256 : (half + 1) * 256] = enter_recv[q].astype(F32)

    igain_rows = igain_ref[...].astype(F32)
    igain = jnp.concatenate([igain_rows[j : j + 1, :] for j in range(4)], axis=1)

    def rs_copy(i, kind):
        src, dst, target = (
            (xs.at[i, 0], xr.at[i, 0], sibling),
            (xs.at[i, 1], xr.at[i, 1], sibling),
            (xs.at[i, 2], xr.at[i, 2], sibling),
            (xs.at[i, 3], xr.at[i, 3], sibling),
            (far_send.at[i, 0], far_recv.at[i, 0], tp_up),
            (far_send.at[i, 1], far_recv.at[i, 1], tp_down),
            (near_send.at[i, 0], near_recv.at[i, 0], tp_up),
            (near_send.at[i, 1], near_recv.at[i, 1], tp_down),
        )[kind]
        return pltpu.make_async_remote_copy(
            src_ref=src,
            dst_ref=dst,
            send_sem=rs_ssem.at[i, kind],
            recv_sem=rs_rsem.at[i, kind],
            device_id={"tp": target},
            device_id_type=MESH,
        )

    def out_block(rows, z, to_core):
        at = pl.multiple_of((z * 2 + to_core) * FEAT, FEAT)
        return dot(mx[rows, :], wo[:, pl.ds(at, FEAT)])

    def project_out(c, d, z):
        rows = pl.ds(pl.multiple_of(c * CHUNK, CHUNK), CHUNK)
        xs[c, d] = out_block(rows, z, 1 - core).astype(BF16)
        rs_copy(c, d).start()
        part[c, d] = out_block(rows, z, core)

    @pl.loop(0, NCHUNK + 1)
    def _(i):
        @pl.when(i < NCHUNK)
        def _():
            rows = pl.ds(pl.multiple_of(i * CHUNK, CHUNK), CHUNK)
            memory = (sloc[i] + pre[i][0:1, :] * entering[...]).astype(BF16)
            mixer = y[rows, :] + ec[rows, :] * dot(cmap[rows, :], memory)
            gated = mixer * sz[rows, :]
            scale = lax.rsqrt(jnp.mean(gated * gated, axis=1, keepdims=True) + EPSILON)
            mx[rows, :] = (gated * scale * igain).astype(BF16)
            project_out(i, 0, far)

        @pl.when(i >= 1)
        def _():
            c = i - 1
            rs_copy(c, 0).wait_recv()
            whole = (part[c, 0] + xr[c, 0].astype(F32)).astype(BF16)
            far_send[c, 0] = whole[:HALF]
            rs_copy(c, 4).start()
            far_send[c, 1] = whole[HALF:]
            rs_copy(c, 5).start()

    @pl.loop(0, NCHUNK)
    def _(c):
        project_out(c, 1, up)
        project_out(c, 2, down)
        rs_copy(c, 1).wait_recv()
        rs_copy(c, 4).wait_recv()
        whole = part[c, 1] + xr[c, 1].astype(F32)
        near_send[c, 0, 0:HALF] = (whole[:HALF] + far_recv[c, 0].astype(F32)).astype(BF16)
        near_send[c, 0, HALF:CHUNK] = whole[HALF:].astype(BF16)
        rs_copy(c, 6).start()
        rs_copy(c, 2).wait_recv()
        rs_copy(c, 5).wait_recv()
        whole = part[c, 2] + xr[c, 2].astype(F32)
        near_send[c, 1, 0:HALF] = whole[:HALF].astype(BF16)
        near_send[c, 1, HALF:CHUNK] = (whole[HALF:] + far_recv[c, 1].astype(F32)).astype(BF16)
        rs_copy(c, 7).start()

    @pl.loop(0, NCHUNK)
    def _(c):
        project_out(c, 3, chip)

    @pl.loop(0, NCHUNK)
    def _(i):
        for kind in range(RING_AG):
            ag_copy(i, kind).wait_send()
        for kind in (0, 1, 2, 4, 5):
            rs_copy(i, kind).wait_send()

    @pl.loop(1, NTP)
    def _(k):
        ss_copy(k).wait_send()

    halo_copy.wait_send()

    @pl.loop(1, NSEQ)
    def _(k):
        piece_copy(k).wait_send()
        enter_copy(k).wait_send()

    @pl.loop(0, NCHUNK)
    def _(c):
        rows = pl.ds(pl.multiple_of(c * CHUNK, CHUNK), CHUNK)
        rs_copy(c, 3).wait_recv()
        part[c, 3] = hidden[rows, :].astype(F32) + (part[c, 3] + xr[c, 3].astype(F32))

    def out_copy(c):
        rows = pl.ds(pl.multiple_of(c * CHUNK, CHUNK), CHUNK)
        return pltpu.make_async_copy(out_ref.at[rows, :], out_hbm.at[rows, :], out_sem.at[c])

    @pl.loop(0, NCHUNK)
    def _(c):
        rows = pl.ds(pl.multiple_of(c * CHUNK, CHUNK), CHUNK)
        rs_copy(c, 6).wait_recv()
        summed = part[c, 3] + near_recv[c, 0].astype(F32)
        rs_copy(c, 7).wait_recv()
        out_ref[rows, :] = (summed + near_recv[c, 1].astype(F32)).astype(BF16)
        out_copy(c).start()

    @pl.loop(0, NCHUNK)
    def _(c):
        rs_copy(c, 3).wait_send()
        rs_copy(c, 6).wait_send()
        rs_copy(c, 7).wait_send()
        out_copy(c).wait()


def on_device(
    hidden,
    norm_gain,
    gate_x_weight,
    state_weight,
    step_weight,
    conv_inner,
    conv_state,
    step_bias,
    decay_log,
    skip_gain,
    inner_gain,
    out_weight,
    initial_state,
):
    gx = gate_x_weight.reshape(MODEL, 2, 4, 128).transpose(0, 2, 1, 3).reshape(MODEL * 8, 128)
    sw = state_weight.reshape(MODEL * 2, 128)
    anywhere = pl.BlockSpec(memory_space=pl.ANY)
    V = pltpu.VMEM
    dma = pltpu.SemaphoreType.DMA
    return pl.pallas_call(
        kernel,
        out_shape=jax.ShapeDtypeStruct((ROWS, FEAT), BF16),
        in_specs=[anywhere] * 13,
        out_specs=anywhere,
        scratch_shapes=[
            V((ROWS, FEAT), BF16),
            V((MODEL // 128, 128), BF16),
            V((HEADS, MODEL), BF16),
            V((4, FEAT), BF16),
            V((8, 128), BF16),
            pltpu.SMEM((HEADS,), F32),
            pltpu.SMEM((HEADS,), F32),
            pltpu.SMEM((HEADS,), F32),
            V((4, 128), BF16),
            V((HEADS * WIDTH, STATE), F32),
            V((ROWS, FEAT), BF16),
            V((MODEL * 8, 128), BF16),
            V((MODEL * 2, 128), BF16),
            V((MODEL, COLS), BF16),
            V((FEAT, MODEL), BF16),
            V((ROWS, MODEL), BF16),
            V((8, 128), F32),
            V((NTP, 8, 128), F32),
            V((ROWS, 128), F32),
            V((ROWS + 16, 768), F32),
            V((8, ROWS), F32),
            V((ROWS, FEAT), F32),
            V((ROWS, FEAT), F32),
            V((ROWS, FEAT), F32),
            V((NCHUNK, STATE, FEAT), F32),
            V((NCHUNK, 8, FEAT), F32),
            V((STATE, FEAT), F32),
            V((8, 128), F32),
            V((ROWS, STATE), BF16),
            V((ROWS, FEAT), BF16),
            V((NCHUNK, STATE, CHUNK), BF16),
            V((NCHUNK, CHUNK, 128), F32),
            V((NCHUNK, HEADS, CHUNK), F32),
            V((NCHUNK, HEADS, CHUNK), F32),
            V((ROWS, FEAT), BF16),
            V((CHUNK, COLS - 512), F32),
            V((16, 768), BF16),
            V((16, 768), BF16),
            V((NSEQ, 16, 384), BF16),
            V((NSEQ, 16, 384), BF16),
            V((NSEQ, 16, 256), BF16),
            V((NSEQ, 16, 256), BF16),
            V((STATE, FEAT), F32),
            V((STATE, FEAT), F32),
            V((NCHUNK, 4, CHUNK, FEAT), BF16),
            V((NCHUNK, 4, CHUNK, FEAT), BF16),
            V((NCHUNK, 4, CHUNK, FEAT), F32),
            V((NCHUNK, 2, HALF, FEAT), BF16),
            V((NCHUNK, 2, CHUNK, FEAT), BF16),
            V((NCHUNK, 2, HALF, FEAT), BF16),
            V((NCHUNK, 2, CHUNK, FEAT), BF16),
            dma((13,)),
            dma((NCHUNK,)),
            dma((NCHUNK, RING_AG)),
            dma((NCHUNK, RING_AG)),
            dma((NTP,)),
            dma((NTP,)),
            dma,
            dma,
            dma((NSEQ,)),
            dma((NSEQ,)),
            dma((NSEQ,)),
            dma((NSEQ,)),
            dma((NCHUNK, RING_RS)),
            dma((NCHUNK, RING_RS)),
        ],
        compiler_params=pltpu.CompilerParams(
            collective_id=0, has_side_effects=True, vmem_limit_bytes=61 << 20
        ),
    )(
        hidden,
        norm_gain.reshape(MODEL // 128, 128),
        gx,
        sw,
        step_weight.T,
        conv_inner,
        conv_state.reshape(8, 128),
        step_bias,
        decay_log,
        skip_gain,
        inner_gain.reshape(4, 128),
        out_weight,
        initial_state.reshape(HEADS * WIDTH, STATE),
    )


def solution(mesh):
    return jax.shard_map(
        on_device,
        mesh=mesh,
        in_specs=(
            P("seq", "tp"),
            P(),
            P(None, None, "tp"),
            P(None, None, "tp"),
            P(None, "tp"),
            P(None, "tp"),
            P(None, None, "tp"),
            P("tp"),
            P("tp"),
            P("tp"),
            P("tp"),
            P("tp", None),
            P("tp", None, None),
        ),
        out_specs=P("seq", "tp"),
        check_vma=False,
    )
```
